512 devices in a mesh: clip: 16 (over x_lo, y), act: 32 (over z, x_hi, core).
Axes of the slice: x: 4 (x_hi: 2, x_lo: 2; x = x_hi * 2 + x_lo), y: 8, z: 8, core: 2. Of those that a mesh axis runs over, the one named last changes fastest.
Arguments:
- clips: float32 [1024, 8192], P('act', 'clip'), may hold values from -6 to 6
- actions: float32 [1024, 16384], P('clip', 'act'), may hold values from -6 to 6
- positive_ids: int32 [8192], P('clip'), may hold values from 0 to 16383
- robot_ids: int32 [16384], P('act'), may hold values from 0 to 15
- robot_bias: float32 [16], replicated, may hold values from -4 to 0
Outputs:
- clip_grad: float32 [1024, 8192], P('act', 'clip')
- action_grad: float32 [1024, 16384], P('clip', 'act')
- loss: float32 [], replicated
The draws below stay inside these ranges and needn't reach their ends.
All inputs are finite; a program needn't handle non-finite values.
Results may differ from the reference program's by a relative error of at most 0.019.
Values may be sent and summed in bfloat16 or wider, within the bound.
No kernel may reach another device: no remote copies, remote signals or barrier semaphores. Data moves between devices by JAX's collectives and lax.ppermute only.
A program may use at most 64 MiB of HBM per device.

```python
import math
import jax
import jax.numpy as jnp
from jax import lax

D = 1024
ROWS = 512
ROBOTS = 16
NC = 8192
NA = 16384


def touch_ends(values, rng, least, largest):
    place = [jax.random.randint(jax.random.fold_in(rng, axis), (), 0, length) for axis, length in enumerate(values.shape)]
    widest = values.shape.index(max(values.shape))
    beside = place[:widest] + [(place[widest] + 1) % values.shape[widest]] + place[widest + 1:]
    return values.at[tuple(place)].set(least).at[tuple(beside)].set(largest)


def level_of(rng, extent, cuts, least, largest):
    loudness = 1.0
    for position, parts in cuts:
        heights = jax.random.uniform(jax.random.fold_in(jax.random.fold_in(rng, 6), position), (parts,), jnp.float32, least / len(cuts), largest / len(cuts))
        loudness = loudness * jnp.repeat(jnp.exp(heights), extent[position] // parts).reshape((-1,) + (1,) * (len(extent) - 1 - position))
    return loudness


def normal_values(own_key, extent, spread, bound, cuts=(), held_as=jnp.bfloat16):
    entries = jax.random.normal(own_key, extent, jnp.float32) * spread
    if len(cuts) > 0:
        entries = level_of(own_key, extent, cuts, -0.22, 0.18) * entries
    return jnp.clip(entries, min=-bound, max=bound).astype(held_as)


def setup_inputs(seed: int = 0) -> dict:
    keys = jax.random.split(jax.random.key(seed), 6)
    return {
        "clips": normal_values(keys[0], (D, NC), 1.0, 6.0, ((0, 32), (1, 16)), jnp.float32),
        "actions": normal_values(keys[1], (D, NA), 1.0, 6.0, ((0, 16), (1, 32)), jnp.float32),
        "positive_ids": touch_ends(jax.random.randint(keys[2], (NC,), 0, NA), jax.random.fold_in(keys[2], 1), 0, NA - 1).astype(jnp.int32),
        "robot_ids": touch_ends(jax.random.randint(keys[3], (NA,), 0, ROBOTS), jax.random.fold_in(keys[3], 1), 0, ROBOTS - 1).astype(jnp.int32),
        "robot_bias": jnp.clip(jax.random.uniform(keys[4], (ROBOTS,), jnp.float32, -4.0, 0.0), -4.0, 0.0),
    }


def round_half(values):
    rounded = values.astype(jnp.bfloat16)
    rounded = lax.optimization_barrier(rounded)
    return rounded.astype(jnp.float32)

def reference(clips, actions, positive_ids, robot_ids, robot_bias):
    clip_half = clips.T.astype(jnp.bfloat16)
    action_half = actions.T.astype(jnp.bfloat16)
    bias_row = robot_bias[robot_ids]
    scale = 2.0 / math.sqrt(D)
    clip_blocks = clip_half.reshape(NC // ROWS, ROWS, D)
    pos_blocks = positive_ids.reshape(NC // ROWS, ROWS)
    columns = jnp.arange(NA, dtype=jnp.int32)
    action_blocks = action_half.reshape(NA // ROWS, ROWS, D).astype(jnp.float32)

    def step(carry, item):
        summed, total = carry
        block, pos_block = item
        logits = jnp.dot(block, action_half.T, preferred_element_type=jnp.float32) * scale + bias_row[None, :]
        sign = jnp.where(pos_block[:, None] == columns[None, :], 1.0, -1.0).astype(jnp.float32)
        total = total + jnp.sum(jnp.logaddexp(jnp.float32(0.0), -sign * logits))
        weights = (-sign * jax.nn.sigmoid(-sign * logits)).astype(jnp.bfloat16)
        weight_blocks = weights.astype(jnp.float32).reshape(ROWS, NA // ROWS, ROWS)
        partials = jnp.einsum('ibj,bjd->bid', weight_blocks, action_blocks)
        grad_rows = lax.optimization_barrier(jnp.sum(round_half(partials), axis=0))
        summed = summed + round_half(jnp.dot(weights.T, block, preferred_element_type=jnp.float32))
        return ((summed, total), grad_rows)
    init = (jnp.zeros((NA, D), jnp.float32), jnp.zeros((), jnp.float32))
    (summed, total), grad_rows = lax.scan(step, init, (clip_blocks, pos_blocks))
    clip_grad = grad_rows.reshape(NC, D).T / math.sqrt(NA)
    action_grad = summed.T / math.sqrt(NC)
    loss = total / (NC * NA)
    return (clip_grad, action_grad, loss)
```

```python
import functools
import math

import jax
import jax.numpy as jnp
from jax import lax
from jax.experimental import pallas as pl
from jax.experimental.pallas import tpu as pltpu
from jax.sharding import PartitionSpec as P

BF16 = jnp.bfloat16
F32 = jnp.float32
LANES = 128
EXTRA = 16
VMEM = pl.BlockSpec(memory_space=pltpu.VMEM)
SMEM = pl.BlockSpec(memory_space=pltpu.SMEM)


def pieces(value):
    high = value.astype(BF16).astype(F32)
    middle = (value - high).astype(BF16).astype(F32)
    low = (value - high - middle).astype(BF16).astype(F32)
    return high, middle, low


def loss_rows(value, shape):
    high, middle, low = pieces(value)
    row = lax.broadcasted_iota(jnp.int32, shape, len(shape) - 2)
    rows = jnp.where(row < 4, high, jnp.where(row < 8, middle, jnp.where(row < 12, low, 0.0)))
    return rows.astype(BF16)


def store_blocks(out_ref, values, first_column):
    blocks = out_ref.shape[0]
    rows = values.shape[0] // blocks
    for part in range(values.shape[1] // LANES):
        at = (first_column // LANES + part) * rows
        columns = values[:, part * LANES : (part + 1) * LANES]
        out_ref[:, at : at + rows, :] = columns.reshape(blocks, rows, LANES).astype(BF16)


def logits_kernel(scale, step, core_ref, own_ref, got_ref, row_bias_ref, column_bias_ref, row_key_ref, column_key_ref,
                  weights_ref, grad_ref, loss_ref):
    core = core_ref[0]
    blocks, _, rows, count = own_ref.shape
    width = blocks * rows
    own = own_ref[:, core].reshape(width, count)
    own_t = own.T
    total = jnp.zeros((1, 1), F32)
    for start in range(0, got_ref.shape[1], step):
        got = got_ref[:, start : start + step]
        logits = jnp.dot(own_t, got, preferred_element_type=F32) * scale
        logits = logits + row_bias_ref[...] + column_bias_ref[:, start : start + step]
        positive = row_key_ref[...] == column_key_ref[:, start : start + step]
        margin = jnp.where(positive, -logits, logits)
        small = jnp.exp(-jnp.abs(margin))
        loss = jnp.maximum(margin, 0.0) + jnp.log1p(small)
        sigmoid = jnp.where(margin >= 0.0, 1.0, small) / (1.0 + small)
        weights = jnp.where(positive, -sigmoid, sigmoid).astype(BF16)
        weights_ref[:, start : start + step] = weights
        total = total + jnp.sum(loss, keepdims=True)
        store_blocks(grad_ref, jnp.dot(own, weights, preferred_element_type=F32), start)
    shape = (grad_ref.shape[0], EXTRA, LANES)
    grad_ref[:, grad_ref.shape[1] - EXTRA :, :] = loss_rows(jnp.broadcast_to(total.reshape(1, 1, 1), shape), shape)
    loss_ref[...] = total


def second_kernel(step, got_ref, weights_ref, grad_ref):
    for start in range(0, weights_ref.shape[0], step):
        weights = weights_ref[start : start + step, :]
        grad = lax.dot_general(got_ref[...], weights, (((1,), (1,)), ((), ())), preferred_element_type=F32)
        store_blocks(grad_ref, grad, start)


def vmem_call(kernel, out_shape, in_specs, flops=0, moved=0):
    return pl.pallas_call(
        kernel,
        out_shape=out_shape,
        in_specs=in_specs,
        out_specs=jax.tree.map(lambda _: VMEM, out_shape),
        compiler_params=pltpu.CompilerParams(vmem_limit_bytes=40 * 1024 * 1024),
        cost_estimate=pl.CostEstimate(flops=flops, bytes_accessed=moved, transcendentals=0),
    )


def summed(received, rows):
    total = jnp.sum(received.astype(F32), axis=0)
    parts = (total.shape[0] - EXTRA) // rows
    grad = total[: parts * rows].reshape(parts, rows, LANES).transpose(1, 0, 2).reshape(rows, parts * LANES)
    at = parts * rows
    return grad, total[at, 0] + total[at + 4, 0] + total[at + 8, 0]


def shards(n_clip, n_act, clips, actions, positive_ids, robot_ids, robot_bias):
    both = ("clip", "act")
    pairs = n_act // 2
    core = lax.axis_index("act") % 2
    first = core == 0
    along_act = [[[k * n_act + 2 * m + c for m in range(pairs)] for k in range(n_clip)] for c in range(2)]
    along_clip = [[[k * n_act + 2 * m + c for k in range(n_clip)] for m in range(pairs)] for c in range(2)]
    clips_first = along_act[0] + along_clip[1]
    actions_first = along_clip[0] + along_act[1]
    swap = [(i, i ^ 1) for i in range(n_act)]
    exchange = functools.partial(lax.all_to_all, axis_name=both, split_axis=0, concat_axis=0)

    clip_half = clips.astype(BF16)
    action_half = actions.astype(BF16)
    rows = action_half.shape[0]
    count = action_half.shape[1]
    width = rows * n_clip
    clip_twice = jnp.concatenate([clip_half, clip_half], axis=0)
    other = lax.ppermute(jnp.where(first, action_half, clip_twice), "act", swap)
    clip_pair = jnp.concatenate([clip_half, other[: rows // 2]], axis=0)
    chunk = jnp.stack([jnp.where(first, clip_pair, other), action_half])
    gathered = exchange(jnp.broadcast_to(chunk[None], (n_clip, 2, rows, count)), axis_index_groups=clips_first)
    got = lax.ppermute(gathered[:, 0].reshape(width, count), "act", swap)

    onehot = (robot_ids[:, None] == jnp.arange(robot_bias.shape[0], dtype=jnp.int32)[None, :]).astype(F32)
    bias = jnp.dot(onehot, robot_bias, precision=lax.Precision.HIGHEST)
    columns = lax.axis_index("act") * count + jnp.arange(count, dtype=jnp.int32)
    zero = jnp.zeros_like(bias)
    row_bias = jnp.where(first, zero, bias)[:, None]
    column_bias = jnp.where(first, bias, zero)[None, :]
    row_key = jnp.where(first, positive_ids, columns)[:, None]
    column_key = jnp.where(first, columns, positive_ids)[None, :]

    parts = count // LANES
    flops = 2 * width * count * count
    weights, near, loss = vmem_call(
        functools.partial(logits_kernel, 2.0 / math.sqrt(width), 256),
        (
            jax.ShapeDtypeStruct((count, count), BF16),
            jax.ShapeDtypeStruct((n_clip, parts * rows + EXTRA, LANES), BF16),
            jax.ShapeDtypeStruct((1, 1), F32),
        ),
        [SMEM] + [VMEM] * 6,
        2 * flops,
        8 * width * count,
    )(core.astype(jnp.int32).reshape(1), gathered, got, row_bias, column_bias, row_key, column_key)
    near_got = exchange(near, axis_index_groups=actions_first)
    far = vmem_call(
        functools.partial(second_kernel, 256),
        jax.ShapeDtypeStruct((n_clip, parts * rows, LANES), BF16),
        [VMEM, VMEM],
        flops,
        4 * width * count,
    )(got, weights)
    near_sum, near_loss = summed(near_got, rows)
    shape = (n_clip, EXTRA, LANES)
    far = jnp.concatenate([far, loss_rows(jnp.broadcast_to(near_loss, shape), shape)], axis=1)
    far_got = exchange(far, axis_index_groups=clips_first)
    far_sum, far_loss = summed(far_got, rows)

    action_grad = jnp.where(first, near_sum, far_sum)
    clip_sum = jnp.where(first, far_sum, near_sum)
    half = rows // 2
    keep = jnp.where(first, clip_sum[:half], clip_sum[half:])
    give = jnp.where(first, clip_sum[half:], clip_sum[:half])
    give = jnp.concatenate([give, jnp.broadcast_to(far_loss, (8, count))], axis=0)
    taken = lax.ppermute(give, "act", swap)
    clip_grad = keep + taken[:half]
    loss = far_loss + taken[half, 0]
    total_clips = count * n_clip
    total_actions = count * n_act
    return (
        clip_grad / math.sqrt(total_actions),
        action_grad / math.sqrt(total_clips),
        loss / (total_clips * total_actions),
    )


def solution(mesh):
    return jax.shard_map(
        functools.partial(shards, mesh.shape["clip"], mesh.shape["act"]),
        mesh=mesh,
        in_specs=(P("act", "clip"), P("clip", "act"), P("clip"), P("act"), P()),
        out_specs=(P("act", "clip"), P("clip", "act"), P()),
        check_vma=False,
    )
```

```python
import functools
import math

import jax
import jax.numpy as jnp
from jax import lax
from jax.experimental import pallas as pl
from jax.experimental.pallas import tpu as pltpu
from jax.sharding import PartitionSpec as P

BF16 = jnp.bfloat16
F32 = jnp.float32
LANES = 128
EXTRA = 16
VMEM = pl.BlockSpec(memory_space=pltpu.VMEM)
SMEM = pl.BlockSpec(memory_space=pltpu.SMEM)
ANY = pl.BlockSpec(memory_space=pl.ANY)


def loss_rows(value, shape):
    high = value.astype(BF16).astype(F32)
    middle = (value - high).astype(BF16).astype(F32)
    low = (value - high - middle).astype(BF16).astype(F32)
    row = lax.broadcasted_iota(jnp.int32, shape, len(shape) - 2)
    rows = jnp.where(row < 4, high, jnp.where(row < 8, middle, jnp.where(row < 12, low, 0.0)))
    return rows.astype(BF16)


def store_blocks(out_ref, values, first_column):
    blocks = out_ref.shape[0]
    rows = values.shape[0] // blocks
    for part in range(values.shape[1] // LANES):
        at = (first_column // LANES + part) * rows
        columns = values[:, part * LANES : (part + 1) * LANES]
        out_ref[:, at : at + rows, :] = columns.reshape(blocks, rows, LANES).astype(BF16)


def cast_kernel(core_ref, clips_ref, actions_ref, clip_ref, action_ref, send_ref):
    clip = clips_ref[...].astype(BF16)
    action = actions_ref[...].astype(BF16)
    clip_ref[...] = clip
    action_ref[...] = action

    @pl.when(core_ref[0] == 0)
    def _():
        send_ref[...] = action

    @pl.when(core_ref[0] != 0)
    def _():
        send_ref[: clip.shape[0], :] = clip
        send_ref[clip.shape[0] :, :] = clip


def chunk_kernel(core_ref, clip_ref, action_ref, other_ref, out_ref):
    half = clip_ref.shape[0]
    blocks = out_ref.shape[0]

    @pl.when(core_ref[0] == 0)
    def _():
        clip = clip_ref[...]
        other = other_ref[:half, :]
        action = action_ref[...]
        for block in range(blocks):
            out_ref[block, 0, :half, :] = clip
            out_ref[block, 0, half:, :] = other
            out_ref[block, 1] = action

    @pl.when(core_ref[0] != 0)
    def _():
        other = other_ref[...]
        action = action_ref[...]
        for block in range(blocks):
            out_ref[block, 0] = other
            out_ref[block, 1] = action


def side_kernel(core_ref, bias_ref, positive_ref, robot_ref, out_ref):
    count = positive_ref.shape[1]
    robot = robot_ref[...]
    bias = jnp.zeros((1, count), F32)
    for index in range(bias_ref.shape[0]):
        bias = jnp.where(robot == index, bias_ref[index], bias)
    zero = jnp.zeros((1, count), F32)
    positive = positive_ref[...].astype(F32)
    columns = (lax.broadcasted_iota(jnp.int32, (1, count), 1) + core_ref[1] * count).astype(F32)
    first = core_ref[0] == 0
    rows = [
        jnp.where(first, zero, bias),
        jnp.where(first, positive, columns),
        jnp.where(first, bias, zero),
        jnp.where(first, columns, positive),
        zero, zero, zero, zero,
    ]
    for index, row in enumerate(rows):
        out_ref[index : index + 1, :] = row


def logits_kernel(scale, step, core_ref, own_ref, got_ref, side_ref, weights_ref, grad_ref, weights, sent):
    core = core_ref[0]
    blocks, _, rows, count = own_ref.shape
    width = blocks * rows
    own = own_ref[:, core].reshape(width, count)
    own_t = own.T
    side_t = side_ref[...].T
    row_bias = side_t[:, 0:1]
    row_key = side_t[:, 1:2]
    total = jnp.zeros((1, 1), F32)
    copies = []
    for index, start in enumerate(range(0, got_ref.shape[1], step)):
        got = got_ref[:, start : start + step]
        logits = jnp.dot(own_t, got, preferred_element_type=F32) * scale
        logits = logits + (row_bias + side_ref[2:3, start : start + step])
        positive = row_key == side_ref[3:4, start : start + step]
        margin = jnp.where(positive, -logits, logits)
        small = jnp.exp(-jnp.abs(margin))
        loss = jnp.maximum(margin, 0.0) + jnp.log1p(small)
        sigmoid = jnp.where(margin >= 0.0, 1.0, small) / (1.0 + small)
        block = jnp.where(positive, -sigmoid, sigmoid).astype(BF16)
        weights[:, start : start + step] = block
        copies.append(
            pltpu.make_async_copy(
                weights.at[:, start : start + step], weights_ref.at[:, start : start + step], sent.at[index]
            )
        )
        copies[-1].start()
        total = total + jnp.sum(loss, keepdims=True)
        store_blocks(grad_ref, jnp.dot(own, block, preferred_element_type=F32), start)
    shape = (grad_ref.shape[0], EXTRA, LANES)
    grad_ref[:, grad_ref.shape[1] - EXTRA :, :] = loss_rows(jnp.broadcast_to(total.reshape(1, 1, 1), shape), shape)
    for copy in copies:
        copy.wait()


def second_kernel(step, got_ref, weights_ref, grad_ref):
    for start in range(0, weights_ref.shape[0], step):
        weights = weights_ref[start : start + step, :]
        grad = lax.dot_general(got_ref[...], weights, (((1,), (1,)), ((), ())), preferred_element_type=F32)
        store_blocks(grad_ref, grad, start)


def summed(received_ref, grad_rows):
    total = received_ref[0].astype(F32)
    for block in range(1, received_ref.shape[0]):
        total = total + received_ref[block].astype(F32)
    parts = [total[at : at + grad_rows] for at in range(0, total.shape[0] - EXTRA, grad_rows)]
    at = total.shape[0] - EXTRA
    loss = total[at : at + 1] + total[at + 4 : at + 5] + total[at + 8 : at + 9]
    return parts, loss


def near_kernel(received_ref, sum_ref, rows_ref):
    parts, loss = summed(received_ref, sum_ref.shape[0])
    for index, part in enumerate(parts):
        sum_ref[:, index * LANES : (index + 1) * LANES] = part
    rows = loss_rows(jnp.broadcast_to(loss, rows_ref.shape[1:]), rows_ref.shape[1:])
    for block in range(rows_ref.shape[0]):
        rows_ref[block] = rows


def far_kernel(clip_scale, action_scale, core_ref, received_ref, near_ref, action_ref, keep_ref, give_ref):
    half = keep_ref.shape[0]
    parts, loss = summed(received_ref, near_ref.shape[0])
    give_ref[half:, :] = jnp.concatenate([jnp.broadcast_to(loss, (8, LANES))] * len(parts), axis=1)

    @pl.when(core_ref[0] == 0)
    def _():
        action_ref[...] = near_ref[...] * action_scale
        for index, part in enumerate(parts):
            columns = slice(index * LANES, (index + 1) * LANES)
            keep_ref[:, columns] = part[:half] * clip_scale
            give_ref[:half, columns] = part[half:] * clip_scale

    @pl.when(core_ref[0] != 0)
    def _():
        keep_ref[...] = near_ref[half:, :] * clip_scale
        give_ref[:half, :] = near_ref[:half, :] * clip_scale
        for index, part in enumerate(parts):
            action_ref[:, index * LANES : (index + 1) * LANES] = part * action_scale


def last_kernel(loss_scale, keep_ref, give_ref, taken_ref, clip_ref, loss_ref):
    half = keep_ref.shape[0]
    clip_ref[...] = keep_ref[...] + taken_ref[:half, :]
    loss_ref[...] = (give_ref[half : half + 1, :1] + taken_ref[half : half + 1, :1]) * loss_scale


def call(kernel, out_shape, in_specs, out_specs=None, scratch=(), flops=0, moved=0):
    return pl.pallas_call(
        kernel,
        out_shape=out_shape,
        in_specs=in_specs,
        out_specs=jax.tree.map(lambda _: VMEM, out_shape) if out_specs is None else out_specs,
        scratch_shapes=scratch,
        compiler_params=pltpu.CompilerParams(vmem_limit_bytes=24 * 1024 * 1024),
        cost_estimate=pl.CostEstimate(flops=flops, bytes_accessed=moved, transcendentals=0),
    )


def shards(n_clip, n_act, clips, actions, positive_ids, robot_ids, robot_bias):
    both = ("clip", "act")
    pairs = n_act // 2
    along_act = [[[k * n_act + 2 * m + c for m in range(pairs)] for k in range(n_clip)] for c in range(2)]
    along_clip = [[[k * n_act + 2 * m + c for k in range(n_clip)] for m in range(pairs)] for c in range(2)]
    clips_first = along_act[0] + along_clip[1]
    actions_first = along_clip[0] + along_act[1]
    swap = [(i, i ^ 1) for i in range(n_act)]
    exchange = functools.partial(lax.all_to_all, axis_name=both, split_axis=0, concat_axis=0)

    half, count = clips.shape
    rows = actions.shape[0]
    width = rows * n_clip
    act = lax.axis_index("act")
    core = jnp.stack([act % 2, act]).astype(jnp.int32)
    shard = jax.ShapeDtypeStruct((rows, count), BF16)
    clip_half, action_half, send = call(
        cast_kernel, (jax.ShapeDtypeStruct((half, count), BF16), shard, shard), [SMEM, VMEM, VMEM]
    )(core, clips, actions)
    other = lax.ppermute(send, "act", swap)
    chunks = call(chunk_kernel, jax.ShapeDtypeStruct((n_clip, 2, rows, count), BF16), [SMEM] + [VMEM] * 3)(
        core, clip_half, action_half, other
    )
    gathered = exchange(chunks, axis_index_groups=clips_first)
    got = lax.ppermute(gathered[:, 0].reshape(width, count), "act", swap)
    side = call(side_kernel, jax.ShapeDtypeStruct((8, count), F32), [SMEM, SMEM, VMEM, VMEM])(
        core, robot_bias, positive_ids[None, :], robot_ids[None, :]
    )

    parts = count // LANES
    flops = 2 * width * count * count
    step = 256
    weights, near = call(
        functools.partial(logits_kernel, 2.0 / math.sqrt(width), step),
        (
            jax.ShapeDtypeStruct((count, count), BF16),
            jax.ShapeDtypeStruct((n_clip, parts * rows + EXTRA, LANES), BF16),
        ),
        [SMEM, VMEM, VMEM, VMEM],
        (ANY, VMEM),
        [pltpu.VMEM((count, count), BF16), pltpu.SemaphoreType.DMA((count // step,))],
        2 * flops,
        8 * width * count,
    )(core, gathered, got, side)
    near_got = exchange(near, axis_index_groups=actions_first)
    far = call(
        functools.partial(second_kernel, step),
        jax.ShapeDtypeStruct((n_clip, parts * rows, LANES), BF16),
        [VMEM, VMEM],
        flops=flops,
        moved=4 * width * count,
    )(got, weights)
    near_sum, far_rows = call(
        near_kernel,
        (jax.ShapeDtypeStruct((rows, count), F32), jax.ShapeDtypeStruct((n_clip, EXTRA, LANES), BF16)),
        [VMEM],
    )(near_got)
    far_got = exchange(jnp.concatenate([far, far_rows], axis=1), axis_index_groups=clips_first)

    total_clips = count * n_clip
    total_actions = count * n_act
    action_grad, keep, give = call(
        functools.partial(far_kernel, 1.0 / math.sqrt(total_actions), 1.0 / math.sqrt(total_clips)),
        (
            jax.ShapeDtypeStruct((rows, count), F32),
            jax.ShapeDtypeStruct((half, count), F32),
            jax.ShapeDtypeStruct((half + 8, count), F32),
        ),
        [SMEM, VMEM, VMEM],
    )(core, far_got, near_sum)
    taken = lax.ppermute(give, "act", swap)
    clip_grad, loss = call(
        functools.partial(last_kernel, 1.0 / (total_clips * total_actions)),
        (jax.ShapeDtypeStruct((half, count), F32), jax.ShapeDtypeStruct((1, 1), F32)),
        [VMEM] * 3,
    )(keep, give, taken)
    return clip_grad, action_grad, loss.reshape(())


def solution(mesh):
    return jax.shard_map(
        functools.partial(shards, mesh.shape["clip"], mesh.shape["act"]),
        mesh=mesh,
        in_specs=(P("act", "clip"), P("clip", "act"), P("clip"), P("act"), P()),
        out_specs=(P("act", "clip"), P("clip", "act"), P()),
        check_vma=False,
    )
```

```python
import functools
import math

import jax
import jax.numpy as jnp
from jax import lax
from jax.experimental import pallas as pl
from jax.experimental.pallas import tpu as pltpu
from jax.sharding import PartitionSpec as P

BF16 = jnp.bfloat16
F32 = jnp.float32
LANES = 128
EXTRA = 16
VMEM = pl.BlockSpec(memory_space=pltpu.VMEM)
SMEM = pl.BlockSpec(memory_space=pltpu.SMEM)
ANY = pl.BlockSpec(memory_space=pl.ANY)


def loss_rows(value, shape):
    high = value.astype(BF16).astype(F32)
    middle = (value - high).astype(BF16).astype(F32)
    low = (value - high - middle).astype(BF16).astype(F32)
    row = lax.broadcasted_iota(jnp.int32, shape, len(shape) - 2)
    rows = jnp.where(row < 4, high, jnp.where(row < 8, middle, jnp.where(row < 12, low, 0.0)))
    return rows.astype(BF16)


def store_blocks(out_ref, values, first_column):
    blocks = out_ref.shape[0]
    rows = values.shape[0] // blocks
    for part in range(values.shape[1] // LANES):
        at = (first_column // LANES + part) * rows
        columns = values[:, part * LANES : (part + 1) * LANES]
        out_ref[:, at : at + rows, :] = columns.reshape(blocks, rows, LANES).astype(BF16)


def cast_kernel(core_ref, clips_ref, actions_ref, clip_ref, action_ref, send_ref, clips, actions, arrived):
    half = clips.shape[0]
    copies = [
        pltpu.make_async_copy(clips_ref, clips, arrived.at[0]),
        pltpu.make_async_copy(actions_ref, actions, arrived.at[1]),
    ]
    for copy in copies:
        copy.start()
    for copy in copies:
        copy.wait()
    clip = clips[...].astype(BF16)
    action = actions[...].astype(BF16)
    clip_ref[...] = clip
    action_ref[...] = action

    @pl.when(core_ref[0] == 0)
    def _():
        send_ref[...] = action

    @pl.when(core_ref[0] != 0)
    def _():
        send_ref[:half, :] = clip
        send_ref[half:, :] = clip


def chunk_kernel(core_ref, clip_ref, action_ref, other_ref, side_ref, out_ref):
    del side_ref
    half = clip_ref.shape[0]
    blocks = out_ref.shape[0]

    @pl.when(core_ref[0] == 0)
    def _():
        clip = clip_ref[...]
        other = other_ref[:half, :]
        action = action_ref[...]
        for block in range(blocks):
            out_ref[block, 0, :half, :] = clip
            out_ref[block, 0, half:, :] = other
            out_ref[block, 1] = action

    @pl.when(core_ref[0] != 0)
    def _():
        other = other_ref[...]
        action = action_ref[...]
        for block in range(blocks):
            out_ref[block, 0] = other
            out_ref[block, 1] = action


def side_kernel(core_ref, bias_ref, positive_ref, robot_ref, out_ref):
    count = positive_ref.shape[1]
    robot = robot_ref[...]
    bias = jnp.zeros((1, count), F32)
    for index in range(bias_ref.shape[0]):
        bias = jnp.where(robot == index, bias_ref[index], bias)
    zero = jnp.zeros((1, count), F32)
    positive = positive_ref[...].astype(F32)
    columns = (lax.broadcasted_iota(jnp.int32, (1, count), 1) + core_ref[1] * count).astype(F32)
    first = core_ref[0] == 0
    rows = [
        jnp.where(first, zero, bias),
        jnp.where(first, positive, columns),
        jnp.where(first, bias, zero),
        jnp.where(first, columns, positive),
        zero, zero, zero, zero,
    ]
    for index, row in enumerate(rows):
        out_ref[index : index + 1, :] = row


def transpose_kernel(core_ref, own_ref, side_ref, own_t_ref, side_t_ref):
    blocks, _, rows, count = own_ref.shape
    own_t_ref[...] = own_ref[:, core_ref[0]].reshape(blocks * rows, count).T
    side_t_ref[...] = side_ref[...].T


def logits_kernel(scale, step, core_ref, own_ref, own_t_ref, got_ref, side_ref, side_t_ref, weights_ref, grad_ref, loss_ref):
    blocks, _, rows, count = own_ref.shape
    width = blocks * rows
    own = own_ref[:, core_ref[0]].reshape(width, count)
    own_t = own_t_ref[...]
    row_bias = side_t_ref[:, 0:1]
    row_key = side_t_ref[:, 1:2]
    total = jnp.zeros((1, 1), F32)
    for start in range(0, count, step):
        got = got_ref[:, start : start + step]
        logits = jnp.dot(own_t, got, preferred_element_type=F32) * scale
        logits = logits + (row_bias + side_ref[2:3, start : start + step])
        positive = row_key == side_ref[3:4, start : start + step]
        margin = jnp.where(positive, -logits, logits)
        small = jnp.exp(-jnp.abs(margin))
        above = 1.0 + small
        inverse = 1.0 / above
        log = jnp.log(above) + (small - (above - 1.0)) * inverse
        total = total + jnp.sum(jnp.maximum(margin, 0.0) + log, keepdims=True)
        sigmoid = jnp.where(margin >= 0.0, inverse, small * inverse)
        weights = jnp.where(positive, -sigmoid, sigmoid).astype(BF16)
        weights_ref[:, start : start + step] = weights
        store_blocks(grad_ref, jnp.dot(own, weights, preferred_element_type=F32), start)
    shape = (grad_ref.shape[0], EXTRA, LANES)
    grad_ref[:, grad_ref.shape[1] - EXTRA :, :] = loss_rows(jnp.broadcast_to(total.reshape(1, 1, 1), shape), shape)
    loss_ref[...] = jnp.broadcast_to(total, loss_ref.shape)


def second_kernel(step, got_ref, weights_ref, grad_ref):
    for start in range(0, weights_ref.shape[0], step):
        weights = weights_ref[start : start + step, :]
        grad = lax.dot_general(got_ref[...], weights, (((1,), (1,)), ((), ())), preferred_element_type=F32)
        store_blocks(grad_ref, grad, start)


def received_loss(rows):
    return rows[0:1] + rows[4:5] + rows[8:9]


def merge_kernel(core_ref, own_ref, got_ref, loss_ref, keep_ref, send_ref, rows_ref):
    blocks, size, _ = own_ref.shape
    loss = loss_ref[0:1, :] + received_loss(got_ref[0, size:, :].astype(F32))
    rows = loss_rows(jnp.broadcast_to(loss, rows_ref.shape[1:]), rows_ref.shape[1:])
    for block in range(blocks):
        rows_ref[block] = rows

    @pl.when(core_ref[0] == 0)
    def _():
        for block in range(blocks):
            keep_ref[block] = (own_ref[block].astype(F32) + got_ref[block, :size, :].astype(F32)).astype(BF16)

    @pl.when((core_ref[0] != 0) & (core_ref[2] == 0))
    def _():
        for block in range(blocks):
            keep_ref[block] = got_ref[block, :size, :]
            send_ref[block] = own_ref[block]

    @pl.when((core_ref[0] != 0) & (core_ref[2] != 0))
    def _():
        for block in range(blocks):
            keep_ref[block] = own_ref[block]
            send_ref[block] = got_ref[block, :size, :]


def add_kernel(core_ref, keep_ref, got_ref, loss_ref, out_ref):
    blocks, size, _ = keep_ref.shape
    total = loss_ref[0].astype(F32)
    for block in range(1, blocks):
        total = total + loss_ref[block].astype(F32)
    rows = loss_rows(jnp.broadcast_to(received_loss(total), total.shape), total.shape)
    for block in range(blocks):
        out_ref[block, size:, :] = rows

    @pl.when(core_ref[0] == 0)
    def _():
        for block in range(blocks):
            out_ref[block, :size, :] = keep_ref[block]

    @pl.when(core_ref[0] != 0)
    def _():
        for block in range(blocks):
            out_ref[block, :size, :] = (keep_ref[block].astype(F32) + got_ref[block].astype(F32)).astype(BF16)


def sum_kernel(clip_scale, action_scale, core_ref, got_ref, keep_ref, give_ref):
    blocks = got_ref.shape[0]
    rows, count = keep_ref.shape
    half = rows // 2

    def over(first, last):
        total = got_ref[first].astype(F32)
        for block in range(first + 1, last):
            total = total + got_ref[block].astype(F32)
        return total

    lower = over(0, blocks // 2)
    upper = over(blocks // 2, blocks)
    both = lower + upper
    loss = received_loss(both[both.shape[0] - EXTRA :])
    give_ref[rows:, :] = jnp.concatenate([jnp.broadcast_to(loss, (8, LANES))] * (count // LANES), axis=1)
    for part in range(count // LANES):
        columns = slice(part * LANES, (part + 1) * LANES)
        at = slice(part * rows, (part + 1) * rows)

        @pl.when(core_ref[0] == 0)
        def _():
            keep_ref[:half, columns] = both[at][:half] * clip_scale
            give_ref[:half, columns] = both[at][half:] * clip_scale

        @pl.when(core_ref[0] != 0)
        def _():
            keep_ref[:, columns] = upper[at] * action_scale
            give_ref[:rows, columns] = lower[at] * action_scale


def last_kernel(loss_scale, core_ref, keep_ref, give_ref, taken_ref, clip_ref, action_ref, loss_ref):
    rows = keep_ref.shape[0]
    half = clip_ref.shape[0]

    @pl.when(core_ref[0] == 0)
    def _():
        clip_ref[...] = keep_ref[:half, :]
        action_ref[...] = taken_ref[:rows, :]
        loss_ref[...] = give_ref[rows : rows + 1, :1] * loss_scale

    @pl.when(core_ref[0] != 0)
    def _():
        clip_ref[...] = taken_ref[:half, :]
        action_ref[...] = keep_ref[...]
        loss_ref[...] = taken_ref[rows : rows + 1, :1] * loss_scale


def call(kernel, out_shape, in_specs, scratch=(), flops=0, moved=0):
    return pl.pallas_call(
        kernel,
        out_shape=out_shape,
        in_specs=in_specs,
        out_specs=jax.tree.map(lambda _: VMEM, out_shape),
        scratch_shapes=scratch,
        compiler_params=pltpu.CompilerParams(vmem_limit_bytes=24 * 1024 * 1024),
        cost_estimate=pl.CostEstimate(flops=flops, bytes_accessed=moved, transcendentals=0),
    )


def shards(n_clip, n_act, clips, actions, positive_ids, robot_ids, robot_bias):
    both = ("clip", "act")
    pairs = n_act // 2
    near = n_clip // 2
    along_act = [[[k * n_act + 2 * m + c for m in range(pairs)] for k in range(n_clip)] for c in range(2)]
    along_clip = [[[k * n_act + 2 * m + c for k in range(n_clip)] for m in range(pairs)] for c in range(2)]
    clips_first = along_act[0] + along_clip[1]
    actions_first = along_clip[0] + along_act[1]
    swap = [(i, i ^ 1) for i in range(n_act)]
    neighbours = [
        (k * n_act + 2 * m + 1, (k + near) % n_clip * n_act + 2 * m + 1) for k in range(n_clip) for m in range(pairs)
    ]
    exchange = functools.partial(lax.all_to_all, axis_name=both, split_axis=0, concat_axis=0)

    half, count = clips.shape
    rows = actions.shape[0]
    width = rows * n_clip
    parts = count // LANES
    act = lax.axis_index("act")
    core = jnp.stack([act % 2, act, lax.axis_index("clip") // near]).astype(jnp.int32)
    shape = jax.ShapeDtypeStruct

    clip_half, action_half, send = call(
        cast_kernel,
        (shape((half, count), BF16), shape((rows, count), BF16), shape((rows, count), BF16)),
        [SMEM, ANY, ANY],
        [pltpu.VMEM((half, count), F32), pltpu.VMEM((rows, count), F32), pltpu.SemaphoreType.DMA((2,))],
    )(core, clips, actions)
    other = lax.ppermute(send, "act", swap)
    side = call(side_kernel, shape((8, count), F32), [SMEM, SMEM, VMEM, VMEM])(
        core, robot_bias, positive_ids[None, :], robot_ids[None, :]
    )
    chunks = call(chunk_kernel, shape((n_clip, 2, rows, count), BF16), [SMEM] + [VMEM] * 4)(
        core, clip_half, action_half, other, side
    )
    gathered = exchange(chunks, axis_index_groups=clips_first)
    got = lax.ppermute(gathered[:, 0].reshape(width, count), "act", swap)
    own_t, side_t = call(
        transpose_kernel, (shape((count, width), BF16), shape((count, 8), F32)), [SMEM, VMEM, VMEM]
    )(core, gathered, side)

    flops = 2 * width * count * count
    step = 256
    weights, first, loss = call(
        functools.partial(logits_kernel, 2.0 / math.sqrt(width), step),
        (
            shape((count, count), BF16),
            shape((n_clip, parts * rows + EXTRA, LANES), BF16),
            shape((8, LANES), F32),
        ),
        [SMEM] + [VMEM] * 5,
        flops=2 * flops,
        moved=8 * width * count,
    )(core, gathered, own_t, got, side, side_t)
    first_got = lax.ppermute(first, "act", swap)
    blocks = shape((n_clip, parts * rows, LANES), BF16)
    second = call(functools.partial(second_kernel, step), blocks, [VMEM, VMEM], flops=flops, moved=4 * width * count)(
        got, weights
    )
    keep, send, loss_sent = call(
        merge_kernel, (blocks, blocks, shape((n_clip, EXTRA, LANES), BF16)), [SMEM] + [VMEM] * 3
    )(core, second, first_got, loss)
    near_got = lax.ppermute(send, both, neighbours)
    loss_got = exchange(loss_sent, axis_index_groups=actions_first)
    ready = call(add_kernel, shape((n_clip, parts * rows + EXTRA, LANES), BF16), [SMEM] + [VMEM] * 3)(
        core, keep, near_got, loss_got
    )
    scattered = exchange(ready, axis_index_groups=clips_first)

    total_clips = count * n_clip
    total_actions = count * n_act
    keep, give = call(
        functools.partial(sum_kernel, 1.0 / math.sqrt(total_actions), 1.0 / math.sqrt(total_clips)),
        (shape((rows, count), F32), shape((rows + 8, count), F32)),
        [SMEM, VMEM],
    )(core, scattered)
    taken = lax.ppermute(give, "act", swap)
    clip_grad, action_grad, loss = call(
        functools.partial(last_kernel, 1.0 / (total_clips * total_actions)),
        (shape((half, count), F32), shape((rows, count), F32), shape((1, 1), F32)),
        [SMEM] + [VMEM] * 3,
    )(core, keep, give, taken)
    return clip_grad, action_grad, loss.reshape(())


def solution(mesh):
    return jax.shard_map(
        functools.partial(shards, mesh.shape["clip"], mesh.shape["act"]),
        mesh=mesh,
        in_specs=(P("act", "clip"), P("clip", "act"), P("clip"), P("act"), P()),
        out_specs=(P("act", "clip"), P("clip", "act"), P()),
        check_vma=False,
    )
```

```python
import functools
import math

import jax
import jax.numpy as jnp
from jax import lax
from jax.experimental import pallas as pl
from jax.experimental.pallas import tpu as pltpu
from jax.sharding import PartitionSpec as P

BF16 = jnp.bfloat16
F32 = jnp.float32
LANES = 128
EXTRA = 16
VMEM = pl.BlockSpec(memory_space=pltpu.VMEM)
SMEM = pl.BlockSpec(memory_space=pltpu.SMEM)


def loss_rows(value, shape):
    high = value.astype(BF16).astype(F32)
    middle = (value - high).astype(BF16).astype(F32)
    low = (value - high - middle).astype(BF16).astype(F32)
    row = lax.broadcasted_iota(jnp.int32, shape, len(shape) - 2)
    rows = jnp.where(row < 4, high, jnp.where(row < 8, middle, jnp.where(row < 12, low, 0.0)))
    return rows.astype(BF16)


def store_blocks(out_ref, values, first_column):
    blocks = out_ref.shape[0]
    rows = values.shape[0] // blocks
    for part in range(values.shape[1] // LANES):
        at = (first_column // LANES + part) * rows
        columns = values[:, part * LANES : (part + 1) * LANES]
        out_ref[:, at : at + rows, :] = columns.reshape(blocks, rows, LANES).astype(BF16)


def side_kernel(core_ref, bias_ref, positive_ref, robot_ref, out_ref, out_t_ref):
    count = positive_ref.shape[1]
    robot = robot_ref[...]
    bias = jnp.zeros((1, count), F32)
    for index in range(bias_ref.shape[1]):
        bias = jnp.where(robot == index, bias_ref[:, index : index + 1], bias)
    zero = jnp.zeros((1, count), F32)
    positive = positive_ref[...].astype(F32)
    columns = (lax.broadcasted_iota(jnp.int32, (1, count), 1) + core_ref[1] * count).astype(F32)
    first = core_ref[0] == 0
    rows = [
        jnp.where(first, zero, bias),
        jnp.where(first, positive, columns),
        jnp.where(first, bias, zero),
        jnp.where(first, columns, positive),
        zero, zero, zero, zero,
    ]
    side = jnp.concatenate(rows, axis=0)
    out_ref[...] = side
    out_t_ref[...] = side.T


def transpose_kernel(core_ref, own_ref, own_t_ref):
    blocks, _, rows, count = own_ref.shape
    own_t_ref[...] = own_ref[:, core_ref[0]].reshape(blocks * rows, count).T


def logits_kernel(scale, step, core_ref, own_ref, own_t_ref, got_ref, side_ref, side_t_ref, weights_ref, grad_ref, loss_ref):
    blocks, _, rows, count = own_ref.shape
    width = blocks * rows
    own = own_ref[:, core_ref[0]].reshape(width, count)
    own_t = own_t_ref[...]
    row_bias = side_t_ref[:, 0:1]
    row_key = side_t_ref[:, 1:2]
    total = jnp.zeros((1, 1), F32)
    for start in range(0, count, step):
        got = got_ref[:, start : start + step]
        logits = jnp.dot(own_t, got, preferred_element_type=F32) * scale
        logits = logits + (row_bias + side_ref[2:3, start : start + step])
        positive = row_key == side_ref[3:4, start : start + step]
        margin = jnp.where(positive, -logits, logits)
        small = jnp.exp(-jnp.abs(margin))
        above = 1.0 + small
        inverse = 1.0 / above
        log = jnp.log(above) + (small - (above - 1.0)) * inverse
        total = total + jnp.sum(jnp.maximum(margin, 0.0) + log, keepdims=True)
        sigmoid = jnp.where(margin >= 0.0, inverse, small * inverse)
        weights = jnp.where(positive, -sigmoid, sigmoid).astype(BF16)
        weights_ref[:, start : start + step] = weights
        store_blocks(grad_ref, jnp.dot(own, weights, preferred_element_type=F32), start)
    shape = (grad_ref.shape[0], EXTRA, LANES)
    grad_ref[:, grad_ref.shape[1] - EXTRA :, :] = loss_rows(jnp.broadcast_to(total.reshape(1, 1, 1), shape), shape)
    loss_ref[...] = jnp.broadcast_to(total, loss_ref.shape)


def second_kernel(step, core_ref, got_ref, weights_ref, first_ref, grad_ref, send_ref):
    size = grad_ref.shape[1]
    for start in range(0, weights_ref.shape[0], step):
        weights = weights_ref[start : start + step, :]
        grad = lax.dot_general(got_ref[...], weights, (((1,), (1,)), ((), ())), preferred_element_type=F32)
        store_blocks(grad_ref, grad, start)

    @pl.when(core_ref[0] == 0)
    def _():
        for block in range(grad_ref.shape[0]):
            send_ref[block] = first_ref[block, :size, :]

    @pl.when(core_ref[0] != 0)
    def _():
        for block in range(grad_ref.shape[0]):
            send_ref[block] = grad_ref[block]


def received_loss(rows):
    return rows[0:1] + rows[4:5] + rows[8:9]


def loss_kernel(loss_ref, got_ref, rows_ref):
    loss = loss_ref[0:1, :] + received_loss(got_ref[0, got_ref.shape[1] - EXTRA :, :].astype(F32))
    rows = loss_rows(jnp.broadcast_to(loss, rows_ref.shape[1:]), rows_ref.shape[1:])
    for block in range(rows_ref.shape[0]):
        rows_ref[block] = rows


def add_kernel(core_ref, own_ref, other_ref, near_ref, loss_ref, out_ref):
    blocks, size, _ = own_ref.shape
    total = loss_ref[0].astype(F32)
    for block in range(1, blocks):
        total = total + loss_ref[block].astype(F32)
    rows = loss_rows(jnp.broadcast_to(received_loss(total), total.shape), total.shape)
    for block in range(blocks):
        out_ref[block, size:, :] = rows
    core, side = core_ref[0], core_ref[2]

    @pl.when(core == 0)
    def _():
        for block in range(blocks):
            added = own_ref[block].astype(F32) + other_ref[block, :size, :].astype(F32)
            out_ref[block, :size, :] = added.astype(BF16)

    @pl.when((core != 0) & (side == 0))
    def _():
        for block in range(blocks):
            added = other_ref[block, :size, :].astype(F32) + near_ref[block].astype(F32)
            out_ref[block, :size, :] = added.astype(BF16)

    @pl.when((core != 0) & (side != 0))
    def _():
        for block in range(blocks):
            added = own_ref[block].astype(F32) + near_ref[block].astype(F32)
            out_ref[block, :size, :] = added.astype(BF16)


def sum_kernel(clip_scale, action_scale, core_ref, got_ref, keep_ref, give_ref):
    blocks = got_ref.shape[0]
    rows, count = keep_ref.shape
    half = rows // 2

    def over(first, last):
        total = got_ref[first].astype(F32)
        for block in range(first + 1, last):
            total = total + got_ref[block].astype(F32)
        return total

    lower = over(0, blocks // 2)
    upper = over(blocks // 2, blocks)
    both = lower + upper
    loss = received_loss(both[both.shape[0] - EXTRA :])
    give_ref[rows:, :] = jnp.concatenate([jnp.broadcast_to(loss, (8, LANES))] * (count // LANES), axis=1)
    for part in range(count // LANES):
        columns = slice(part * LANES, (part + 1) * LANES)
        at = slice(part * rows, (part + 1) * rows)

        @pl.when(core_ref[0] == 0)
        def _():
            keep_ref[:half, columns] = both[at][:half] * clip_scale
            give_ref[:half, columns] = both[at][half:] * clip_scale

        @pl.when(core_ref[0] != 0)
        def _():
            keep_ref[:, columns] = upper[at] * action_scale
            give_ref[:rows, columns] = lower[at] * action_scale


def last_kernel(loss_scale, core_ref, keep_ref, give_ref, taken_ref, clip_ref, action_ref, loss_ref):
    rows = keep_ref.shape[0]
    half = clip_ref.shape[0]

    @pl.when(core_ref[0] == 0)
    def _():
        clip_ref[...] = keep_ref[:half, :]
        action_ref[...] = taken_ref[:rows, :]
        loss_ref[...] = give_ref[rows : rows + 1, :1] * loss_scale

    @pl.when(core_ref[0] != 0)
    def _():
        clip_ref[...] = taken_ref[:half, :]
        action_ref[...] = keep_ref[...]
        loss_ref[...] = taken_ref[rows : rows + 1, :1] * loss_scale


def call(kernel, out_shape, in_specs, scratch=(), flops=0, moved=0):
    return pl.pallas_call(
        kernel,
        out_shape=out_shape,
        in_specs=in_specs,
        out_specs=jax.tree.map(lambda _: VMEM, out_shape),
        scratch_shapes=scratch,
        compiler_params=pltpu.CompilerParams(vmem_limit_bytes=24 * 1024 * 1024),
        cost_estimate=pl.CostEstimate(flops=flops, bytes_accessed=moved, transcendentals=0),
    )


def shards(n_clip, n_act, clips, actions, positive_ids, robot_ids, robot_bias):
    both = ("clip", "act")
    pairs = n_act // 2
    near = n_clip // 2
    along_act = [[[k * n_act + 2 * m + c for m in range(pairs)] for k in range(n_clip)] for c in range(2)]
    along_clip = [[[k * n_act + 2 * m + c for k in range(n_clip)] for m in range(pairs)] for c in range(2)]
    clips_first = along_act[0] + along_clip[1]
    actions_first = along_clip[0] + along_act[1]
    swap = [(i, i ^ 1) for i in range(n_act)]
    neighbours = []
    for k in range(near):
        for m in range(pairs):
            low, high = k * n_act + 2 * m, (k + near) * n_act + 2 * m
            neighbours += [(high, low + 1), (low + 1, high + 1)]
    exchange = functools.partial(lax.all_to_all, axis_name=both, split_axis=0, concat_axis=0)

    half, count = clips.shape
    rows = actions.shape[0]
    width = rows * n_clip
    parts = count // LANES
    act = lax.axis_index("act")
    core = jnp.stack([act % 2, act, lax.axis_index("clip") // near]).astype(jnp.int32)
    shape = jax.ShapeDtypeStruct

    first_core = act % 2 == 0
    clip_twice = jnp.broadcast_to(clips[None], (2, half, count)).reshape(rows, count)
    send = jnp.where(first_core, actions, clip_twice).astype(BF16)
    mine = jnp.where(first_core, clip_twice, actions).astype(BF16)
    other = lax.ppermute(send, "act", swap)
    clip_pair = jnp.concatenate([mine[:half], other[:half]], axis=0)
    chunk = jnp.stack([jnp.where(first_core, clip_pair, other), mine])
    chunks = jnp.broadcast_to(chunk[None], (n_clip, 2, rows, count))
    chunks, positive_ids, robot_ids, robot_bias = lax.optimization_barrier(
        (chunks, positive_ids, robot_ids, robot_bias)
    )
    gathered = exchange(chunks, axis_index_groups=clips_first)
    side, side_t = call(side_kernel, (shape((8, count), F32), shape((count, 8), F32)), [SMEM] + [VMEM] * 3)(
        core, robot_bias[None, :], positive_ids[None, :], robot_ids[None, :]
    )
    got = lax.ppermute(gathered[:, 0].reshape(width, count), "act", swap)
    own_t = call(transpose_kernel, shape((count, width), BF16), [SMEM, VMEM])(core, gathered)

    flops = 2 * width * count * count
    step = 256
    weights, first, loss = call(
        functools.partial(logits_kernel, 2.0 / math.sqrt(width), step),
        (
            shape((count, count), BF16),
            shape((n_clip, parts * rows + EXTRA, LANES), BF16),
            shape((8, LANES), F32),
        ),
        [SMEM] + [VMEM] * 5,
        flops=2 * flops,
        moved=8 * width * count,
    )(core, gathered, own_t, got, side, side_t)
    first_got = lax.ppermute(first, "act", swap)
    blocks = shape((n_clip, parts * rows, LANES), BF16)
    second, send = call(
        functools.partial(second_kernel, step),
        (blocks, blocks),
        [SMEM] + [VMEM] * 3,
        flops=flops,
        moved=8 * width * count,
    )(core, got, weights, first)
    near_got = lax.ppermute(send, both, neighbours)
    loss_sent = call(loss_kernel, shape((n_clip, EXTRA, LANES), BF16), [VMEM, VMEM])(loss, first_got)
    loss_got = exchange(loss_sent, axis_index_groups=actions_first)
    ready = call(add_kernel, shape((n_clip, parts * rows + EXTRA, LANES), BF16), [SMEM] + [VMEM] * 4)(
        core, second, first_got, near_got, loss_got
    )
    scattered = exchange(ready, axis_index_groups=clips_first)

    total_clips = count * n_clip
    total_actions = count * n_act
    keep, give = call(
        functools.partial(sum_kernel, 1.0 / math.sqrt(total_actions), 1.0 / math.sqrt(total_clips)),
        (shape((rows, count), F32), shape((rows + 8, count), F32)),
        [SMEM, VMEM],
    )(core, scattered)
    taken = lax.ppermute(give, "act", swap)
    clip_grad, action_grad, loss = call(
        functools.partial(last_kernel, 1.0 / (total_clips * total_actions)),
        (shape((half, count), F32), shape((rows, count), F32), shape((1, 1), F32)),
        [SMEM] + [VMEM] * 3,
    )(core, keep, give, taken)
    return clip_grad, action_grad, loss.reshape(())


def solution(mesh):
    return jax.shard_map(
        functools.partial(shards, mesh.shape["clip"], mesh.shape["act"]),
        mesh=mesh,
        in_specs=(P("act", "clip"), P("clip", "act"), P("clip"), P("act"), P()),
        out_specs=(P("act", "clip"), P("clip", "act"), P()),
        check_vma=False,
    )
```

```python
import functools
import math

import jax
import jax.numpy as jnp
from jax import lax
from jax.experimental import pallas as pl
from jax.experimental.pallas import tpu as pltpu
from jax.sharding import PartitionSpec as P

BF16 = jnp.bfloat16
F32 = jnp.float32
LANES = 128
EXTRA = 16
VMEM = pl.BlockSpec(memory_space=pltpu.VMEM)
SMEM = pl.BlockSpec(memory_space=pltpu.SMEM)


def loss_rows(value, shape):
    high = value.astype(BF16).astype(F32)
    middle = (value - high).astype(BF16).astype(F32)
    low = (value - high - middle).astype(BF16).astype(F32)
    row = lax.broadcasted_iota(jnp.int32, shape, len(shape) - 2)
    rows = jnp.where(row < 4, high, jnp.where(row < 8, middle, jnp.where(row < 12, low, 0.0)))
    return rows.astype(BF16)


def store_blocks(out_ref, values, first_column):
    blocks = out_ref.shape[0]
    rows = values.shape[0] // blocks
    for part in range(values.shape[1] // LANES):
        at = (first_column // LANES + part) * rows
        columns = values[:, part * LANES : (part + 1) * LANES]
        out_ref[:, at : at + rows, :] = columns.reshape(blocks, rows, LANES).astype(BF16)


def chunk_kernel(core_ref, mine_ref, other_ref, out_ref):
    half = mine_ref.shape[0] // 2
    mine = mine_ref[...]
    other = other_ref[...]
    pair = jnp.concatenate([mine[:half], other[:half]], axis=0)

    @pl.when(core_ref[0] == 0)
    def _():
        for block in range(out_ref.shape[0]):
            out_ref[block, 0] = pair
            out_ref[block, 1] = pair

    @pl.when(core_ref[0] != 0)
    def _():
        for block in range(out_ref.shape[0]):
            out_ref[block, 0] = other
            out_ref[block, 1] = mine


def side_kernel(robots, core_ref, own_ref, table_ref, own_t_ref, out_ref, out_t_ref):
    blocks, _, size, _ = own_ref.shape
    count = table_ref.shape[1]
    robot = table_ref[1:2, :]
    bias = jnp.zeros((1, count), F32)
    for index in range(robots):
        bias = jnp.where(robot == index, table_ref[2:3, index : index + 1], bias)
    zero = jnp.zeros((1, count), F32)
    positive = table_ref[0:1, :]
    columns = (lax.broadcasted_iota(jnp.int32, (1, count), 1) + core_ref[1] * count).astype(F32)
    first = core_ref[0] == 0
    rows = [
        jnp.where(first, zero, bias),
        jnp.where(first, positive, columns),
        jnp.where(first, bias, zero),
        jnp.where(first, columns, positive),
        zero, zero, zero, zero,
    ]
    side = jnp.concatenate(rows, axis=0)
    out_ref[...] = side
    out_t_ref[...] = side.T
    own_t_ref[...] = own_ref[:, core_ref[0]].reshape(blocks * size, count).T


def logits_kernel(scale, step, core_ref, own_ref, own_t_ref, got_ref, side_ref, side_t_ref, weights_ref, grad_ref, loss_ref):
    blocks, _, rows, count = own_ref.shape
    width = blocks * rows
    own = own_ref[:, core_ref[0]].reshape(width, count)
    own_t = own_t_ref[...]
    row_bias = side_t_ref[:, 0:1]
    row_key = side_t_ref[:, 1:2]
    total = jnp.zeros((1, 1), F32)
    for start in range(0, count, step):
        got = got_ref[:, start : start + step]
        logits = jnp.dot(own_t, got, preferred_element_type=F32) * scale
        logits = logits + (row_bias + side_ref[2:3, start : start + step])
        positive = row_key == side_ref[3:4, start : start + step]
        margin = jnp.where(positive, -logits, logits)
        small = jnp.exp(-jnp.abs(margin))
        above = 1.0 + small
        inverse = 1.0 / above
        log = jnp.log(above) + (small - (above - 1.0)) * inverse
        total = total + jnp.sum(jnp.maximum(margin, 0.0) + log, keepdims=True)
        sigmoid = jnp.where(margin >= 0.0, inverse, small * inverse)
        weights = jnp.where(positive, -sigmoid, sigmoid).astype(BF16)
        weights_ref[:, start : start + step] = weights
        store_blocks(grad_ref, jnp.dot(own, weights, preferred_element_type=F32), start)
    loss_ref[...] = jnp.broadcast_to(total, loss_ref.shape)


def second_kernel(step, core_ref, got_ref, weights_ref, first_ref, loss_ref, grad_ref, send_ref, rows_ref):
    size = grad_ref.shape[1]
    rows_ref[...] = loss_rows(jnp.broadcast_to(loss_ref[0:1, :], rows_ref.shape), rows_ref.shape)
    for start in range(0, weights_ref.shape[0], step):
        weights = weights_ref[start : start + step, :]
        grad = lax.dot_general(got_ref[...], weights, (((1,), (1,)), ((), ())), preferred_element_type=F32)
        store_blocks(grad_ref, grad, start)

    @pl.when(core_ref[0] == 0)
    def _():
        for block in range(grad_ref.shape[0]):
            send_ref[block] = first_ref[block]

    @pl.when(core_ref[0] != 0)
    def _():
        for block in range(grad_ref.shape[0]):
            send_ref[block] = grad_ref[block]


def received_loss(rows):
    return rows[0:1] + rows[4:5] + rows[8:9]


def add_kernel(core_ref, own_ref, other_ref, near_ref, loss_ref, out_ref):
    blocks, size, _ = own_ref.shape
    total = loss_ref[0].astype(F32)
    for block in range(1, blocks):
        total = total + loss_ref[block].astype(F32)
    rows = loss_rows(jnp.broadcast_to(received_loss(total), total.shape), total.shape)
    for block in range(blocks):
        out_ref[block, size:, :] = rows
    core, side = core_ref[0], core_ref[2]

    @pl.when(core == 0)
    def _():
        for block in range(blocks):
            added = own_ref[block].astype(F32) + other_ref[block].astype(F32)
            out_ref[block, :size, :] = added.astype(BF16)

    @pl.when((core != 0) & (side == 0))
    def _():
        for block in range(blocks):
            added = other_ref[block].astype(F32) + near_ref[block].astype(F32)
            out_ref[block, :size, :] = added.astype(BF16)

    @pl.when((core != 0) & (side != 0))
    def _():
        for block in range(blocks):
            added = own_ref[block].astype(F32) + near_ref[block].astype(F32)
            out_ref[block, :size, :] = added.astype(BF16)


def sum_kernel(clip_scale, action_scale, core_ref, got_ref, keep_ref, give_ref):
    blocks = got_ref.shape[0]
    rows, count = keep_ref.shape
    half = rows // 2

    def over(first, last):
        total = got_ref[first].astype(F32)
        for block in range(first + 1, last):
            total = total + got_ref[block].astype(F32)
        return total

    lower = over(0, blocks // 2)
    upper = over(blocks // 2, blocks)
    both = lower + upper
    loss = received_loss(both[both.shape[0] - EXTRA :])
    give_ref[rows:, :] = jnp.concatenate([jnp.broadcast_to(loss, (8, LANES))] * (count // LANES), axis=1)
    for part in range(count // LANES):
        columns = slice(part * LANES, (part + 1) * LANES)
        at = slice(part * rows, (part + 1) * rows)

        @pl.when(core_ref[0] == 0)
        def _():
            keep_ref[:half, columns] = both[at][:half] * clip_scale
            give_ref[:half, columns] = both[at][half:] * clip_scale

        @pl.when(core_ref[0] != 0)
        def _():
            keep_ref[:, columns] = upper[at] * action_scale
            give_ref[:rows, columns] = lower[at] * action_scale


def last_kernel(loss_scale, core_ref, keep_ref, give_ref, taken_ref, clip_ref, action_ref, loss_ref):
    rows = keep_ref.shape[0]
    half = clip_ref.shape[0]
    loss_ref[...] = (give_ref[rows : rows + 1, :1] + taken_ref[rows : rows + 1, :1]) * loss_scale

    @pl.when(core_ref[0] == 0)
    def _():
        clip_ref[...] = keep_ref[:half, :]
        action_ref[...] = taken_ref[:rows, :]

    @pl.when(core_ref[0] != 0)
    def _():
        clip_ref[...] = taken_ref[:half, :]
        action_ref[...] = keep_ref[...]


def call(kernel, out_shape, in_specs, scratch=(), flops=0, moved=0):
    return pl.pallas_call(
        kernel,
        out_shape=out_shape,
        in_specs=in_specs,
        out_specs=jax.tree.map(lambda _: VMEM, out_shape),
        scratch_shapes=scratch,
        compiler_params=pltpu.CompilerParams(vmem_limit_bytes=12 * 1024 * 1024),
        cost_estimate=pl.CostEstimate(flops=flops, bytes_accessed=moved, transcendentals=0),
    )


def shards(n_clip, n_act, clips, actions, positive_ids, robot_ids, robot_bias):
    both = ("clip", "act")
    pairs = n_act // 2
    near = n_clip // 2
    along_act = [[[k * n_act + 2 * m + c for m in range(pairs)] for k in range(n_clip)] for c in range(2)]
    along_clip = [[[k * n_act + 2 * m + c for k in range(n_clip)] for m in range(pairs)] for c in range(2)]
    clips_first = along_act[0] + along_clip[1]
    actions_first = along_clip[0] + along_act[1]
    swap = [(i, i ^ 1) for i in range(n_act)]
    neighbours = []
    for k in range(near):
        for m in range(pairs):
            low, high = k * n_act + 2 * m, (k + near) * n_act + 2 * m
            neighbours += [(high, low + 1), (low + 1, high + 1)]
    exchange = functools.partial(lax.all_to_all, axis_name=both, split_axis=0, concat_axis=0)

    half, count = clips.shape
    rows = actions.shape[0]
    width = rows * n_clip
    parts = count // LANES
    act = lax.axis_index("act")
    core = jnp.stack([act % 2, act, lax.axis_index("clip") // near]).astype(jnp.int32)
    shape = jax.ShapeDtypeStruct

    first_core = act % 2 == 0
    clip_twice = jnp.broadcast_to(clips[None], (2, half, count)).reshape(rows, count)
    send = jnp.where(first_core, actions, clip_twice).astype(BF16)
    mine = jnp.where(first_core, clip_twice, actions).astype(BF16)
    other = lax.ppermute(send, "act", swap)
    chunks = call(chunk_kernel, shape((n_clip, 2, rows, count), BF16), [SMEM, VMEM, VMEM])(core, mine, other)
    robots = robot_bias.shape[0]
    table = jnp.stack([positive_ids.astype(F32), robot_ids.astype(F32), jnp.pad(robot_bias, (0, count - robots))])
    chunks, table = lax.optimization_barrier((chunks, table))
    gathered = exchange(chunks, axis_index_groups=clips_first)
    got = lax.ppermute(gathered[:, 0].reshape(width, count), "act", swap)
    own_t, side, side_t = call(
        functools.partial(side_kernel, robots),
        (shape((count, width), BF16), shape((8, count), F32), shape((count, 8), F32)),
        [SMEM, VMEM, VMEM],
    )(core, gathered, table)

    flops = 2 * width * count * count
    step = 256
    blocks = shape((n_clip, parts * rows, LANES), BF16)
    loss_blocks = shape((n_clip, EXTRA, LANES), BF16)
    weights, first, loss = call(
        functools.partial(logits_kernel, 2.0 / math.sqrt(width), step),
        (shape((count, count), BF16), blocks, shape((8, LANES), F32)),
        [SMEM] + [VMEM] * 5,
        flops=2 * flops,
        moved=8 * width * count,
    )(core, gathered, own_t, got, side, side_t)
    first_got = lax.ppermute(first, "act", swap)
    second, send, loss_sent = call(
        functools.partial(second_kernel, step),
        (blocks, blocks, loss_blocks),
        [SMEM] + [VMEM] * 4,
        flops=flops,
        moved=8 * width * count,
    )(core, got, weights, first, loss)
    near_got = lax.ppermute(send, both, neighbours)
    loss_got = exchange(loss_sent, axis_index_groups=actions_first)
    ready = call(add_kernel, shape((n_clip, parts * rows + EXTRA, LANES), BF16), [SMEM] + [VMEM] * 4)(
        core, second, first_got, near_got, loss_got
    )
    scattered = exchange(ready, axis_index_groups=clips_first)

    total_clips = count * n_clip
    total_actions = count * n_act
    keep, give = call(
        functools.partial(sum_kernel, 1.0 / math.sqrt(total_actions), 1.0 / math.sqrt(total_clips)),
        (shape((rows, count), F32), shape((rows + 8, count), F32)),
        [SMEM, VMEM],
    )(core, scattered)
    taken = lax.ppermute(give, "act", swap)
    clip_grad, action_grad, loss = call(
        functools.partial(last_kernel, 1.0 / (total_clips * total_actions)),
        (shape((half, count), F32), shape((rows, count), F32), shape((1, 1), F32)),
        [SMEM] + [VMEM] * 3,
    )(core, keep, give, taken)
    return clip_grad, action_grad, loss.reshape(())


def solution(mesh):
    return jax.shard_map(
        functools.partial(shards, mesh.shape["clip"], mesh.shape["act"]),
        mesh=mesh,
        in_specs=(P("act", "clip"), P("clip", "act"), P("clip"), P("act"), P()),
        out_specs=(P("act", "clip"), P("clip", "act"), P()),
        check_vma=False,
    )
```

```python
import functools
import math

import jax
import jax.numpy as jnp
from jax import lax
from jax.experimental import pallas as pl
from jax.experimental.pallas import tpu as pltpu
from jax.sharding import PartitionSpec as P

BF16 = jnp.bfloat16
F32 = jnp.float32
LANES = 128
EXTRA = 16
VMEM = pl.BlockSpec(memory_space=pltpu.VMEM)
SMEM = pl.BlockSpec(memory_space=pltpu.SMEM)


def loss_rows(value, shape):
    high = value.astype(BF16).astype(F32)
    middle = (value - high).astype(BF16).astype(F32)
    low = (value - high - middle).astype(BF16).astype(F32)
    row = lax.broadcasted_iota(jnp.int32, shape, len(shape) - 2)
    rows = jnp.where(row < 4, high, jnp.where(row < 8, middle, jnp.where(row < 12, low, 0.0)))
    return rows.astype(BF16)


def store_blocks(out_ref, values, first_column):
    blocks = out_ref.shape[0]
    rows = values.shape[0] // blocks
    for part in range(values.shape[1] // LANES):
        at = (first_column // LANES + part) * rows
        columns = values[:, part * LANES : (part + 1) * LANES]
        out_ref[:, at : at + rows, :] = columns.reshape(blocks, rows, LANES).astype(BF16)


def chunk_kernel(core_ref, mine_ref, other_ref, out_ref):
    blocks = out_ref.shape[0]
    half = mine_ref.shape[0] // 2
    mine = mine_ref[...]
    other = other_ref[...]

    @pl.when(core_ref[0] == 0)
    def _():
        pair = jnp.concatenate([mine[:half], other[:half]], axis=0)
        for block in range(blocks):
            out_ref[block] = pair

    @pl.when(core_ref[0] != 0)
    def _():
        for block in range(blocks // 2):
            out_ref[block] = other
        for block in range(blocks // 2, blocks):
            out_ref[block] = mine


def side_kernel(core_ref, bias_ref, ids_ref, got_ref, out_ref, out_t_ref):
    count = ids_ref.shape[1]
    first = core_ref[0] == 0
    robot = jnp.where(first & (core_ref[2] == 0), ids_ref[1:2, :], got_ref[1:2, :])
    bias = jnp.zeros((1, count), F32)
    for index in range(bias_ref.shape[1]):
        bias = jnp.where(robot == index, bias_ref[:, index : index + 1], bias)
    zero = jnp.zeros((1, count), F32)
    positive = jnp.where(first, ids_ref[0:1, :], got_ref[0:1, :]).astype(F32)
    columns = (lax.broadcasted_iota(jnp.int32, (1, count), 1) + core_ref[1] * count).astype(F32)
    rows = [
        jnp.where(first, zero, bias),
        jnp.where(first, positive, columns),
        jnp.where(first, bias, zero),
        jnp.where(first, columns, positive),
        zero, zero, zero, zero,
    ]
    side = jnp.concatenate(rows, axis=0)
    out_ref[...] = side
    out_t_ref[...] = side.T


def transpose_kernel(own_ref, own_t_ref):
    own_t_ref[...] = own_ref[...].T


def logits_kernel(scale, step, own_ref, own_t_ref, got_ref, side_ref, side_t_ref, weights_ref, grad_ref, loss_ref):
    count = own_ref.shape[1]
    own = own_ref[...]
    own_t = own_t_ref[...]
    row_bias = side_t_ref[:, 0:1]
    row_key = side_t_ref[:, 1:2]
    total = jnp.zeros((1, 1), F32)
    for start in range(0, count, step):
        got = got_ref[:, start : start + step]
        logits = jnp.dot(own_t, got, preferred_element_type=F32) * scale
        logits = logits + (row_bias + side_ref[2:3, start : start + step])
        positive = row_key == side_ref[3:4, start : start + step]
        margin = jnp.where(positive, -logits, logits)
        small = jnp.exp(-jnp.abs(margin))
        above = 1.0 + small
        inverse = 1.0 / above
        log = jnp.log(above) + (small - (above - 1.0)) * inverse
        total = total + jnp.sum(jnp.maximum(margin, 0.0) + log, keepdims=True)
        sigmoid = jnp.where(margin >= 0.0, inverse, small * inverse)
        weights = jnp.where(positive, -sigmoid, sigmoid).astype(BF16)
        weights_ref[:, start : start + step] = weights
        store_blocks(grad_ref, jnp.dot(own, weights, preferred_element_type=F32), start)
    loss_ref[...] = jnp.broadcast_to(total, loss_ref.shape)


def second_kernel(step, got_ref, weights_ref, loss_ref, grad_ref, rows_ref):
    rows_ref[...] = loss_rows(jnp.broadcast_to(loss_ref[0:1, :], rows_ref.shape), rows_ref.shape)
    for start in range(0, weights_ref.shape[0], step):
        weights = weights_ref[start : start + step, :]
        grad = lax.dot_general(got_ref[...], weights, (((1,), (1,)), ((), ())), preferred_element_type=F32)
        store_blocks(grad_ref, grad, start)


def received_loss(rows):
    return rows[0:1] + rows[4:5] + rows[8:9]


def add_kernel(own_ref, got_ref, loss_ref, out_ref):
    blocks, size, _ = own_ref.shape
    total = loss_ref[0].astype(F32)
    for block in range(1, blocks):
        total = total + loss_ref[block].astype(F32)
    rows = loss_rows(jnp.broadcast_to(received_loss(total), total.shape), total.shape)
    for block in range(blocks):
        out_ref[block, size:, :] = rows
        out_ref[block, :size, :] = (own_ref[block].astype(F32) + got_ref[block].astype(F32)).astype(BF16)


def sum_kernel(clip_scale, action_scale, core_ref, got_ref, keep_ref, give_ref):
    blocks = got_ref.shape[0]
    rows, count = keep_ref.shape
    half = rows // 2

    def over(first, last):
        total = got_ref[first].astype(F32)
        for block in range(first + 1, last):
            total = total + got_ref[block].astype(F32)
        return total

    lower = over(0, blocks // 2)
    upper = over(blocks // 2, blocks)
    both = lower + upper
    loss = received_loss(both[both.shape[0] - EXTRA :])
    give_ref[rows:, :] = jnp.concatenate([jnp.broadcast_to(loss, (8, LANES))] * (count // LANES), axis=1)
    for part in range(count // LANES):
        columns = slice(part * LANES, (part + 1) * LANES)
        at = slice(part * rows, (part + 1) * rows)

        @pl.when(core_ref[0] == 0)
        def _():
            keep_ref[:half, columns] = both[at][:half] * clip_scale
            give_ref[:half, columns] = both[at][half:] * clip_scale

        @pl.when(core_ref[0] != 0)
        def _():
            keep_ref[:, columns] = upper[at] * action_scale
            give_ref[:rows, columns] = lower[at] * action_scale


def last_kernel(loss_scale, core_ref, keep_ref, give_ref, taken_ref, clip_ref, action_ref, loss_ref):
    rows = keep_ref.shape[0]
    half = clip_ref.shape[0]
    loss_ref[...] = (give_ref[rows : rows + 1, :1] + taken_ref[rows : rows + 1, :1]) * loss_scale

    @pl.when(core_ref[0] == 0)
    def _():
        clip_ref[...] = keep_ref[:half, :]
        action_ref[...] = taken_ref[:rows, :]

    @pl.when(core_ref[0] != 0)
    def _():
        clip_ref[...] = taken_ref[:half, :]
        action_ref[...] = keep_ref[...]


def call(kernel, out_shape, in_specs, scratch=(), flops=0, moved=0):
    return pl.pallas_call(
        kernel,
        out_shape=out_shape,
        in_specs=in_specs,
        out_specs=jax.tree.map(lambda _: VMEM, out_shape),
        scratch_shapes=scratch,
        compiler_params=pltpu.CompilerParams(vmem_limit_bytes=12 * 1024 * 1024),
        cost_estimate=pl.CostEstimate(flops=flops, bytes_accessed=moved, transcendentals=0),
    )


def shards(n_clip, n_act, clips, actions, positive_ids, robot_ids, robot_bias):
    both = ("clip", "act")
    pairs = n_act // 2
    near = n_clip // 2
    along_act = [[[k * n_act + 2 * m + c for m in range(pairs)] for k in range(n_clip)] for c in range(2)]
    along_clip = [[[k * n_act + 2 * m + c for k in range(n_clip)] for m in range(pairs)] for c in range(2)]
    clips_first = along_act[0] + along_clip[1]
    actions_first = along_clip[0] + along_act[1]
    swap = [(i, i ^ 1) for i in range(n_act)]
    gather_pass, scatter_pass, ids_pass = [], [], []
    for k in range(near):
        for m in range(pairs):
            low, high = k * n_act + 2 * m, (k + near) * n_act + 2 * m
            gather_pass += [(low + 1, low), (high + 1, high), (low, high + 1), (high, low + 1)]
            scatter_pass += [(low, low + 1), (high, high + 1), (low + 1, high), (high + 1, low)]
            ids_pass += [(high, low + 1), (low + 1, high + 1), (high + 1, high)]
    exchange = functools.partial(lax.all_to_all, axis_name=both, split_axis=0, concat_axis=0)

    half, count = clips.shape
    rows = actions.shape[0]
    width = rows * n_clip
    parts = count // LANES
    act = lax.axis_index("act")
    side_of = lax.axis_index("clip") // near
    core = jnp.stack([act % 2, act - act % 2 + side_of, side_of]).astype(jnp.int32)
    shape = jax.ShapeDtypeStruct

    first_core = act % 2 == 0
    clip_twice = jnp.broadcast_to(clips[None], (2, half, count)).reshape(rows, count)
    send = jnp.where(first_core, actions, clip_twice).astype(BF16)
    mine = jnp.where(first_core, clip_twice, actions).astype(BF16)
    other = lax.ppermute(send, "act", swap)
    chunks = call(chunk_kernel, shape((n_clip, rows, count), BF16), [SMEM, VMEM, VMEM])(core, mine, other)
    ids = jnp.stack([positive_ids, robot_ids])
    own = exchange(chunks, axis_index_groups=clips_first).reshape(width, count)
    got = lax.ppermute(own, both, gather_pass)
    own_t = call(transpose_kernel, shape((count, width), BF16), [VMEM])(own)
    ids_got = lax.ppermute(ids, both, ids_pass)
    side, side_t = call(side_kernel, (shape((8, count), F32), shape((count, 8), F32)), [SMEM] + [VMEM] * 3)(
        core, robot_bias[None, :], ids, ids_got
    )

    flops = 2 * width * count * count
    step = 256
    blocks = shape((n_clip, parts * rows, LANES), BF16)
    loss_blocks = shape((n_clip, EXTRA, LANES), BF16)
    weights, first, loss = call(
        functools.partial(logits_kernel, 2.0 / math.sqrt(width), step),
        (shape((count, count), BF16), blocks, shape((8, LANES), F32)),
        [VMEM] * 5,
        flops=2 * flops,
        moved=8 * width * count,
    )(own, own_t, got, side, side_t)
    first_got = lax.ppermute(first, both, scatter_pass)
    second, loss_sent = call(
        functools.partial(second_kernel, step),
        (blocks, loss_blocks),
        [VMEM] * 3,
        flops=flops,
        moved=8 * width * count,
    )(got, weights, loss)
    loss_got = exchange(loss_sent, axis_index_groups=actions_first)
    ready = call(add_kernel, shape((n_clip, parts * rows + EXTRA, LANES), BF16), [VMEM] * 3)(
        second, first_got, loss_got
    )
    scattered = exchange(ready, axis_index_groups=clips_first)

    total_clips = count * n_clip
    total_actions = count * n_act
    keep, give = call(
        functools.partial(sum_kernel, 1.0 / math.sqrt(total_actions), 1.0 / math.sqrt(total_clips)),
        (shape((rows, count), F32), shape((rows + 8, count), F32)),
        [SMEM, VMEM],
    )(core, scattered)
    taken = lax.ppermute(give, "act", swap)
    clip_grad, action_grad, loss = call(
        functools.partial(last_kernel, 1.0 / (total_clips * total_actions)),
        (shape((half, count), F32), shape((rows, count), F32), shape((1, 1), F32)),
        [SMEM] + [VMEM] * 3,
    )(core, keep, give, taken)
    return clip_grad, action_grad, loss.reshape(())


def solution(mesh):
    return jax.shard_map(
        functools.partial(shards, mesh.shape["clip"], mesh.shape["act"]),
        mesh=mesh,
        in_specs=(P("act", "clip"), P("clip", "act"), P("clip"), P("act"), P()),
        out_specs=(P("act", "clip"), P("clip", "act"), P()),
        check_vma=False,
    )
```

```python
import functools
import math

import jax
import jax.numpy as jnp
from jax import lax
from jax.experimental import pallas as pl
from jax.experimental.pallas import tpu as pltpu
from jax.sharding import PartitionSpec as P

BF16 = jnp.bfloat16
F32 = jnp.float32
LANES = 128
EXTRA = 16
VMEM = pl.BlockSpec(memory_space=pltpu.VMEM)
SMEM = pl.BlockSpec(memory_space=pltpu.SMEM)


def loss_rows(value, shape):
    high = value.astype(BF16).astype(F32)
    middle = (value - high).astype(BF16).astype(F32)
    low = (value - high - middle).astype(BF16).astype(F32)
    row = lax.broadcasted_iota(jnp.int32, shape, len(shape) - 2)
    rows = jnp.where(row < 4, high, jnp.where(row < 8, middle, jnp.where(row < 12, low, 0.0)))
    return rows.astype(BF16)


def store_blocks(out_ref, values, first_column):
    blocks = out_ref.shape[0]
    rows = values.shape[0] // blocks
    for part in range(values.shape[1] // LANES):
        at = (first_column // LANES + part) * rows
        columns = values[:, part * LANES : (part + 1) * LANES]
        out_ref[:, at : at + rows, :] = columns.reshape(blocks, rows, LANES).astype(BF16)


def block_of(index, blocks):
    return (index // (blocks // 2) + index) % 2


def chunk_kernel(core_ref, mine_ref, other_ref, out_ref):
    blocks = out_ref.shape[0]
    half = mine_ref.shape[0] // 2
    mine = mine_ref[...]
    other = other_ref[...]

    @pl.when(core_ref[0] == 0)
    def _():
        pair = jnp.concatenate([mine[:half], other[:half]], axis=0)
        for block in range(blocks):
            out_ref[block] = pair

    @pl.when(core_ref[0] != 0)
    def _():
        for block in range(blocks):
            out_ref[block] = mine if block_of(block, blocks) else other


def split_kernel(own_ref, positive_ref, robot_ref, low_ref, high_ref):
    width = own_ref.shape[0]
    positive = positive_ref[...]
    rows = [positive // LANES, positive % LANES, robot_ref[...]]
    rows = jnp.concatenate(rows + [jnp.zeros_like(positive)] * (EXTRA - len(rows)), axis=0)
    rows = rows.astype(F32).astype(BF16)
    half = low_ref.shape[1]
    low_ref[:width, :] = own_ref[:, :half]
    low_ref[width:, :] = rows[:, :half]
    high_ref[:width, :] = own_ref[:, half:]
    high_ref[width:, :] = rows[:, half:]


def transpose_kernel(own_ref, own_t_ref):
    own_t_ref[...] = own_ref[...].T


def sides(core_ref, bias_ref, positive_ref, robot_ref, got_rows):
    count = robot_ref.shape[1]
    first = core_ref[0] == 0
    robot = jnp.where(core_ref[0] == core_ref[2], robot_ref[...].astype(F32), got_rows[2:3, :])
    bias = jnp.zeros((1, count), F32)
    for index in range(bias_ref.shape[1]):
        bias = jnp.where(robot == index, bias_ref[:, index : index + 1], bias)
    zero = jnp.zeros((1, count), F32)
    positive = jnp.where(first, positive_ref[...].astype(F32), got_rows[0:1, :] * LANES + got_rows[1:2, :])
    action = (lax.broadcasted_iota(jnp.int32, (1, count), 1) + core_ref[1] * count).astype(F32)
    rows = [jnp.where(first, zero, bias), jnp.where(first, positive, action)]
    columns = [jnp.where(first, bias, zero), jnp.where(first, action, positive)]
    rows = jnp.concatenate(rows + [zero] * 6, axis=0).T
    return rows[:, 0:1], rows[:, 1:2], columns[0], columns[1]


def logits_kernel(scale, core_ref, bias_ref, positive_ref, robot_ref, own_ref, own_t_ref, low_ref, high_ref,
                  weights_ref, low_grad_ref, high_grad_ref, loss_ref):
    width = own_ref.shape[0]
    step = low_ref.shape[1]
    got_rows = jnp.concatenate([low_ref[width:, :], high_ref[width:, :]], axis=1).astype(F32)
    row_bias, row_key, column_bias, column_key = sides(core_ref, bias_ref, positive_ref, robot_ref, got_rows)
    own = own_ref[...]
    own_t = own_t_ref[...]
    total = jnp.zeros((1, 1), F32)
    for start, got_ref, grad_ref in ((0, low_ref, low_grad_ref), (step, high_ref, high_grad_ref)):
        logits = jnp.dot(own_t, got_ref[:width, :], preferred_element_type=F32) * scale
        logits = logits + (row_bias + column_bias[:, start : start + step])
        positive = row_key == column_key[:, start : start + step]
        margin = jnp.where(positive, -logits, logits)
        small = jnp.exp(-jnp.abs(margin))
        above = 1.0 + small
        inverse = 1.0 / above
        log = jnp.log(above) + (small - (above - 1.0)) * inverse
        total = total + jnp.sum(jnp.maximum(margin, 0.0) + log, keepdims=True)
        sigmoid = jnp.where(margin >= 0.0, inverse, small * inverse)
        weights = jnp.where(positive, -sigmoid, sigmoid).astype(BF16)
        weights_ref[:, start : start + step] = weights
        store_blocks(grad_ref, jnp.dot(own, weights, preferred_element_type=F32), 0)
    loss_ref[...] = jnp.broadcast_to(total, loss_ref.shape)


def second_kernel(low_ref, high_ref, weights_ref, loss_ref, grad_ref, rows_ref):
    rows_ref[...] = loss_rows(jnp.broadcast_to(loss_ref[0:1, :], rows_ref.shape), rows_ref.shape)
    step = low_ref.shape[1]
    width = low_ref.shape[0] - EXTRA
    by_columns = (((1,), (1,)), ((), ()))
    for start in range(0, weights_ref.shape[0], step):
        weights = weights_ref[start : start + step, :]
        grad = lax.dot_general(low_ref[:width, :], weights[:, :step], by_columns, preferred_element_type=F32)
        grad += lax.dot_general(high_ref[:width, :], weights[:, step:], by_columns, preferred_element_type=F32)
        store_blocks(grad_ref, grad, start)


def received_loss(rows):
    return rows[0:1] + rows[4:5] + rows[8:9]


def add_kernel(own_ref, low_ref, high_ref, loss_ref, out_ref):
    blocks, size, _ = own_ref.shape
    half = size // 2
    total = loss_ref[0].astype(F32)
    for block in range(1, blocks):
        total = total + loss_ref[block].astype(F32)
    rows = loss_rows(jnp.broadcast_to(received_loss(total), total.shape), total.shape)
    for block in range(blocks):
        own = own_ref[block].astype(F32)
        out_ref[block, :half, :] = (own[:half] + low_ref[block].astype(F32)).astype(BF16)
        out_ref[block, half:size, :] = (own[half:] + high_ref[block].astype(F32)).astype(BF16)
        out_ref[block, size:, :] = rows


def sum_kernel(clip_scale, action_scale, core_ref, got_ref, keep_ref, give_ref):
    blocks = got_ref.shape[0]
    rows, count = keep_ref.shape
    half = rows // 2

    def over(kind):
        chosen = [block for block in range(blocks) if block_of(block, blocks) == kind]
        total = got_ref[chosen[0]].astype(F32)
        for block in chosen[1:]:
            total = total + got_ref[block].astype(F32)
        return total

    lower = over(0)
    upper = over(1)
    both = lower + upper
    loss = received_loss(both[both.shape[0] - EXTRA :])
    give_ref[rows:, :] = jnp.concatenate([jnp.broadcast_to(loss, (8, LANES))] * (count // LANES), axis=1)
    for part in range(count // LANES):
        columns = slice(part * LANES, (part + 1) * LANES)
        at = slice(part * rows, (part + 1) * rows)

        @pl.when(core_ref[0] == 0)
        def _():
            keep_ref[:half, columns] = both[at][:half] * clip_scale
            give_ref[:half, columns] = both[at][half:] * clip_scale

        @pl.when(core_ref[0] != 0)
        def _():
            keep_ref[:, columns] = upper[at] * action_scale
            give_ref[:rows, columns] = lower[at] * action_scale


def last_kernel(loss_scale, core_ref, keep_ref, give_ref, taken_ref, clip_ref, action_ref, loss_ref):
    rows = keep_ref.shape[0]
    half = clip_ref.shape[0]
    loss_ref[...] = (give_ref[rows : rows + 1, :1] + taken_ref[rows : rows + 1, :1]) * loss_scale

    @pl.when(core_ref[0] == 0)
    def _():
        clip_ref[...] = keep_ref[:half, :]
        action_ref[...] = taken_ref[:rows, :]

    @pl.when(core_ref[0] != 0)
    def _():
        clip_ref[...] = taken_ref[:half, :]
        action_ref[...] = keep_ref[...]


def call(kernel, out_shape, in_specs, scratch=(), flops=0, moved=0):
    return pl.pallas_call(
        kernel,
        out_shape=out_shape,
        in_specs=in_specs,
        out_specs=jax.tree.map(lambda _: VMEM, out_shape),
        scratch_shapes=scratch,
        compiler_params=pltpu.CompilerParams(vmem_limit_bytes=12 * 1024 * 1024),
        cost_estimate=pl.CostEstimate(flops=flops, bytes_accessed=moved, transcendentals=0),
    )


def shards(n_clip, n_act, clips, actions, positive_ids, robot_ids, robot_bias):
    both = ("clip", "act")
    pairs = n_act // 2
    near = n_clip // 2
    along_act = [[[k * n_act + 2 * m + c for m in range(pairs)] for k in range(n_clip)] for c in range(2)]
    along_clip = [[[k * n_act + 2 * m + c for k in range(n_clip)] for m in range(pairs)] for c in range(2)]
    clips_first = along_act[0] + along_clip[1]
    actions_first = along_clip[0] + along_act[1]
    swap = [(i, i ^ 1) for i in range(n_act)]
    gather_pass, scatter_pass = [], []
    for neighbour in (lambda k: (k + near) % n_clip, lambda k: k ^ 1):
        there = [(k * n_act + 2 * m, neighbour(k) * n_act + 2 * m + 1) for k in range(n_clip) for m in range(pairs)]
        here = [(k * n_act + 2 * m, k * n_act + 2 * m + 1) for k in range(n_clip) for m in range(pairs)]
        gather_pass.append(there + [(b, a) for a, b in here])
        scatter_pass.append(here + [(b, a) for a, b in there])
    exchange = functools.partial(lax.all_to_all, axis_name=both, split_axis=0, concat_axis=0)

    half, count = clips.shape
    rows = actions.shape[0]
    width = rows * n_clip
    parts = count // LANES
    act = lax.axis_index("act")
    kind = block_of(lax.axis_index("clip"), n_clip)
    core = jnp.stack([act % 2, act - act % 2 + kind, kind]).astype(jnp.int32)
    shape = jax.ShapeDtypeStruct

    first_core = act % 2 == 0
    clip_twice = jnp.broadcast_to(clips[None], (2, half, count)).reshape(rows, count)
    send = jnp.where(first_core, actions, clip_twice).astype(BF16)
    mine = jnp.where(first_core, clip_twice, actions).astype(BF16)
    other = lax.ppermute(send, "act", swap)
    chunks = call(chunk_kernel, shape((n_clip, rows, count), BF16), [SMEM, VMEM, VMEM])(core, mine, other)
    positive_ids, robot_ids = positive_ids[None, :], robot_ids[None, :]
    own = exchange(chunks, axis_index_groups=clips_first).reshape(width, count)
    halves = shape((width + EXTRA, count // 2), BF16)
    low, high = call(split_kernel, (halves, halves), [VMEM] * 3)(own, positive_ids, robot_ids)
    low = lax.ppermute(low, both, gather_pass[0])
    high = lax.ppermute(high, both, gather_pass[1])
    own_t = call(transpose_kernel, shape((count, width), BF16), [VMEM])(own)

    flops = 2 * width * count * count
    blocks = shape((n_clip, parts * rows, LANES), BF16)
    half_blocks = shape((n_clip, parts * rows // 2, LANES), BF16)
    loss_blocks = shape((n_clip, EXTRA, LANES), BF16)
    weights, low_grad, high_grad, loss = call(
        functools.partial(logits_kernel, 2.0 / math.sqrt(width)),
        (shape((count, count), BF16), half_blocks, half_blocks, shape((8, LANES), F32)),
        [SMEM] + [VMEM] * 7,
        flops=2 * flops,
        moved=8 * width * count,
    )(core, robot_bias[None, :], positive_ids, robot_ids, own, own_t, low, high)
    low_got = lax.ppermute(low_grad, both, scatter_pass[0])
    high_got = lax.ppermute(high_grad, both, scatter_pass[1])
    second, loss_sent = call(second_kernel, (blocks, loss_blocks), [VMEM] * 4, flops=flops, moved=8 * width * count)(
        low, high, weights, loss
    )
    loss_got = exchange(loss_sent, axis_index_groups=actions_first)
    ready = call(add_kernel, shape((n_clip, parts * rows + EXTRA, LANES), BF16), [VMEM] * 4)(
        second, low_got, high_got, loss_got
    )
    scattered = exchange(ready, axis_index_groups=clips_first)

    total_clips = count * n_clip
    total_actions = count * n_act
    keep, give = call(
        functools.partial(sum_kernel, 1.0 / math.sqrt(total_actions), 1.0 / math.sqrt(total_clips)),
        (shape((rows, count), F32), shape((rows + 8, count), F32)),
        [SMEM, VMEM],
    )(core, scattered)
    taken = lax.ppermute(give, "act", swap)
    clip_grad, action_grad, loss = call(
        functools.partial(last_kernel, 1.0 / (total_clips * total_actions)),
        (shape((half, count), F32), shape((rows, count), F32), shape((1, 1), F32)),
        [SMEM] + [VMEM] * 3,
    )(core, keep, give, taken)
    return clip_grad, action_grad, loss.reshape(())


def solution(mesh):
    return jax.shard_map(
        functools.partial(shards, mesh.shape["clip"], mesh.shape["act"]),
        mesh=mesh,
        in_specs=(P("act", "clip"), P("clip", "act"), P("clip"), P("act"), P()),
        out_specs=(P("act", "clip"), P("clip", "act"), P()),
        check_vma=False,
    )
```

```python
import functools
import math

import jax
import jax.numpy as jnp
from jax import lax
from jax.experimental import pallas as pl
from jax.experimental.pallas import tpu as pltpu
from jax.sharding import PartitionSpec as P

BF16 = jnp.bfloat16
F32 = jnp.float32
LANES = 128
EXTRA = 16
VMEM = pl.BlockSpec(memory_space=pltpu.VMEM)
SMEM = pl.BlockSpec(memory_space=pltpu.SMEM)


def loss_rows(value, shape):
    high = value.astype(BF16).astype(F32)
    middle = (value - high).astype(BF16).astype(F32)
    low = (value - high - middle).astype(BF16).astype(F32)
    row = lax.broadcasted_iota(jnp.int32, shape, len(shape) - 2)
    rows = jnp.where(row < 4, high, jnp.where(row < 8, middle, jnp.where(row < 12, low, 0.0)))
    return rows.astype(BF16)


def store_blocks(out_ref, values, first_column):
    blocks = out_ref.shape[0]
    rows = values.shape[0] // blocks
    for part in range(values.shape[1] // LANES):
        at = (first_column // LANES + part) * rows
        columns = values[:, part * LANES : (part + 1) * LANES]
        out_ref[:, at : at + rows, :] = columns.reshape(blocks, rows, LANES).astype(BF16)


def block_of(index, blocks):
    return (index // (blocks // 2) + index) % 2


def chunk_kernel(core_ref, mine_ref, other_ref, out_ref):
    blocks = out_ref.shape[0]
    half = mine_ref.shape[0] // 2
    mine = mine_ref[...]
    other = other_ref[...]

    @pl.when(core_ref[0] == 0)
    def _():
        pair = jnp.concatenate([mine[:half], other[:half]], axis=0)
        for block in range(blocks):
            out_ref[block] = pair

    @pl.when(core_ref[0] != 0)
    def _():
        for block in range(blocks):
            out_ref[block] = mine if block_of(block, blocks) else other


def split_kernel(own_ref, positive_ref, robot_ref, low_ref, high_ref):
    width = own_ref.shape[0]
    half = low_ref.shape[1]
    positive = positive_ref[...]
    robots = [robot_ref[:, :half], robot_ref[:, half:]]
    padding = [jnp.zeros_like(robots[0])] * (EXTRA - 4)
    for out_ref, start in ((low_ref, 0), (high_ref, half)):
        part = positive[:, start : start + half]
        rows = jnp.concatenate([part // LANES, part % LANES] + robots + padding, axis=0)
        out_ref[:width, :] = own_ref[:, start : start + half]
        out_ref[width:, :] = rows.astype(F32).astype(BF16)


def transpose_kernel(own_ref, own_t_ref):
    own_t_ref[...] = own_ref[...].T


def sides(start, core_ref, bias_ref, positive_ref, robot_ref, got_rows):
    count = robot_ref.shape[1]
    step = got_rows.shape[1]
    part = slice(start, start + step)
    first = core_ref[0] == 0
    arrived = jnp.concatenate([got_rows[2:3, :], got_rows[3:4, :]], axis=1)
    robot = jnp.where(core_ref[0] == core_ref[2], robot_ref[...].astype(F32), arrived)
    bias = jnp.zeros((1, count), F32)
    for index in range(bias_ref.shape[1]):
        bias = jnp.where(robot == index, bias_ref[:, index : index + 1], bias)
    zero = jnp.zeros((1, count), F32)
    action = (lax.broadcasted_iota(jnp.int32, (1, count), 1) + core_ref[1] * count).astype(F32)
    rows = [jnp.where(first, zero, bias), jnp.where(first, positive_ref[...].astype(F32), action)]
    rows = jnp.concatenate(rows + [zero] * 6, axis=0).T
    column_bias = jnp.where(first, bias, zero)[:, part]
    column_key = jnp.where(first, action[:, part], got_rows[0:1, :] * LANES + got_rows[1:2, :])
    return rows[:, 0:1], rows[:, 1:2], column_bias, column_key


def logits_kernel(scale, start, core_ref, bias_ref, positive_ref, robot_ref, own_ref, own_t_ref, got_ref, before_ref,
                  weights_ref, grad_ref, loss_ref):
    width = own_ref.shape[0]
    got_rows = got_ref[width:, :].astype(F32)
    row_bias, row_key, column_bias, column_key = sides(start, core_ref, bias_ref, positive_ref, robot_ref, got_rows)
    logits = jnp.dot(own_t_ref[...], got_ref[:width, :], preferred_element_type=F32) * scale
    logits = logits + (row_bias + column_bias)
    positive = row_key == column_key
    margin = jnp.where(positive, -logits, logits)
    small = jnp.exp(-jnp.abs(margin))
    above = 1.0 + small
    inverse = 1.0 / above
    log = jnp.log(above) + (small - (above - 1.0)) * inverse
    sigmoid = jnp.where(margin >= 0.0, inverse, small * inverse)
    weights = jnp.where(positive, -sigmoid, sigmoid).astype(BF16)
    weights_ref[...] = weights
    store_blocks(grad_ref, jnp.dot(own_ref[...], weights, preferred_element_type=F32), 0)
    total = jnp.sum(jnp.maximum(margin, 0.0) + log, keepdims=True)
    if before_ref is None:
        loss_ref[...] = jnp.broadcast_to(total, loss_ref.shape)
    else:
        total = jnp.broadcast_to((total + before_ref[0:1, 0:1])[None], loss_ref.shape)
        loss_ref[...] = loss_rows(total, loss_ref.shape)


def low_kernel(scale, *refs):
    logits_kernel(scale, 0, *refs[:7], None, *refs[7:])


def high_kernel(scale, *refs):
    logits_kernel(scale, refs[6].shape[1], *refs)


def received_loss(rows):
    return rows[0:1] + rows[4:5] + rows[8:9]


def second_kernel(low_ref, high_ref, low_weights_ref, high_weights_ref, low_got_ref, high_got_ref, loss_ref, out_ref):
    blocks = out_ref.shape[0]
    step = low_ref.shape[1]
    width = low_ref.shape[0] - EXTRA
    size = width // blocks
    total = loss_ref[0].astype(F32)
    for block in range(1, blocks):
        total = total + loss_ref[block].astype(F32)
    rows = loss_rows(jnp.broadcast_to(received_loss(total), total.shape), total.shape)
    for block in range(blocks):
        out_ref[block, out_ref.shape[1] - EXTRA :, :] = rows
    by_columns = (((1,), (1,)), ((), ()))
    for start, got_ref in ((0, low_got_ref), (step, high_got_ref)):
        half = slice(start, start + step)
        grad = lax.dot_general(low_ref[:width, :], low_weights_ref[half, :], by_columns, preferred_element_type=F32)
        grad += lax.dot_general(high_ref[:width, :], high_weights_ref[half, :], by_columns, preferred_element_type=F32)
        for part in range(step // LANES):
            at = slice(part * size, (part + 1) * size)
            columns = grad[:, part * LANES : (part + 1) * LANES].astype(BF16).reshape(blocks, size, LANES)
            added = columns.astype(F32) + got_ref[:, at, :].astype(F32)
            first = (start // LANES + part) * size
            out_ref[:, first : first + size, :] = added.astype(BF16)


def sum_kernel(clip_scale, action_scale, core_ref, got_ref, keep_ref, give_ref):
    blocks = got_ref.shape[0]
    rows, count = keep_ref.shape
    half = rows // 2

    def over(kind):
        chosen = [block for block in range(blocks) if block_of(block, blocks) == kind]
        total = got_ref[chosen[0]].astype(F32)
        for block in chosen[1:]:
            total = total + got_ref[block].astype(F32)
        return total

    lower = over(0)
    upper = over(1)
    both = lower + upper
    loss = received_loss(both[both.shape[0] - EXTRA :])
    give_ref[rows:, :] = jnp.concatenate([jnp.broadcast_to(loss, (8, LANES))] * (count // LANES), axis=1)
    for part in range(count // LANES):
        columns = slice(part * LANES, (part + 1) * LANES)
        at = slice(part * rows, (part + 1) * rows)

        @pl.when(core_ref[0] == 0)
        def _():
            keep_ref[:half, columns] = both[at][:half] * clip_scale
            give_ref[:half, columns] = both[at][half:] * clip_scale

        @pl.when(core_ref[0] != 0)
        def _():
            keep_ref[:, columns] = upper[at] * action_scale
            give_ref[:rows, columns] = lower[at] * action_scale


def last_kernel(loss_scale, core_ref, keep_ref, give_ref, taken_ref, clip_ref, action_ref, loss_ref):
    rows = keep_ref.shape[0]
    half = clip_ref.shape[0]
    loss_ref[...] = (give_ref[rows : rows + 1, :1] + taken_ref[rows : rows + 1, :1]) * loss_scale

    @pl.when(core_ref[0] == 0)
    def _():
        clip_ref[...] = keep_ref[:half, :]
        action_ref[...] = taken_ref[:rows, :]

    @pl.when(core_ref[0] != 0)
    def _():
        clip_ref[...] = taken_ref[:half, :]
        action_ref[...] = keep_ref[...]


def call(kernel, out_shape, in_specs, scratch=(), flops=0, moved=0):
    return pl.pallas_call(
        kernel,
        out_shape=out_shape,
        in_specs=in_specs,
        out_specs=jax.tree.map(lambda _: VMEM, out_shape),
        scratch_shapes=scratch,
        compiler_params=pltpu.CompilerParams(vmem_limit_bytes=12 * 1024 * 1024),
        cost_estimate=pl.CostEstimate(flops=flops, bytes_accessed=moved, transcendentals=0),
    )


def shards(n_clip, n_act, clips, actions, positive_ids, robot_ids, robot_bias):
    both = ("clip", "act")
    pairs = n_act // 2
    near = n_clip // 2
    along_act = [[[k * n_act + 2 * m + c for m in range(pairs)] for k in range(n_clip)] for c in range(2)]
    along_clip = [[[k * n_act + 2 * m + c for k in range(n_clip)] for m in range(pairs)] for c in range(2)]
    clips_first = along_act[0] + along_clip[1]
    actions_first = along_clip[0] + along_act[1]
    swap = [(i, i ^ 1) for i in range(n_act)]
    gather_pass, scatter_pass = [], []
    for neighbour in (lambda k: (k + near) % n_clip, lambda k: k ^ 1):
        there = [(k * n_act + 2 * m, neighbour(k) * n_act + 2 * m + 1) for k in range(n_clip) for m in range(pairs)]
        here = [(k * n_act + 2 * m, k * n_act + 2 * m + 1) for k in range(n_clip) for m in range(pairs)]
        gather_pass.append(there + [(b, a) for a, b in here])
        scatter_pass.append(here + [(b, a) for a, b in there])
    exchange = functools.partial(lax.all_to_all, axis_name=both, split_axis=0, concat_axis=0)

    half, count = clips.shape
    rows = actions.shape[0]
    width = rows * n_clip
    parts = count // LANES
    act = lax.axis_index("act")
    kind = block_of(lax.axis_index("clip"), n_clip)
    core = jnp.stack([act % 2, act - act % 2 + kind, kind]).astype(jnp.int32)
    shape = jax.ShapeDtypeStruct

    first_core = act % 2 == 0
    clip_twice = jnp.broadcast_to(clips[None], (2, half, count)).reshape(rows, count)
    send = jnp.where(first_core, actions, clip_twice).astype(BF16)
    mine = jnp.where(first_core, clip_twice, actions).astype(BF16)
    other = lax.ppermute(send, "act", swap)
    chunks = call(chunk_kernel, shape((n_clip, rows, count), BF16), [SMEM, VMEM, VMEM])(core, mine, other)
    positive_ids, robot_ids = positive_ids[None, :], robot_ids[None, :]
    own = exchange(chunks, axis_index_groups=clips_first).reshape(width, count)
    halves = shape((width + EXTRA, count // 2), BF16)
    low, high = call(split_kernel, (halves, halves), [VMEM] * 3)(own, positive_ids, robot_ids)
    low = lax.ppermute(low, both, gather_pass[0])
    high = lax.ppermute(high, both, gather_pass[1])
    own_t = call(transpose_kernel, shape((count, width), BF16), [VMEM])(own)

    flops = 2 * width * count * count
    half_blocks = shape((n_clip, parts * rows // 2, LANES), BF16)
    scale = 2.0 / math.sqrt(width)
    fixed = (core, robot_bias[None, :], positive_ids, robot_ids, own, own_t)
    def results(loss):
        return (shape((count, count // 2), BF16), half_blocks, loss)

    cost = {"flops": flops, "moved": 4 * width * count}
    specs = [SMEM] + [VMEM] * 6
    low_weights, low_grad, loss = call(
        functools.partial(low_kernel, scale), results(shape((8, LANES), F32)), specs, **cost
    )(*fixed, low)
    low_got = lax.ppermute(low_grad, both, scatter_pass[0])
    high_weights, high_grad, loss_sent = call(
        functools.partial(high_kernel, scale), results(shape((n_clip, EXTRA, LANES), BF16)), specs + [VMEM], **cost
    )(*fixed, high, loss)
    high_got = lax.ppermute(high_grad, both, scatter_pass[1])
    loss_got = exchange(loss_sent, axis_index_groups=actions_first)
    ready = call(second_kernel, shape((n_clip, parts * rows + EXTRA, LANES), BF16), [VMEM] * 7, **cost)(
        low, high, low_weights, high_weights, low_got, high_got, loss_got
    )
    scattered = exchange(ready, axis_index_groups=clips_first)

    total_clips = count * n_clip
    total_actions = count * n_act
    keep, give = call(
        functools.partial(sum_kernel, 1.0 / math.sqrt(total_actions), 1.0 / math.sqrt(total_clips)),
        (shape((rows, count), F32), shape((rows + 8, count), F32)),
        [SMEM, VMEM],
    )(core, scattered)
    taken = lax.ppermute(give, "act", swap)
    clip_grad, action_grad, loss = call(
        functools.partial(last_kernel, 1.0 / (total_clips * total_actions)),
        (shape((half, count), F32), shape((rows, count), F32), shape((1, 1), F32)),
        [SMEM] + [VMEM] * 3,
    )(core, keep, give, taken)
    return clip_grad, action_grad, loss.reshape(())


def solution(mesh):
    return jax.shard_map(
        functools.partial(shards, mesh.shape["clip"], mesh.shape["act"]),
        mesh=mesh,
        in_specs=(P("act", "clip"), P("clip", "act"), P("clip"), P("act"), P()),
        out_specs=(P("act", "clip"), P("clip", "act"), P()),
        check_vma=False,
    )
```

```python
import functools
import math

import jax
import jax.numpy as jnp
from jax import lax
from jax.experimental import pallas as pl
from jax.experimental.pallas import tpu as pltpu
from jax.sharding import PartitionSpec as P

BF16 = jnp.bfloat16
F32 = jnp.float32
LANES = 128
EXTRA = 16
VMEM = pl.BlockSpec(memory_space=pltpu.VMEM)
SMEM = pl.BlockSpec(memory_space=pltpu.SMEM)


def loss_rows(value, shape):
    high = value.astype(BF16).astype(F32)
    middle = (value - high).astype(BF16).astype(F32)
    low = (value - high - middle).astype(BF16).astype(F32)
    row = lax.broadcasted_iota(jnp.int32, shape, len(shape) - 2)
    rows = jnp.where(row < 4, high, jnp.where(row < 8, middle, jnp.where(row < 12, low, 0.0)))
    return rows.astype(BF16)


def store_blocks(out_ref, values, first_column):
    blocks = out_ref.shape[0]
    rows = values.shape[0] // blocks
    for part in range(values.shape[1] // LANES):
        at = (first_column // LANES + part) * rows
        columns = values[:, part * LANES : (part + 1) * LANES]
        out_ref[:, at : at + rows, :] = columns.reshape(blocks, rows, LANES).astype(BF16)


def block_of(index, blocks):
    return (index // (blocks // 2) + index) % 2


def split_kernel(own_ref, positive_ref, robot_ref, low_ref, high_ref):
    width = own_ref.shape[0]
    half = low_ref.shape[1]
    positive = positive_ref[...]
    robots = [robot_ref[:, :half], robot_ref[:, half:]]
    padding = [jnp.zeros_like(robots[0])] * (EXTRA - 4)
    for out_ref, start in ((low_ref, 0), (high_ref, half)):
        part = positive[:, start : start + half]
        rows = jnp.concatenate([part // LANES, part % LANES] + robots + padding, axis=0)
        out_ref[:width, :] = own_ref[:, start : start + half]
        out_ref[width:, :] = rows.astype(F32).astype(BF16)


def transpose_kernel(own_ref, own_t_ref):
    own_t_ref[...] = own_ref[...].T


def sides(start, core_ref, bias_ref, positive_ref, robot_ref, got_rows):
    count = robot_ref.shape[1]
    step = got_rows.shape[1]
    part = slice(start, start + step)
    first = core_ref[0] == 0
    arrived = jnp.concatenate([got_rows[2:3, :], got_rows[3:4, :]], axis=1)
    robot = jnp.where(core_ref[0] == core_ref[2], robot_ref[...].astype(F32), arrived)
    bias = jnp.zeros((1, count), F32)
    for index in range(bias_ref.shape[1]):
        bias = jnp.where(robot == index, bias_ref[:, index : index + 1], bias)
    zero = jnp.zeros((1, count), F32)
    action = (lax.broadcasted_iota(jnp.int32, (1, count), 1) + core_ref[1] * count).astype(F32)
    rows = [jnp.where(first, zero, bias), jnp.where(first, positive_ref[...].astype(F32), action)]
    rows = jnp.concatenate(rows + [zero] * 6, axis=0).T
    column_bias = jnp.where(first, bias, zero)[:, part]
    column_key = jnp.where(first, action[:, part], got_rows[0:1, :] * LANES + got_rows[1:2, :])
    return rows[:, 0:1], rows[:, 1:2], column_bias, column_key


def logits_kernel(scale, start, core_ref, bias_ref, positive_ref, robot_ref, own_ref, own_t_ref, got_ref, before_ref,
                  weights_ref, grad_ref, loss_ref):
    width = own_ref.shape[0]
    got_rows = got_ref[width:, :].astype(F32)
    row_bias, row_key, column_bias, column_key = sides(start, core_ref, bias_ref, positive_ref, robot_ref, got_rows)
    got = got_ref[:width, :]
    total = jnp.zeros((1, got.shape[1]), F32)
    for row in range(0, own_t_ref.shape[0], LANES):
        part = slice(row, row + LANES)
        logits = jnp.dot(own_t_ref[part, :], got, preferred_element_type=F32) * scale
        logits = logits + (row_bias[part] + column_bias)
        positive = row_key[part] == column_key
        margin = jnp.where(positive, -logits, logits)
        small = jnp.exp(-jnp.abs(margin))
        above = 1.0 + small
        inverse = 1.0 / above
        log = jnp.log(above) + (small - (above - 1.0)) * inverse
        sigmoid = jnp.where(margin >= 0.0, inverse, small * inverse)
        weights_ref[part, :] = jnp.where(positive, -sigmoid, sigmoid).astype(BF16)
        total = total + jnp.sum(jnp.maximum(margin, 0.0) + log, axis=0, keepdims=True)
    store_blocks(grad_ref, jnp.dot(own_ref[...], weights_ref[...], preferred_element_type=F32), 0)
    total = jnp.sum(total, keepdims=True)
    if before_ref is None:
        loss_ref[...] = jnp.broadcast_to(total, loss_ref.shape)
    else:
        total = jnp.broadcast_to((total + before_ref[0:1, 0:1])[None], loss_ref.shape)
        loss_ref[...] = loss_rows(total, loss_ref.shape)


def low_kernel(scale, *refs):
    logits_kernel(scale, 0, *refs[:7], None, *refs[7:])


def high_kernel(scale, *refs):
    logits_kernel(scale, refs[6].shape[1], *refs)


def received_loss(rows):
    return rows[0:1] + rows[4:5] + rows[8:9]


def add_second(start, low_ref, high_ref, low_weights_ref, high_weights_ref, got_ref, out_ref):
    blocks, got_size, _ = got_ref.shape
    step = low_ref.shape[1]
    width = low_ref.shape[0] - EXTRA
    size = width // blocks
    by_columns = (((1,), (1,)), ((), ()))
    half = slice(start, start + step)
    grad = lax.dot_general(low_ref[:width, :], low_weights_ref[half, :], by_columns, preferred_element_type=F32)
    grad += lax.dot_general(high_ref[:width, :], high_weights_ref[half, :], by_columns, preferred_element_type=F32)
    first = start // step * got_size
    for part in range(step // LANES):
        at = slice(part * size, (part + 1) * size)
        columns = grad[:, part * LANES : (part + 1) * LANES].astype(BF16).reshape(blocks, size, LANES)
        added = columns.astype(F32) + got_ref[:, at, :].astype(F32)
        out_ref[:, first + part * size : first + (part + 1) * size, :] = added.astype(BF16)


def second_kernel(low_ref, high_ref, low_weights_ref, high_weights_ref, got_ref, loss_ref, out_ref, rows_ref):
    add_second(0, low_ref, high_ref, low_weights_ref, high_weights_ref, got_ref, out_ref)
    total = loss_ref[0].astype(F32)
    for block in range(1, loss_ref.shape[0]):
        total = total + loss_ref[block].astype(F32)
    rows_ref[...] = loss_rows(jnp.broadcast_to(received_loss(total), total.shape), total.shape)


def third_kernel(low_ref, high_ref, low_weights_ref, high_weights_ref, got_ref, before_ref, rows_ref, out_ref):
    blocks, before, _ = before_ref.shape
    for block in range(blocks):
        out_ref[block, :before, :] = before_ref[block]
        out_ref[block, out_ref.shape[1] - EXTRA :, :] = rows_ref[...]
    add_second(low_ref.shape[1], low_ref, high_ref, low_weights_ref, high_weights_ref, got_ref, out_ref)


def sum_kernel(clip_scale, action_scale, core_ref, got_ref, keep_ref, give_ref):
    blocks = got_ref.shape[0]
    rows, count = keep_ref.shape
    half = rows // 2

    def over(kind):
        chosen = [block for block in range(blocks) if block_of(block, blocks) == kind]
        total = got_ref[chosen[0]].astype(F32)
        for block in chosen[1:]:
            total = total + got_ref[block].astype(F32)
        return total

    lower = over(0)
    upper = over(1)
    both = lower + upper
    loss = received_loss(both[both.shape[0] - EXTRA :])
    give_ref[rows:, :] = jnp.concatenate([jnp.broadcast_to(loss, (8, LANES))] * (count // LANES), axis=1)
    for part in range(count // LANES):
        columns = slice(part * LANES, (part + 1) * LANES)
        at = slice(part * rows, (part + 1) * rows)

        @pl.when(core_ref[0] == 0)
        def _():
            keep_ref[:half, columns] = both[at][:half] * clip_scale
            give_ref[:half, columns] = both[at][half:] * clip_scale

        @pl.when(core_ref[0] != 0)
        def _():
            keep_ref[:, columns] = upper[at] * action_scale
            give_ref[:rows, columns] = lower[at] * action_scale


def last_kernel(loss_scale, core_ref, keep_ref, give_ref, taken_ref, clip_ref, action_ref, loss_ref):
    rows = keep_ref.shape[0]
    half = clip_ref.shape[0]
    loss_ref[...] = (give_ref[rows : rows + 1, :1] + taken_ref[rows : rows + 1, :1]) * loss_scale

    @pl.when(core_ref[0] == 0)
    def _():
        clip_ref[...] = keep_ref[:half, :]
        action_ref[...] = taken_ref[:rows, :]

    @pl.when(core_ref[0] != 0)
    def _():
        clip_ref[...] = taken_ref[:half, :]
        action_ref[...] = keep_ref[...]


def call(kernel, out_shape, in_specs, scratch=(), flops=0, moved=0):
    return pl.pallas_call(
        kernel,
        out_shape=out_shape,
        in_specs=in_specs,
        out_specs=jax.tree.map(lambda _: VMEM, out_shape),
        scratch_shapes=scratch,
        compiler_params=pltpu.CompilerParams(vmem_limit_bytes=12 * 1024 * 1024),
        cost_estimate=pl.CostEstimate(flops=flops, bytes_accessed=moved, transcendentals=0),
    )


def shards(n_clip, n_act, clips, actions, positive_ids, robot_ids, robot_bias):
    both = ("clip", "act")
    pairs = n_act // 2
    near = n_clip // 2
    along_act = [[[k * n_act + 2 * m + c for m in range(pairs)] for k in range(n_clip)] for c in range(2)]
    along_clip = [[[k * n_act + 2 * m + c for k in range(n_clip)] for m in range(pairs)] for c in range(2)]
    clips_first = along_act[0] + along_clip[1]
    actions_first = along_clip[0] + along_act[1]
    swap = [(i, i ^ 1) for i in range(n_act)]
    gather_pass, scatter_pass = [], []
    for neighbour in (lambda k: (k + near) % n_clip, lambda k: k ^ 1):
        there = [(k * n_act + 2 * m, neighbour(k) * n_act + 2 * m + 1) for k in range(n_clip) for m in range(pairs)]
        here = [(k * n_act + 2 * m, k * n_act + 2 * m + 1) for k in range(n_clip) for m in range(pairs)]
        gather_pass.append(there + [(b, a) for a, b in here])
        scatter_pass.append(here + [(b, a) for a, b in there])
    exchange = functools.partial(lax.all_to_all, axis_name=both, split_axis=0, concat_axis=0)

    half, count = clips.shape
    rows = actions.shape[0]
    width = rows * n_clip
    parts = count // LANES
    act = lax.axis_index("act")
    kind = block_of(lax.axis_index("clip"), n_clip)
    core = jnp.stack([act % 2, act - act % 2 + kind, kind]).astype(jnp.int32)
    shape = jax.ShapeDtypeStruct

    first_core = act % 2 == 0
    clip_twice = jnp.broadcast_to(clips[None], (2, half, count)).reshape(rows, count)
    send = jnp.where(first_core, actions, clip_twice).astype(BF16)
    mine = jnp.where(first_core, clip_twice, actions).astype(BF16)
    other = lax.ppermute(send, "act", swap)
    pair = jnp.concatenate([mine[:half], other[:half]], axis=0)
    takes_mine = block_of(jnp.arange(n_clip), n_clip)[:, None, None] == 1
    chunks = jnp.where(first_core, pair[None], jnp.where(takes_mine, mine[None], other[None]))
    positive_ids, robot_ids = positive_ids[None, :], robot_ids[None, :]
    own = exchange(chunks, axis_index_groups=clips_first).reshape(width, count)
    halves = shape((width + EXTRA, count // 2), BF16)
    low, high = call(split_kernel, (halves, halves), [VMEM] * 3)(own, positive_ids, robot_ids)
    low = lax.ppermute(low, both, gather_pass[0])
    high = lax.ppermute(high, both, gather_pass[1])
    own_t = call(transpose_kernel, shape((count, width), BF16), [VMEM])(own)

    flops = 2 * width * count * count
    half_blocks = shape((n_clip, parts * rows // 2, LANES), BF16)
    scale = 2.0 / math.sqrt(width)
    fixed = (core, robot_bias[None, :], positive_ids, robot_ids, own, own_t)
    def results(loss):
        return (shape((count, count // 2), BF16), half_blocks, loss)

    cost = {"flops": flops, "moved": 4 * width * count}
    specs = [SMEM] + [VMEM] * 6
    low_weights, low_grad, loss = call(
        functools.partial(low_kernel, scale), results(shape((8, LANES), F32)), specs, **cost
    )(*fixed, low)
    low_got = lax.ppermute(low_grad, both, scatter_pass[0])
    high_weights, high_grad, loss_sent = call(
        functools.partial(high_kernel, scale), results(shape((n_clip, EXTRA, LANES), BF16)), specs + [VMEM], **cost
    )(*fixed, high, loss)
    high_got = lax.ppermute(high_grad, both, scatter_pass[1])
    loss_got = exchange(loss_sent, axis_index_groups=actions_first)
    operands = (low, high, low_weights, high_weights)
    begun, loss_sum = call(second_kernel, (half_blocks, shape((EXTRA, LANES), BF16)), [VMEM] * 6, **cost)(
        *operands, low_got, loss_got
    )
    ready = call(third_kernel, shape((n_clip, parts * rows + EXTRA, LANES), BF16), [VMEM] * 7, **cost)(
        *operands, high_got, begun, loss_sum
    )
    scattered = exchange(ready, axis_index_groups=clips_first)

    total_clips = count * n_clip
    total_actions = count * n_act
    keep, give = call(
        functools.partial(sum_kernel, 1.0 / math.sqrt(total_actions), 1.0 / math.sqrt(total_clips)),
        (shape((rows, count), F32), shape((rows + 8, count), F32)),
        [SMEM, VMEM],
    )(core, scattered)
    taken = lax.ppermute(give, "act", swap)
    clip_grad, action_grad, loss = call(
        functools.partial(last_kernel, 1.0 / (total_clips * total_actions)),
        (shape((half, count), F32), shape((rows, count), F32), shape((1, 1), F32)),
        [SMEM] + [VMEM] * 3,
    )(core, keep, give, taken)
    return clip_grad, action_grad, loss.reshape(())


def solution(mesh):
    return jax.shard_map(
        functools.partial(shards, mesh.shape["clip"], mesh.shape["act"]),
        mesh=mesh,
        in_specs=(P("act", "clip"), P("clip", "act"), P("clip"), P("act"), P()),
        out_specs=(P("act", "clip"), P("clip", "act"), P()),
        check_vma=False,
    )
```

```python
import functools
import math

import jax
import jax.numpy as jnp
from jax import lax
from jax.experimental import pallas as pl
from jax.experimental.pallas import tpu as pltpu
from jax.sharding import PartitionSpec as P

BF16 = jnp.bfloat16
F32 = jnp.float32
LANES = 128
EXTRA = 16
VMEM = pl.BlockSpec(memory_space=pltpu.VMEM)
ANY = pl.BlockSpec(memory_space=pl.ANY)


def loss_rows(value, shape):
    high = value.astype(BF16).astype(F32)
    middle = (value - high).astype(BF16).astype(F32)
    low = (value - high - middle).astype(BF16).astype(F32)
    row = lax.broadcasted_iota(jnp.int32, shape, len(shape) - 2)
    rows = jnp.where(row < 4, high, jnp.where(row < 8, middle, jnp.where(row < 12, low, 0.0)))
    return rows.astype(BF16)


def store_blocks(out_ref, values, first_column):
    blocks = out_ref.shape[0]
    rows = values.shape[0] // blocks
    for part in range(values.shape[1] // LANES):
        at = (first_column // LANES + part) * rows
        columns = values[:, part * LANES : (part + 1) * LANES]
        out_ref[:, at : at + rows, :] = columns.reshape(blocks, rows, LANES).astype(BF16)


def block_of(index, blocks):
    return (index // (blocks // 2) + index) % 2


def place(n_clip):
    act = lax.axis_index("act")
    core = lax.rem(act, 2)
    clip = lax.axis_index("clip")
    kind = lax.rem(lax.div(clip, n_clip // 2) + clip, 2)
    return core, kind, act - core + kind


def split_kernel(own_ref, positive_ref, robot_ref, low_ref, high_ref):
    width = own_ref.shape[0]
    half = low_ref.shape[1]
    positive = positive_ref[...]
    robots = [robot_ref[:, :half], robot_ref[:, half:]]
    padding = [jnp.zeros_like(robots[0])] * (EXTRA - 4)
    for out_ref, start in ((low_ref, 0), (high_ref, half)):
        part = positive[:, start : start + half]
        rows = jnp.concatenate([part // LANES, part % LANES] + robots + padding, axis=0)
        out_ref[:width, :] = own_ref[:, start : start + half]
        out_ref[width:, :] = rows.astype(F32).astype(BF16)


def transpose_kernel(own_ref, own_t_ref):
    own_t_ref[...] = own_ref[...].T


def sides(n_clip, start, bias_ref, positive_ref, robot_ref, got_rows):
    count = robot_ref.shape[1]
    step = got_rows.shape[1]
    part = slice(start, start + step)
    core, kind, index = place(n_clip)
    first = core == 0
    arrived = jnp.concatenate([got_rows[2:3, :], got_rows[3:4, :]], axis=1)
    robot = jnp.where(core == kind, robot_ref[...].astype(F32), arrived)
    bias = jnp.zeros((1, count), F32)
    for each in range(bias_ref.shape[1]):
        bias = jnp.where(robot == each, bias_ref[:, each : each + 1], bias)
    zero = jnp.zeros((1, count), F32)
    action = (lax.broadcasted_iota(jnp.int32, (1, count), 1) + index * count).astype(F32)
    rows = [jnp.where(first, zero, bias), jnp.where(first, positive_ref[...].astype(F32), action)]
    rows = jnp.concatenate(rows + [zero] * 6, axis=0).T
    column_bias = jnp.where(first, bias, zero)[:, part]
    column_key = jnp.where(first, action[:, part], got_rows[0:1, :] * LANES + got_rows[1:2, :])
    return rows[:, 0:1], rows[:, 1:2], column_bias, column_key


def logits_kernel(n_clip, scale, start, bias_ref, positive_ref, robot_ref, own_ref, own_t_ref, got_ref, before_ref,
                  weights_ref, grad_ref, loss_ref):
    width = own_ref.shape[0]
    got_rows = got_ref[width:, :].astype(F32)
    row_bias, row_key, column_bias, column_key = sides(n_clip, start, bias_ref, positive_ref, robot_ref, got_rows)
    got = got_ref[:width, :]
    total = jnp.zeros((1, got.shape[1]), F32)
    for row in range(0, own_t_ref.shape[0], LANES):
        part = slice(row, row + LANES)
        logits = jnp.dot(own_t_ref[part, :], got, preferred_element_type=F32) * scale
        logits = logits + (row_bias[part] + column_bias)
        positive = row_key[part] == column_key
        margin = jnp.where(positive, -logits, logits)
        small = jnp.exp(-jnp.abs(margin))
        above = 1.0 + small
        inverse = 1.0 / above
        log = jnp.log(above) + (small - (above - 1.0)) * inverse
        sigmoid = jnp.where(margin >= 0.0, inverse, small * inverse)
        weights_ref[part, :] = jnp.where(positive, -sigmoid, sigmoid).astype(BF16)
        total = total + jnp.sum(jnp.maximum(margin, 0.0) + log, axis=0, keepdims=True)
    store_blocks(grad_ref, jnp.dot(own_ref[...], weights_ref[...], preferred_element_type=F32), 0)
    total = jnp.sum(total, keepdims=True)
    if before_ref is None:
        loss_ref[...] = jnp.broadcast_to(total, loss_ref.shape)
    else:
        total = jnp.broadcast_to((total + before_ref[0:1, 0:1])[None], loss_ref.shape)
        loss_ref[...] = loss_rows(total, loss_ref.shape)


def low_kernel(n_clip, scale, *refs):
    logits_kernel(n_clip, scale, 0, *refs[:6], None, *refs[6:])


def high_kernel(n_clip, scale, *refs):
    logits_kernel(n_clip, scale, refs[5].shape[1], *refs)


def received_loss(rows):
    return rows[0:1] + rows[4:5] + rows[8:9]


def add_second(start, low_ref, high_ref, low_weights_ref, high_weights_ref, got_ref, out_ref):
    blocks, got_size, _ = got_ref.shape
    step = low_ref.shape[1]
    width = low_ref.shape[0] - EXTRA
    size = width // blocks
    by_columns = (((1,), (1,)), ((), ()))
    half = slice(start, start + step)
    grad = lax.dot_general(low_ref[:width, :], low_weights_ref[half, :], by_columns, preferred_element_type=F32)
    grad += lax.dot_general(high_ref[:width, :], high_weights_ref[half, :], by_columns, preferred_element_type=F32)
    first = start // step * got_size
    for part in range(step // LANES):
        at = slice(part * size, (part + 1) * size)
        columns = grad[:, part * LANES : (part + 1) * LANES].astype(BF16).reshape(blocks, size, LANES)
        added = columns.astype(F32) + got_ref[:, at, :].astype(F32)
        out_ref[:, first + part * size : first + (part + 1) * size, :] = added.astype(BF16)


def second_kernel(low_ref, high_ref, low_weights_ref, high_weights_ref, got_ref, loss_ref, out_ref, rows_ref):
    add_second(0, low_ref, high_ref, low_weights_ref, high_weights_ref, got_ref, out_ref)
    total = loss_ref[0].astype(F32)
    for block in range(1, loss_ref.shape[0]):
        total = total + loss_ref[block].astype(F32)
    rows_ref[...] = loss_rows(jnp.broadcast_to(received_loss(total), total.shape), total.shape)


def third_kernel(low_ref, high_ref, low_weights_ref, high_weights_ref, got_ref, before_ref, rows_ref, out_ref):
    blocks, before, _ = before_ref.shape
    for block in range(blocks):
        out_ref[block, :before, :] = before_ref[block]
        out_ref[block, out_ref.shape[1] - EXTRA :, :] = rows_ref[...]
    add_second(low_ref.shape[1], low_ref, high_ref, low_weights_ref, high_weights_ref, got_ref, out_ref)


def sum_kernel(clip_scale, action_scale, got_ref, keep_ref, give_ref):
    blocks = got_ref.shape[0]
    rows, count = keep_ref.shape
    half = rows // 2
    core = place(blocks)[0]

    def over(kind):
        chosen = [block for block in range(blocks) if block_of(block, blocks) == kind]
        total = got_ref[chosen[0]].astype(F32)
        for block in chosen[1:]:
            total = total + got_ref[block].astype(F32)
        return total

    lower = over(0)
    upper = over(1)
    both = lower + upper
    loss = received_loss(both[both.shape[0] - EXTRA :])
    give_ref[rows:, :] = jnp.concatenate([jnp.broadcast_to(loss, (8, LANES))] * (count // LANES), axis=1)
    for part in range(count // LANES):
        columns = slice(part * LANES, (part + 1) * LANES)
        at = slice(part * rows, (part + 1) * rows)

        @pl.when(core == 0)
        def _():
            keep_ref[:half, columns] = both[at][:half] * clip_scale
            give_ref[:half, columns] = both[at][half:] * clip_scale

        @pl.when(core != 0)
        def _():
            keep_ref[:, columns] = upper[at] * action_scale
            give_ref[:rows, columns] = lower[at] * action_scale


def last_kernel(n_clip, loss_scale, keep_ref, give_ref, taken_ref, clip_ref, action_ref, loss_ref, sent):
    rows = keep_ref.shape[0]
    half = clip_ref.shape[0]
    core = place(n_clip)[0]

    def write(clip, action):
        copies = [pltpu.make_async_copy(clip, clip_ref, sent.at[0]), pltpu.make_async_copy(action, action_ref, sent.at[1])]
        for copy in copies:
            copy.start()
        for copy in copies:
            copy.wait()

    @pl.when(core == 0)
    def _():
        write(keep_ref.at[:half, :], taken_ref.at[:rows, :])

    @pl.when(core != 0)
    def _():
        write(taken_ref.at[:half, :], keep_ref)

    loss_ref[...] = (give_ref[rows : rows + 1, :1] + taken_ref[rows : rows + 1, :1]) * loss_scale


def call(kernel, out_shape, in_specs, out_specs=None, scratch=(), flops=0, moved=0):
    return pl.pallas_call(
        kernel,
        out_shape=out_shape,
        in_specs=in_specs,
        out_specs=jax.tree.map(lambda _: VMEM, out_shape) if out_specs is None else out_specs,
        scratch_shapes=scratch,
        compiler_params=pltpu.CompilerParams(vmem_limit_bytes=12 * 1024 * 1024),
        cost_estimate=pl.CostEstimate(flops=flops, bytes_accessed=moved, transcendentals=0),
    )


def shards(n_clip, n_act, clips, actions, positive_ids, robot_ids, robot_bias):
    both = ("clip", "act")
    pairs = n_act // 2
    near = n_clip // 2
    along_act = [[[k * n_act + 2 * m + c for m in range(pairs)] for k in range(n_clip)] for c in range(2)]
    along_clip = [[[k * n_act + 2 * m + c for k in range(n_clip)] for m in range(pairs)] for c in range(2)]
    clips_first = along_act[0] + along_clip[1]
    actions_first = along_clip[0] + along_act[1]
    swap = [(i, i ^ 1) for i in range(n_act)]
    gather_pass, scatter_pass = [], []
    for neighbour in (lambda k: (k + near) % n_clip, lambda k: k ^ 1):
        there = [(k * n_act + 2 * m, neighbour(k) * n_act + 2 * m + 1) for k in range(n_clip) for m in range(pairs)]
        here = [(k * n_act + 2 * m, k * n_act + 2 * m + 1) for k in range(n_clip) for m in range(pairs)]
        gather_pass.append(there + [(b, a) for a, b in here])
        scatter_pass.append(here + [(b, a) for a, b in there])
    exchange = functools.partial(lax.all_to_all, axis_name=both, split_axis=0, concat_axis=0)

    half, count = clips.shape
    rows = actions.shape[0]
    width = rows * n_clip
    parts = count // LANES
    act = lax.axis_index("act")
    shape = jax.ShapeDtypeStruct

    first_core = act % 2 == 0
    clip_twice = jnp.broadcast_to(clips[None], (2, half, count)).reshape(rows, count)
    send = jnp.where(first_core, actions, clip_twice).astype(BF16)
    mine = jnp.where(first_core, clip_twice, actions).astype(BF16)
    other = lax.ppermute(send, "act", swap)
    pair = jnp.concatenate([mine[:half], other[:half]], axis=0)
    takes_mine = block_of(jnp.arange(n_clip), n_clip)[:, None, None] == 1
    chunks = jnp.where(first_core, pair[None], jnp.where(takes_mine, mine[None], other[None]))
    positive_ids, robot_ids = positive_ids[None, :], robot_ids[None, :]
    own = exchange(chunks, axis_index_groups=clips_first).reshape(width, count)
    halves = shape((width + EXTRA, count // 2), BF16)
    low, high = call(split_kernel, (halves, halves), [VMEM] * 3)(own, positive_ids, robot_ids)
    low = lax.ppermute(low, both, gather_pass[0])
    high = lax.ppermute(high, both, gather_pass[1])
    own_t = call(transpose_kernel, shape((count, width), BF16), [VMEM])(own)

    flops = 2 * width * count * count
    half_blocks = shape((n_clip, parts * rows // 2, LANES), BF16)
    scale = 2.0 / math.sqrt(width)
    fixed = (robot_bias[None, :], positive_ids, robot_ids, own, own_t)
    def results(loss):
        return (shape((count, count // 2), BF16), half_blocks, loss)

    cost = {"flops": flops, "moved": 4 * width * count}
    specs = [VMEM] * 6
    low_weights, low_grad, loss = call(
        functools.partial(low_kernel, n_clip, scale), results(shape((8, LANES), F32)), specs, **cost
    )(*fixed, low)
    low_got = lax.ppermute(low_grad, both, scatter_pass[0])
    high_weights, high_grad, loss_sent = call(
        functools.partial(high_kernel, n_clip, scale), results(shape((n_clip, EXTRA, LANES), BF16)), specs + [VMEM], **cost
    )(*fixed, high, loss)
    high_got = lax.ppermute(high_grad, both, scatter_pass[1])
    loss_got = exchange(loss_sent, axis_index_groups=actions_first)
    operands = (low, high, low_weights, high_weights)
    begun, loss_sum = call(second_kernel, (half_blocks, shape((EXTRA, LANES), BF16)), [VMEM] * 6, **cost)(
        *operands, low_got, loss_got
    )
    ready = call(third_kernel, shape((n_clip, parts * rows + EXTRA, LANES), BF16), [VMEM] * 7, **cost)(
        *operands, high_got, begun, loss_sum
    )
    scattered = exchange(ready, axis_index_groups=clips_first)

    total_clips = count * n_clip
    total_actions = count * n_act
    keep, give = call(
        functools.partial(sum_kernel, 1.0 / math.sqrt(total_actions), 1.0 / math.sqrt(total_clips)),
        (shape((rows, count), F32), shape((rows + 8, count), F32)),
        [VMEM],
    )(scattered)
    taken = lax.ppermute(give, "act", swap)
    clip_grad, action_grad, loss = call(
        functools.partial(last_kernel, n_clip, 1.0 / (total_clips * total_actions)),
        (shape((half, count), F32), shape((rows, count), F32), shape((1, 1), F32)),
        [VMEM] * 3,
        (ANY, ANY, VMEM),
        [pltpu.SemaphoreType.DMA((2,))],
    )(keep, give, taken)
    return clip_grad, action_grad, loss.reshape(())


def solution(mesh):
    return jax.shard_map(
        functools.partial(shards, mesh.shape["clip"], mesh.shape["act"]),
        mesh=mesh,
        in_specs=(P("act", "clip"), P("clip", "act"), P("clip"), P("act"), P()),
        out_specs=(P("act", "clip"), P("clip", "act"), P()),
        check_vma=False,
    )
```

```python
import functools
import math

import jax
import jax.numpy as jnp
from jax import lax
from jax.experimental import pallas as pl
from jax.experimental.pallas import tpu as pltpu
from jax.sharding import PartitionSpec as P

BF16 = jnp.bfloat16
F32 = jnp.float32
LANES = 128
EXTRA = 16
VMEM = pl.BlockSpec(memory_space=pltpu.VMEM)
ANY = pl.BlockSpec(memory_space=pl.ANY)


def loss_rows(value, shape):
    high = value.astype(BF16).astype(F32)
    middle = (value - high).astype(BF16).astype(F32)
    low = (value - high - middle).astype(BF16).astype(F32)
    row = lax.broadcasted_iota(jnp.int32, shape, len(shape) - 2)
    rows = jnp.where(row < 4, high, jnp.where(row < 8, middle, jnp.where(row < 12, low, 0.0)))
    return rows.astype(BF16)


def store_blocks(out_ref, values, first_column):
    blocks = out_ref.shape[0]
    rows = values.shape[0] // blocks
    for part in range(values.shape[1] // LANES):
        at = (first_column // LANES + part) * rows
        columns = values[:, part * LANES : (part + 1) * LANES]
        out_ref[:, at : at + rows, :] = columns.reshape(blocks, rows, LANES).astype(BF16)


def block_of(index, blocks):
    return (index // (blocks // 2) + index) % 2


def place(n_clip):
    act = lax.axis_index("act")
    core = lax.rem(act, 2)
    clip = lax.axis_index("clip")
    kind = lax.rem(lax.div(clip, n_clip // 2) + clip, 2)
    return core, kind, act - core + kind


def split_kernel(own_ref, positive_ref, robot_ref, low_ref, high_ref):
    width = own_ref.shape[0]
    half = low_ref.shape[1]
    positive = positive_ref[...]
    robots = [robot_ref[:, :half], robot_ref[:, half:]]
    padding = [jnp.zeros_like(robots[0])] * (EXTRA - 4)
    for out_ref, start in ((low_ref, 0), (high_ref, half)):
        part = positive[:, start : start + half]
        rows = jnp.concatenate([part // LANES, part % LANES] + robots + padding, axis=0)
        out_ref[:width, :] = own_ref[:, start : start + half]
        out_ref[width:, :] = rows.astype(F32).astype(BF16)


def transpose_kernel(own_ref, own_t_ref):
    own_t_ref[...] = own_ref[...].T


def sides(n_clip, start, bias_ref, positive_ref, robot_ref, got_rows):
    count = robot_ref.shape[1]
    step = got_rows.shape[1]
    part = slice(start, start + step)
    core, kind, index = place(n_clip)
    first = core == 0
    arrived = jnp.concatenate([got_rows[2:3, :], got_rows[3:4, :]], axis=1)
    robot = jnp.where(core == kind, robot_ref[...].astype(F32), arrived)
    bias = jnp.zeros((1, count), F32)
    for each in range(bias_ref.shape[1]):
        bias = jnp.where(robot == each, bias_ref[:, each : each + 1], bias)
    zero = jnp.zeros((1, count), F32)
    action = (lax.broadcasted_iota(jnp.int32, (1, count), 1) + index * count).astype(F32)
    rows = [jnp.where(first, zero, bias), jnp.where(first, positive_ref[...].astype(F32), action)]
    rows = jnp.concatenate(rows + [zero] * 6, axis=0).T
    column_bias = jnp.where(first, bias, zero)[:, part]
    column_key = jnp.where(first, action[:, part], got_rows[0:1, :] * LANES + got_rows[1:2, :])
    return rows[:, 0:1], rows[:, 1:2], column_bias, column_key


def logits_kernel(n_clip, scale, start, bias_ref, positive_ref, robot_ref, own_ref, own_t_ref, got_ref, before_ref,
                  weights_ref, grad_ref, loss_ref):
    width = own_ref.shape[0]
    got_rows = got_ref[width:, :].astype(F32)
    row_bias, row_key, column_bias, column_key = sides(n_clip, start, bias_ref, positive_ref, robot_ref, got_rows)
    got = got_ref[:width, :]
    total = jnp.zeros((1, got.shape[1]), F32)
    for row in range(0, own_t_ref.shape[0], LANES):
        part = slice(row, row + LANES)
        logits = jnp.dot(own_t_ref[part, :], got, preferred_element_type=F32) * scale
        logits = logits + (row_bias[part] + column_bias)
        positive = row_key[part] == column_key
        margin = jnp.where(positive, -logits, logits)
        small = jnp.exp(-jnp.abs(margin))
        above = 1.0 + small
        inverse = 1.0 / above
        log = jnp.log(above) + (small - (above - 1.0)) * inverse
        sigmoid = jnp.where(margin >= 0.0, inverse, small * inverse)
        weights_ref[part, :] = jnp.where(positive, -sigmoid, sigmoid).astype(BF16)
        total = total + jnp.sum(jnp.maximum(margin, 0.0) + log, axis=0, keepdims=True)
    store_blocks(grad_ref, jnp.dot(own_ref[...], weights_ref[...], preferred_element_type=F32), 0)
    total = jnp.sum(total, keepdims=True)
    if before_ref is None:
        loss_ref[...] = jnp.broadcast_to(total, loss_ref.shape)
    else:
        total = jnp.broadcast_to((total + before_ref[0:1, 0:1])[None], loss_ref.shape)
        loss_ref[...] = loss_rows(total, loss_ref.shape)


def low_kernel(n_clip, scale, *refs):
    logits_kernel(n_clip, scale, 0, *refs[:6], None, *refs[6:])


def high_kernel(n_clip, scale, *refs):
    logits_kernel(n_clip, scale, refs[5].shape[1], *refs)


def received_loss(rows):
    return rows[0:1] + rows[4:5] + rows[8:9]


def second_kernel(low_ref, high_ref, low_weights_ref, high_weights_ref, low_got_ref, high_got_ref, loss_ref, out_ref):
    blocks = out_ref.shape[0]
    step = low_ref.shape[1]
    width = low_ref.shape[0] - EXTRA
    size = width // blocks
    total = loss_ref[0].astype(F32)
    for block in range(1, blocks):
        total = total + loss_ref[block].astype(F32)
    rows = loss_rows(jnp.broadcast_to(received_loss(total), total.shape), total.shape)
    for block in range(blocks):
        out_ref[block, out_ref.shape[1] - EXTRA :, :] = rows
    by_columns = (((1,), (1,)), ((), ()))
    for start, got_ref in ((0, low_got_ref), (step, high_got_ref)):
        half = slice(start, start + step)
        grad = lax.dot_general(low_ref[:width, :], low_weights_ref[half, :], by_columns, preferred_element_type=F32)
        grad += lax.dot_general(high_ref[:width, :], high_weights_ref[half, :], by_columns, preferred_element_type=F32)
        for part in range(step // LANES):
            at = slice(part * size, (part + 1) * size)
            columns = grad[:, part * LANES : (part + 1) * LANES].astype(BF16).reshape(blocks, size, LANES)
            added = columns.astype(F32) + got_ref[:, at, :].astype(F32)
            first = (start // LANES + part) * size
            out_ref[:, first : first + size, :] = added.astype(BF16)


def sum_kernel(clip_scale, action_scale, got_ref, keep_ref, give_ref):
    blocks = got_ref.shape[0]
    rows, count = keep_ref.shape
    half = rows // 2
    core = place(blocks)[0]

    def over(kind):
        chosen = [block for block in range(blocks) if block_of(block, blocks) == kind]
        total = got_ref[chosen[0]].astype(F32)
        for block in chosen[1:]:
            total = total + got_ref[block].astype(F32)
        return total

    lower = over(0)
    upper = over(1)
    both = lower + upper
    loss = received_loss(both[both.shape[0] - EXTRA :])
    give_ref[rows:, :] = jnp.concatenate([jnp.broadcast_to(loss, (8, LANES))] * (count // LANES), axis=1)
    for part in range(count // LANES):
        columns = slice(part * LANES, (part + 1) * LANES)
        at = slice(part * rows, (part + 1) * rows)

        @pl.when(core == 0)
        def _():
            keep_ref[:half, columns] = both[at][:half] * clip_scale
            give_ref[:half, columns] = both[at][half:] * clip_scale

        @pl.when(core != 0)
        def _():
            keep_ref[:, columns] = upper[at] * action_scale
            give_ref[:rows, columns] = lower[at] * action_scale


def last_kernel(n_clip, loss_scale, keep_ref, give_ref, taken_ref, clip_ref, action_ref, loss_ref, sent):
    rows = keep_ref.shape[0]
    half = clip_ref.shape[0]
    core = place(n_clip)[0]

    def write(clip, action):
        copies = [pltpu.make_async_copy(clip, clip_ref, sent.at[0]), pltpu.make_async_copy(action, action_ref, sent.at[1])]
        for copy in copies:
            copy.start()
        for copy in copies:
            copy.wait()

    @pl.when(core == 0)
    def _():
        write(keep_ref.at[:half, :], taken_ref.at[:rows, :])

    @pl.when(core != 0)
    def _():
        write(taken_ref.at[:half, :], keep_ref)

    loss_ref[...] = (give_ref[rows : rows + 1, :1] + taken_ref[rows : rows + 1, :1]) * loss_scale


def call(kernel, out_shape, in_specs, out_specs=None, scratch=(), flops=0, moved=0):
    return pl.pallas_call(
        kernel,
        out_shape=out_shape,
        in_specs=in_specs,
        out_specs=jax.tree.map(lambda _: VMEM, out_shape) if out_specs is None else out_specs,
        scratch_shapes=scratch,
        compiler_params=pltpu.CompilerParams(vmem_limit_bytes=12 * 1024 * 1024),
        cost_estimate=pl.CostEstimate(flops=flops, bytes_accessed=moved, transcendentals=0),
    )


def shards(n_clip, n_act, clips, actions, positive_ids, robot_ids, robot_bias):
    both = ("clip", "act")
    pairs = n_act // 2
    near = n_clip // 2
    along_act = [[[k * n_act + 2 * m + c for m in range(pairs)] for k in range(n_clip)] for c in range(2)]
    along_clip = [[[k * n_act + 2 * m + c for k in range(n_clip)] for m in range(pairs)] for c in range(2)]
    clips_first = along_act[0] + along_clip[1]
    actions_first = along_clip[0] + along_act[1]
    swap = [(i, i ^ 1) for i in range(n_act)]
    gather_pass, scatter_pass = [], []
    for neighbour in (lambda k: (k + near) % n_clip, lambda k: k ^ 1):
        there = [(k * n_act + 2 * m, neighbour(k) * n_act + 2 * m + 1) for k in range(n_clip) for m in range(pairs)]
        here = [(k * n_act + 2 * m, k * n_act + 2 * m + 1) for k in range(n_clip) for m in range(pairs)]
        gather_pass.append(there + [(b, a) for a, b in here])
        scatter_pass.append(here + [(b, a) for a, b in there])
    exchange = functools.partial(lax.all_to_all, axis_name=both, split_axis=0, concat_axis=0)

    half, count = clips.shape
    rows = actions.shape[0]
    width = rows * n_clip
    parts = count // LANES
    act = lax.axis_index("act")
    shape = jax.ShapeDtypeStruct

    first_core = act % 2 == 0
    clip_twice = jnp.broadcast_to(clips[None], (2, half, count)).reshape(rows, count)
    send = jnp.where(first_core, actions, clip_twice).astype(BF16)
    mine = jnp.where(first_core, clip_twice, actions).astype(BF16)
    other = lax.ppermute(send, "act", swap)
    pair = jnp.concatenate([mine[:half], other[:half]], axis=0)
    takes_mine = block_of(jnp.arange(n_clip), n_clip)[:, None, None] == 1
    chunks = jnp.where(first_core, pair[None], jnp.where(takes_mine, mine[None], other[None]))
    positive_ids, robot_ids = positive_ids[None, :], robot_ids[None, :]
    own = exchange(chunks, axis_index_groups=clips_first).reshape(width, count)
    halves = shape((width + EXTRA, count // 2), BF16)
    low, high = call(split_kernel, (halves, halves), [VMEM] * 3)(own, positive_ids, robot_ids)
    low = lax.ppermute(low, both, gather_pass[0])
    high = lax.ppermute(high, both, gather_pass[1])
    own_t = call(transpose_kernel, shape((count, width), BF16), [VMEM])(own)

    flops = 2 * width * count * count
    half_blocks = shape((n_clip, parts * rows // 2, LANES), BF16)
    scale = 2.0 / math.sqrt(width)
    fixed = (robot_bias[None, :], positive_ids, robot_ids, own, own_t)
    def results(loss):
        return (shape((count, count // 2), BF16), half_blocks, loss)

    cost = {"flops": flops, "moved": 4 * width * count}
    specs = [VMEM] * 6
    low_weights, low_grad, loss = call(
        functools.partial(low_kernel, n_clip, scale), results(shape((8, LANES), F32)), specs, **cost
    )(*fixed, low)
    low_got = lax.ppermute(low_grad, both, scatter_pass[0])
    high_weights, high_grad, loss_sent = call(
        functools.partial(high_kernel, n_clip, scale), results(shape((n_clip, EXTRA, LANES), BF16)), specs + [VMEM], **cost
    )(*fixed, high, loss)
    high_got = lax.ppermute(high_grad, both, scatter_pass[1])
    loss_got = exchange(loss_sent, axis_index_groups=actions_first)
    operands = (low, high, low_weights, high_weights)
    low_got, loss_got = lax.optimization_barrier((low_got, loss_got))
    ready = call(second_kernel, shape((n_clip, parts * rows + EXTRA, LANES), BF16), [VMEM] * 7, **cost)(
        *operands, low_got, high_got, loss_got
    )
    scattered = exchange(ready, axis_index_groups=clips_first)

    total_clips = count * n_clip
    total_actions = count * n_act
    keep, give = call(
        functools.partial(sum_kernel, 1.0 / math.sqrt(total_actions), 1.0 / math.sqrt(total_clips)),
        (shape((rows, count), F32), shape((rows + 8, count), F32)),
        [VMEM],
    )(scattered)
    taken = lax.ppermute(give, "act", swap)
    clip_grad, action_grad, loss = call(
        functools.partial(last_kernel, n_clip, 1.0 / (total_clips * total_actions)),
        (shape((half, count), F32), shape((rows, count), F32), shape((1, 1), F32)),
        [VMEM] * 3,
        (ANY, ANY, VMEM),
        [pltpu.SemaphoreType.DMA((2,))],
    )(keep, give, taken)
    return clip_grad, action_grad, loss.reshape(())


def solution(mesh):
    return jax.shard_map(
        functools.partial(shards, mesh.shape["clip"], mesh.shape["act"]),
        mesh=mesh,
        in_specs=(P("act", "clip"), P("clip", "act"), P("clip"), P("act"), P()),
        out_specs=(P("act", "clip"), P("clip", "act"), P()),
        check_vma=False,
    )
```

```python
import functools
import math

import jax
import jax.numpy as jnp
from jax import lax
from jax.experimental import pallas as pl
from jax.experimental.pallas import tpu as pltpu
from jax.sharding import PartitionSpec as P

BF16 = jnp.bfloat16
F32 = jnp.float32
LANES = 128
EXTRA = 16
VMEM = pl.BlockSpec(memory_space=pltpu.VMEM)
ANY = pl.BlockSpec(memory_space=pl.ANY)


def loss_rows(value, shape):
    high = value.astype(BF16).astype(F32)
    middle = (value - high).astype(BF16).astype(F32)
    low = (value - high - middle).astype(BF16).astype(F32)
    row = lax.broadcasted_iota(jnp.int32, shape, len(shape) - 2)
    rows = jnp.where(row < 4, high, jnp.where(row < 8, middle, jnp.where(row < 12, low, 0.0)))
    return rows.astype(BF16)


def store_blocks(out_ref, values, first_column):
    blocks = out_ref.shape[0]
    rows = values.shape[0] // blocks
    for part in range(values.shape[1] // LANES):
        at = (first_column // LANES + part) * rows
        columns = values[:, part * LANES : (part + 1) * LANES]
        out_ref[:, at : at + rows, :] = columns.reshape(blocks, rows, LANES).astype(BF16)


def block_of(index, blocks):
    return (index // (blocks // 2) + index) % 2


def place(n_clip):
    act = lax.axis_index("act")
    core = lax.rem(act, 2)
    clip = lax.axis_index("clip")
    kind = lax.rem(lax.div(clip, n_clip // 2) + clip, 2)
    return core, kind, act - core + kind


def split_kernel(own_ref, positive_ref, robot_ref, low_ref, high_ref):
    width = own_ref.shape[0]
    half = low_ref.shape[1]
    positive = positive_ref[...]
    robots = [robot_ref[:, :half], robot_ref[:, half:]]
    padding = [jnp.zeros_like(robots[0])] * (EXTRA - 4)
    for out_ref, start in ((low_ref, 0), (high_ref, half)):
        part = positive[:, start : start + half]
        rows = jnp.concatenate([part // LANES, part % LANES] + robots + padding, axis=0)
        out_ref[:width, :] = own_ref[:, start : start + half]
        out_ref[width:, :] = rows.astype(F32).astype(BF16)


def transpose_kernel(own_ref, own_t_ref):
    own_t_ref[...] = own_ref[...].T


def sides(n_clip, start, bias_ref, positive_ref, robot_ref, got_rows):
    count = robot_ref.shape[1]
    step = got_rows.shape[1]
    part = slice(start, start + step)
    core, kind, index = place(n_clip)
    first = core == 0
    arrived = jnp.concatenate([got_rows[2:3, :], got_rows[3:4, :]], axis=1)
    robot = jnp.where(core == kind, robot_ref[...].astype(F32), arrived)
    bias = jnp.zeros((1, count), F32)
    for each in range(bias_ref.shape[1]):
        bias = jnp.where(robot == each, bias_ref[:, each : each + 1], bias)
    zero = jnp.zeros((1, count), F32)
    action = (lax.broadcasted_iota(jnp.int32, (1, count), 1) + index * count).astype(F32)
    rows = [jnp.where(first, zero, bias), jnp.where(first, positive_ref[...].astype(F32), action)]
    rows = jnp.concatenate(rows + [zero] * 6, axis=0).T
    column_bias = jnp.where(first, bias, zero)[:, part]
    column_key = jnp.where(first, action[:, part], got_rows[0:1, :] * LANES + got_rows[1:2, :])
    return rows[:, 0:1], rows[:, 1:2], column_bias, column_key


def logits_kernel(n_clip, scale, start, bias_ref, positive_ref, robot_ref, own_ref, own_t_ref, got_ref, before_ref,
                  weights_ref, grad_ref, loss_ref):
    width = own_ref.shape[0]
    got_rows = got_ref[width:, :].astype(F32)
    row_bias, row_key, column_bias, column_key = sides(n_clip, start, bias_ref, positive_ref, robot_ref, got_rows)
    got = got_ref[:width, :]
    total = jnp.zeros((1, got.shape[1]), F32)
    for row in range(0, own_t_ref.shape[0], LANES):
        part = slice(row, row + LANES)
        logits = jnp.dot(own_t_ref[part, :], got, preferred_element_type=F32) * scale
        logits = logits + (row_bias[part] + column_bias)
        positive = row_key[part] == column_key
        margin = jnp.where(positive, -logits, logits)
        small = jnp.exp(-jnp.abs(margin))
        above = 1.0 + small
        inverse = 1.0 / above
        log = jnp.log(above) + (small - (above - 1.0)) * inverse
        sigmoid = jnp.where(margin >= 0.0, inverse, small * inverse)
        weights_ref[part, :] = jnp.where(positive, -sigmoid, sigmoid).astype(BF16)
        total = total + jnp.sum(jnp.maximum(margin, 0.0) + log, axis=0, keepdims=True)
    store_blocks(grad_ref, jnp.dot(own_ref[...], weights_ref[...], preferred_element_type=F32), 0)
    total = jnp.sum(total, keepdims=True)
    if before_ref is None:
        loss_ref[...] = jnp.broadcast_to(total, loss_ref.shape)
    else:
        total = jnp.broadcast_to((total + before_ref[0:1, 0:1])[None], loss_ref.shape)
        loss_ref[...] = loss_rows(total, loss_ref.shape)


def low_kernel(n_clip, scale, *refs):
    logits_kernel(n_clip, scale, 0, *refs[:6], None, *refs[6:])


def high_kernel(n_clip, scale, *refs):
    logits_kernel(n_clip, scale, refs[5].shape[1], *refs)


def received_loss(rows):
    return rows[0:1] + rows[4:5] + rows[8:9]


def second_kernel(low_ref, high_ref, low_weights_ref, high_weights_ref, low_got_ref, high_got_ref, loss_ref, out_ref):
    blocks = out_ref.shape[0]
    step = low_ref.shape[1]
    width = low_ref.shape[0] - EXTRA
    size = width // blocks
    total = loss_ref[0].astype(F32)
    for block in range(1, blocks):
        total = total + loss_ref[block].astype(F32)
    rows = loss_rows(jnp.broadcast_to(received_loss(total), total.shape), total.shape)
    for block in range(blocks):
        out_ref[block, out_ref.shape[1] - EXTRA :, :] = rows
    by_columns = (((1,), (1,)), ((), ()))
    for start, got_ref in ((0, low_got_ref), (step, high_got_ref)):
        half = slice(start, start + step)
        grad = lax.dot_general(low_ref[:width, :], low_weights_ref[half, :], by_columns, preferred_element_type=F32)
        grad += lax.dot_general(high_ref[:width, :], high_weights_ref[half, :], by_columns, preferred_element_type=F32)
        for part in range(step // LANES):
            at = slice(part * size, (part + 1) * size)
            columns = grad[:, part * LANES : (part + 1) * LANES].astype(BF16).reshape(blocks, size, LANES)
            added = columns.astype(F32) + got_ref[:, at, :].astype(F32)
            first = (start // LANES + part) * size
            out_ref[:, first : first + size, :] = added.astype(BF16)


def sum_kernel(clip_scale, action_scale, got_ref, keep_ref, give_ref):
    blocks = got_ref.shape[0]
    rows, count = keep_ref.shape
    half = rows // 2
    core = place(blocks)[0]

    def over(kind):
        chosen = [block for block in range(blocks) if block_of(block, blocks) == kind]
        total = got_ref[chosen[0]].astype(F32)
        for block in chosen[1:]:
            total = total + got_ref[block].astype(F32)
        return total

    lower = over(0)
    upper = over(1)
    both = lower + upper
    loss = received_loss(both[both.shape[0] - EXTRA :])
    give_ref[rows:, :] = jnp.concatenate([jnp.broadcast_to(loss, (8, LANES))] * (count // LANES), axis=1)
    for part in range(count // LANES):
        columns = slice(part * LANES, (part + 1) * LANES)
        at = slice(part * rows, (part + 1) * rows)

        @pl.when(core == 0)
        def _():
            keep_ref[:half, columns] = both[at][:half] * clip_scale
            give_ref[:half, columns] = both[at][half:] * clip_scale

        @pl.when(core != 0)
        def _():
            keep_ref[:, columns] = upper[at] * action_scale
            give_ref[:rows, columns] = lower[at] * action_scale


def last_kernel(n_clip, loss_scale, keep_ref, give_ref, taken_ref, clip_ref, action_ref, loss_ref, loss, sent):
    rows = keep_ref.shape[0]
    half = clip_ref.shape[0]
    core = place(n_clip)[0]
    loss[...] = (give_ref[rows : rows + 1, :1] + taken_ref[rows : rows + 1, :1]) * loss_scale

    def write(clip, action):
        pairs = [(clip, clip_ref), (action, action_ref), (loss, loss_ref)]
        copies = [pltpu.make_async_copy(source, target, sent.at[i]) for i, (source, target) in enumerate(pairs)]
        for copy in copies:
            copy.start()
        for copy in copies:
            copy.wait()

    @pl.when(core == 0)
    def _():
        write(keep_ref.at[:half, :], taken_ref.at[:rows, :])

    @pl.when(core != 0)
    def _():
        write(taken_ref.at[:half, :], keep_ref)


def call(kernel, out_shape, in_specs, out_specs=None, scratch=(), flops=0, moved=0):
    return pl.pallas_call(
        kernel,
        out_shape=out_shape,
        in_specs=in_specs,
        out_specs=jax.tree.map(lambda _: VMEM, out_shape) if out_specs is None else out_specs,
        scratch_shapes=scratch,
        compiler_params=pltpu.CompilerParams(vmem_limit_bytes=12 * 1024 * 1024),
        cost_estimate=pl.CostEstimate(flops=flops, bytes_accessed=moved, transcendentals=0),
    )


def shards(n_clip, n_act, clips, actions, positive_ids, robot_ids, robot_bias):
    both = ("clip", "act")
    pairs = n_act // 2
    near = n_clip // 2
    along_act = [[[k * n_act + 2 * m + c for m in range(pairs)] for k in range(n_clip)] for c in range(2)]
    along_clip = [[[k * n_act + 2 * m + c for k in range(n_clip)] for m in range(pairs)] for c in range(2)]
    clips_first = along_act[0] + along_clip[1]
    actions_first = along_clip[0] + along_act[1]
    swap = [(i, i ^ 1) for i in range(n_act)]
    gather_pass, scatter_pass = [], []
    for neighbour in (lambda k: (k + near) % n_clip, lambda k: k ^ 1):
        there = [(k * n_act + 2 * m, neighbour(k) * n_act + 2 * m + 1) for k in range(n_clip) for m in range(pairs)]
        here = [(k * n_act + 2 * m, k * n_act + 2 * m + 1) for k in range(n_clip) for m in range(pairs)]
        gather_pass.append(there + [(b, a) for a, b in here])
        scatter_pass.append(here + [(b, a) for a, b in there])
    exchange = functools.partial(lax.all_to_all, axis_name=both, split_axis=0, concat_axis=0)

    half, count = clips.shape
    rows = actions.shape[0]
    width = rows * n_clip
    parts = count // LANES
    act = lax.axis_index("act")
    shape = jax.ShapeDtypeStruct

    first_core = act % 2 == 0
    clip_twice = jnp.broadcast_to(clips[None], (2, half, count)).reshape(rows, count)
    send = jnp.where(first_core, actions, clip_twice).astype(BF16)
    mine = jnp.where(first_core, clip_twice, actions).astype(BF16)
    other = lax.ppermute(send, "act", swap)
    pair = jnp.concatenate([mine[:half], other[:half]], axis=0)
    takes_mine = block_of(jnp.arange(n_clip), n_clip)[:, None, None] == 1
    chunks = jnp.where(first_core, pair[None], jnp.where(takes_mine, mine[None], other[None]))
    positive_ids, robot_ids = positive_ids[None, :], robot_ids[None, :]
    own = exchange(chunks, axis_index_groups=clips_first).reshape(width, count)
    halves = shape((width + EXTRA, count // 2), BF16)
    low, high = call(split_kernel, (halves, halves), [VMEM] * 3)(own, positive_ids, robot_ids)
    low = lax.ppermute(low, both, gather_pass[0])
    high = lax.ppermute(high, both, gather_pass[1])
    own_t = call(transpose_kernel, shape((count, width), BF16), [VMEM])(own)

    flops = 2 * width * count * count
    half_blocks = shape((n_clip, parts * rows // 2, LANES), BF16)
    scale = 2.0 / math.sqrt(width)
    fixed = (robot_bias[None, :], positive_ids, robot_ids, own, own_t)
    def results(loss):
        return (shape((count, count // 2), BF16), half_blocks, loss)

    cost = {"flops": flops, "moved": 4 * width * count}
    specs = [VMEM] * 6
    low_weights, low_grad, loss = call(
        functools.partial(low_kernel, n_clip, scale), results(shape((8, LANES), F32)), specs, **cost
    )(*fixed, low)
    low_got = lax.ppermute(low_grad, both, scatter_pass[0])
    high_weights, high_grad, loss_sent = call(
        functools.partial(high_kernel, n_clip, scale), results(shape((n_clip, EXTRA, LANES), BF16)), specs + [VMEM], **cost
    )(*fixed, high, loss)
    high_got = lax.ppermute(high_grad, both, scatter_pass[1])
    loss_got = exchange(loss_sent, axis_index_groups=actions_first)
    operands = (low, high, low_weights, high_weights)
    low_got, loss_got = lax.optimization_barrier((low_got, loss_got))
    ready = call(second_kernel, shape((n_clip, parts * rows + EXTRA, LANES), BF16), [VMEM] * 7, **cost)(
        *operands, low_got, high_got, loss_got
    )
    scattered = exchange(ready, axis_index_groups=clips_first)

    total_clips = count * n_clip
    total_actions = count * n_act
    keep, give = call(
        functools.partial(sum_kernel, 1.0 / math.sqrt(total_actions), 1.0 / math.sqrt(total_clips)),
        (shape((rows, count), F32), shape((rows + 8, count), F32)),
        [VMEM],
    )(scattered)
    taken = lax.ppermute(give, "act", swap)
    clip_grad, action_grad, loss = call(
        functools.partial(last_kernel, n_clip, 1.0 / (total_clips * total_actions)),
        (shape((half, count), F32), shape((rows, count), F32), shape((1, 1), F32)),
        [VMEM] * 3,
        (ANY, ANY, ANY),
        [pltpu.VMEM((1, 1), F32), pltpu.SemaphoreType.DMA((3,))],
    )(keep, give, taken)
    return clip_grad, action_grad, loss.reshape(())


def solution(mesh):
    return jax.shard_map(
        functools.partial(shards, mesh.shape["clip"], mesh.shape["act"]),
        mesh=mesh,
        in_specs=(P("act", "clip"), P("clip", "act"), P("clip"), P("act"), P()),
        out_specs=(P("act", "clip"), P("clip", "act"), P()),
        check_vma=False,
    )
```

```python
import functools
import math

import jax
import jax.numpy as jnp
from jax import lax
from jax.experimental import pallas as pl
from jax.experimental.pallas import tpu as pltpu
from jax.sharding import PartitionSpec as P

BF16 = jnp.bfloat16
F32 = jnp.float32
LANES = 128
EXTRA = 16
VMEM = pl.BlockSpec(memory_space=pltpu.VMEM)
ANY = pl.BlockSpec(memory_space=pl.ANY)


def loss_rows(value, shape):
    high = value.astype(BF16).astype(F32)
    middle = (value - high).astype(BF16).astype(F32)
    low = (value - high - middle).astype(BF16).astype(F32)
    row = lax.broadcasted_iota(jnp.int32, shape, len(shape) - 2)
    rows = jnp.where(row < 4, high, jnp.where(row < 8, middle, jnp.where(row < 12, low, 0.0)))
    return rows.astype(BF16)


def store_blocks(out_ref, values, first_column):
    blocks = out_ref.shape[0]
    rows = values.shape[0] // blocks
    for part in range(values.shape[1] // LANES):
        at = (first_column // LANES + part) * rows
        columns = values[:, part * LANES : (part + 1) * LANES]
        out_ref[:, at : at + rows, :] = columns.reshape(blocks, rows, LANES).astype(BF16)


def block_of(index, blocks):
    return (index // (blocks // 2) + index) % 2


def member(position):
    return position ^ 12


def place(n_clip):
    act = lax.axis_index("act")
    core = lax.rem(act, 2)
    clip = lax.axis_index("clip")
    kind = lax.rem(lax.div(clip, n_clip // 2) + clip, 2)
    return core, kind, act - core + kind


def split_kernel(own_ref, positive_ref, robot_ref, low_ref, high_ref):
    width = own_ref.shape[0]
    half = low_ref.shape[1]
    positive = positive_ref[...]
    robots = [robot_ref[:, :half], robot_ref[:, half:]]
    padding = [jnp.zeros_like(robots[0])] * (EXTRA - 4)
    for out_ref, start in ((low_ref, 0), (high_ref, half)):
        part = positive[:, start : start + half]
        rows = jnp.concatenate([part // LANES, part % LANES] + robots + padding, axis=0)
        out_ref[:width, :] = own_ref[:, start : start + half]
        out_ref[width:, :] = rows.astype(F32).astype(BF16)


def transpose_kernel(own_ref, own_t_ref):
    own_t_ref[...] = own_ref[...].T


def sides(n_clip, start, bias_ref, positive_ref, robot_ref, got_rows):
    count = robot_ref.shape[1]
    step = got_rows.shape[1]
    part = slice(start, start + step)
    core, kind, index = place(n_clip)
    first = core == 0
    arrived = jnp.concatenate([got_rows[2:3, :], got_rows[3:4, :]], axis=1)
    robot = jnp.where(core == kind, robot_ref[...].astype(F32), arrived)
    bias = jnp.zeros((1, count), F32)
    for each in range(bias_ref.shape[1]):
        bias = jnp.where(robot == each, bias_ref[:, each : each + 1], bias)
    zero = jnp.zeros((1, count), F32)
    action = (lax.broadcasted_iota(jnp.int32, (1, count), 1) + index * count).astype(F32)
    rows = [jnp.where(first, zero, bias), jnp.where(first, positive_ref[...].astype(F32), action)]
    rows = jnp.concatenate(rows + [zero] * 6, axis=0).T
    column_bias = jnp.where(first, bias, zero)[:, part]
    column_key = jnp.where(first, action[:, part], got_rows[0:1, :] * LANES + got_rows[1:2, :])
    return rows[:, 0:1], rows[:, 1:2], column_bias, column_key


def logits_kernel(n_clip, scale, start, bias_ref, positive_ref, robot_ref, own_ref, own_t_ref, got_ref, before_ref,
                  weights_ref, grad_ref, loss_ref):
    width = own_ref.shape[0]
    got_rows = got_ref[width:, :].astype(F32)
    row_bias, row_key, column_bias, column_key = sides(n_clip, start, bias_ref, positive_ref, robot_ref, got_rows)
    got = got_ref[:width, :]
    total = jnp.zeros((1, got.shape[1]), F32)
    for row in range(0, own_t_ref.shape[0], LANES):
        part = slice(row, row + LANES)
        logits = jnp.dot(own_t_ref[part, :], got, preferred_element_type=F32) * scale
        logits = logits + (row_bias[part] + column_bias)
        positive = row_key[part] == column_key
        margin = jnp.where(positive, -logits, logits)
        small = jnp.exp(-jnp.abs(margin))
        above = 1.0 + small
        inverse = 1.0 / above
        log = jnp.log(above) + (small - (above - 1.0)) * inverse
        sigmoid = jnp.where(margin >= 0.0, inverse, small * inverse)
        weights_ref[part, :] = jnp.where(positive, -sigmoid, sigmoid).astype(BF16)
        total = total + jnp.sum(jnp.maximum(margin, 0.0) + log, axis=0, keepdims=True)
    store_blocks(grad_ref, jnp.dot(own_ref[...], weights_ref[...], preferred_element_type=F32), 0)
    total = jnp.sum(total, keepdims=True)
    if before_ref is None:
        loss_ref[...] = jnp.broadcast_to(total, loss_ref.shape)
    else:
        total = jnp.broadcast_to((total + before_ref[0:1, 0:1])[None], loss_ref.shape)
        loss_ref[...] = loss_rows(total, loss_ref.shape)


def low_kernel(n_clip, scale, *refs):
    logits_kernel(n_clip, scale, 0, *refs[:6], None, *refs[6:])


def high_kernel(n_clip, scale, *refs):
    logits_kernel(n_clip, scale, refs[5].shape[1], *refs)


def received_loss(rows):
    return rows[0:1] + rows[4:5] + rows[8:9]


def second_kernel(low_ref, high_ref, low_weights_ref, high_weights_ref, low_got_ref, high_got_ref, loss_ref, out_ref):
    blocks = out_ref.shape[0]
    step = low_ref.shape[1]
    width = low_ref.shape[0] - EXTRA
    size = width // blocks
    total = loss_ref[0].astype(F32)
    for block in range(1, blocks):
        total = total + loss_ref[block].astype(F32)
    rows = loss_rows(jnp.broadcast_to(received_loss(total), total.shape), total.shape)
    for block in range(blocks):
        out_ref[block, out_ref.shape[1] - EXTRA :, :] = rows
    by_columns = (((1,), (1,)), ((), ()))
    for start, got_ref in ((0, low_got_ref), (step, high_got_ref)):
        half = slice(start, start + step)
        grad = lax.dot_general(low_ref[:width, :], low_weights_ref[half, :], by_columns, preferred_element_type=F32)
        grad += lax.dot_general(high_ref[:width, :], high_weights_ref[half, :], by_columns, preferred_element_type=F32)
        for part in range(step // LANES):
            at = slice(part * size, (part + 1) * size)
            columns = grad[:, part * LANES : (part + 1) * LANES].astype(BF16).reshape(blocks, size, LANES)
            added = columns.astype(F32) + got_ref[:, at, :].astype(F32)
            first = (start // LANES + part) * size
            out_ref[:, first : first + size, :] = added.astype(BF16)


def sum_kernel(clip_scale, action_scale, got_ref, keep_ref, give_ref):
    blocks = got_ref.shape[0]
    rows, count = keep_ref.shape
    half = rows // 2
    core = place(blocks)[0]

    def over(kind):
        chosen = [block for block in range(blocks) if block_of(member(block), blocks) == kind]
        total = got_ref[chosen[0]].astype(F32)
        for block in chosen[1:]:
            total = total + got_ref[block].astype(F32)
        return total

    lower = over(0)
    upper = over(1)
    both = lower + upper
    loss = received_loss(both[both.shape[0] - EXTRA :])
    give_ref[rows:, :] = jnp.concatenate([jnp.broadcast_to(loss, (8, LANES))] * (count // LANES), axis=1)
    for part in range(count // LANES):
        columns = slice(part * LANES, (part + 1) * LANES)
        at = slice(part * rows, (part + 1) * rows)

        @pl.when(core == 0)
        def _():
            keep_ref[:half, columns] = both[at][:half] * clip_scale
            give_ref[:half, columns] = both[at][half:] * clip_scale

        @pl.when(core != 0)
        def _():
            keep_ref[:, columns] = upper[at] * action_scale
            give_ref[:rows, columns] = lower[at] * action_scale


def last_kernel(n_clip, loss_scale, keep_ref, give_ref, taken_ref, clip_ref, action_ref, loss_ref, loss, sent):
    rows = keep_ref.shape[0]
    half = clip_ref.shape[0]
    core = place(n_clip)[0]
    loss[...] = (give_ref[rows : rows + 1, :1] + taken_ref[rows : rows + 1, :1]) * loss_scale

    def write(clip, action):
        pairs = [(clip, clip_ref), (action, action_ref), (loss, loss_ref)]
        copies = [pltpu.make_async_copy(source, target, sent.at[i]) for i, (source, target) in enumerate(pairs)]
        for copy in copies:
            copy.start()
        for copy in copies:
            copy.wait()

    @pl.when(core == 0)
    def _():
        write(keep_ref.at[:half, :], taken_ref.at[:rows, :])

    @pl.when(core != 0)
    def _():
        write(taken_ref.at[:half, :], keep_ref)


def call(kernel, out_shape, in_specs, out_specs=None, scratch=(), flops=0, moved=0):
    return pl.pallas_call(
        kernel,
        out_shape=out_shape,
        in_specs=in_specs,
        out_specs=jax.tree.map(lambda _: VMEM, out_shape) if out_specs is None else out_specs,
        scratch_shapes=scratch,
        compiler_params=pltpu.CompilerParams(vmem_limit_bytes=12 * 1024 * 1024),
        cost_estimate=pl.CostEstimate(flops=flops, bytes_accessed=moved, transcendentals=0),
    )


def shards(n_clip, n_act, clips, actions, positive_ids, robot_ids, robot_bias):
    both = ("clip", "act")
    pairs = n_act // 2
    near = n_clip // 2
    order = [member(i) for i in range(n_clip)]
    along_act = [[[k * n_act + 2 * m + c for m in order] for k in range(n_clip)] for c in range(2)]
    along_clip = [[[k * n_act + 2 * m + c for k in order] for m in range(pairs)] for c in range(2)]
    clips_first = along_act[0] + along_clip[1]
    actions_first = along_clip[0] + along_act[1]
    swap = [(i, i ^ 1) for i in range(n_act)]
    gather_pass, scatter_pass = [], []
    for neighbour in (lambda k: (k + near) % n_clip, lambda k: k ^ 1):
        there = [(k * n_act + 2 * m, neighbour(k) * n_act + 2 * m + 1) for k in range(n_clip) for m in range(pairs)]
        here = [(k * n_act + 2 * m, k * n_act + 2 * m + 1) for k in range(n_clip) for m in range(pairs)]
        gather_pass.append(there + [(b, a) for a, b in here])
        scatter_pass.append(here + [(b, a) for a, b in there])
    exchange = functools.partial(lax.all_to_all, axis_name=both, split_axis=0, concat_axis=0)

    half, count = clips.shape
    rows = actions.shape[0]
    width = rows * n_clip
    parts = count // LANES
    act = lax.axis_index("act")
    shape = jax.ShapeDtypeStruct

    first_core = act % 2 == 0
    clip_twice = jnp.broadcast_to(clips[None], (2, half, count)).reshape(rows, count)
    send = jnp.where(first_core, actions, clip_twice).astype(BF16)
    mine = jnp.where(first_core, clip_twice, actions).astype(BF16)
    other = lax.ppermute(send, "act", swap)
    pair = jnp.concatenate([mine[:half], other[:half]], axis=0)
    takes_mine = block_of(member(jnp.arange(n_clip)), n_clip)[:, None, None] == 1
    chunks = jnp.where(first_core, pair[None], jnp.where(takes_mine, mine[None], other[None]))
    positive_ids, robot_ids = positive_ids[None, :], robot_ids[None, :]
    own = exchange(chunks, axis_index_groups=clips_first).reshape(width, count)
    halves = shape((width + EXTRA, count // 2), BF16)
    low, high = call(split_kernel, (halves, halves), [VMEM] * 3)(own, positive_ids, robot_ids)
    low = lax.ppermute(low, both, gather_pass[0])
    high = lax.ppermute(high, both, gather_pass[1])
    own_t = call(transpose_kernel, shape((count, width), BF16), [VMEM])(own)

    flops = 2 * width * count * count
    half_blocks = shape((n_clip, parts * rows // 2, LANES), BF16)
    scale = 2.0 / math.sqrt(width)
    fixed = (robot_bias[None, :], positive_ids, robot_ids, own, own_t)
    def results(loss):
        return (shape((count, count // 2), BF16), half_blocks, loss)

    cost = {"flops": flops, "moved": 4 * width * count}
    specs = [VMEM] * 6
    low_weights, low_grad, loss = call(
        functools.partial(low_kernel, n_clip, scale), results(shape((8, LANES), F32)), specs, **cost
    )(*fixed, low)
    low_got = lax.ppermute(low_grad, both, scatter_pass[0])
    high_weights, high_grad, loss_sent = call(
        functools.partial(high_kernel, n_clip, scale), results(shape((n_clip, EXTRA, LANES), BF16)), specs + [VMEM], **cost
    )(*fixed, high, loss)
    high_got = lax.ppermute(high_grad, both, scatter_pass[1])
    loss_got = exchange(loss_sent, axis_index_groups=actions_first)
    operands = (low, high, low_weights, high_weights)
    low_got, loss_got = lax.optimization_barrier((low_got, loss_got))
    ready = call(second_kernel, shape((n_clip, parts * rows + EXTRA, LANES), BF16), [VMEM] * 7, **cost)(
        *operands, low_got, high_got, loss_got
    )
    scattered = exchange(ready, axis_index_groups=clips_first)

    total_clips = count * n_clip
    total_actions = count * n_act
    keep, give = call(
        functools.partial(sum_kernel, 1.0 / math.sqrt(total_actions), 1.0 / math.sqrt(total_clips)),
        (shape((rows, count), F32), shape((rows + 8, count), F32)),
        [VMEM],
    )(scattered)
    taken = lax.ppermute(give, "act", swap)
    clip_grad, action_grad, loss = call(
        functools.partial(last_kernel, n_clip, 1.0 / (total_clips * total_actions)),
        (shape((half, count), F32), shape((rows, count), F32), shape((1, 1), F32)),
        [VMEM] * 3,
        (ANY, ANY, ANY),
        [pltpu.VMEM((1, 1), F32), pltpu.SemaphoreType.DMA((3,))],
    )(keep, give, taken)
    return clip_grad, action_grad, loss.reshape(())


def solution(mesh):
    return jax.shard_map(
        functools.partial(shards, mesh.shape["clip"], mesh.shape["act"]),
        mesh=mesh,
        in_specs=(P("act", "clip"), P("clip", "act"), P("clip"), P("act"), P()),
        out_specs=(P("act", "clip"), P("clip", "act"), P()),
        check_vma=False,
    )
```

```python
import functools
import math

import jax
import jax.numpy as jnp
from jax import lax
from jax.experimental import pallas as pl
from jax.experimental.pallas import tpu as pltpu
from jax.sharding import PartitionSpec as P

BF16 = jnp.bfloat16
F32 = jnp.float32
LANES = 128
ORDER = (13, 12, 14, 15, 11, 10, 9, 6, 8, 7, 4, 5, 3, 2, 1, 0)
EXTRA = 16
VMEM = pl.BlockSpec(memory_space=pltpu.VMEM)
ANY = pl.BlockSpec(memory_space=pl.ANY)


def loss_rows(value, shape):
    high = value.astype(BF16).astype(F32)
    middle = (value - high).astype(BF16).astype(F32)
    low = (value - high - middle).astype(BF16).astype(F32)
    row = lax.broadcasted_iota(jnp.int32, shape, len(shape) - 2)
    rows = jnp.where(row < 4, high, jnp.where(row < 8, middle, jnp.where(row < 12, low, 0.0)))
    return rows.astype(BF16)


def store_blocks(out_ref, values, first_column):
    blocks = out_ref.shape[0]
    rows = values.shape[0] // blocks
    for part in range(values.shape[1] // LANES):
        at = (first_column // LANES + part) * rows
        columns = values[:, part * LANES : (part + 1) * LANES]
        out_ref[:, at : at + rows, :] = columns.reshape(blocks, rows, LANES).astype(BF16)


def block_of(index, blocks):
    return (index // (blocks // 2) + index) % 2


def member(position):
    return ORDER[position]


def place(n_clip):
    act = lax.axis_index("act")
    core = lax.rem(act, 2)
    clip = lax.axis_index("clip")
    kind = lax.rem(lax.div(clip, n_clip // 2) + clip, 2)
    return core, kind, act - core + kind


def split_kernel(own_ref, positive_ref, robot_ref, low_ref, high_ref):
    width = own_ref.shape[0]
    half = low_ref.shape[1]
    positive = positive_ref[...]
    robots = [robot_ref[:, :half], robot_ref[:, half:]]
    padding = [jnp.zeros_like(robots[0])] * (EXTRA - 4)
    for out_ref, start in ((low_ref, 0), (high_ref, half)):
        part = positive[:, start : start + half]
        rows = jnp.concatenate([part // LANES, part % LANES] + robots + padding, axis=0)
        out_ref[:width, :] = own_ref[:, start : start + half]
        out_ref[width:, :] = rows.astype(F32).astype(BF16)


def transpose_kernel(own_ref, own_t_ref):
    own_t_ref[...] = own_ref[...].T


def sides(n_clip, start, bias_ref, positive_ref, robot_ref, got_rows):
    count = robot_ref.shape[1]
    step = got_rows.shape[1]
    part = slice(start, start + step)
    core, kind, index = place(n_clip)
    first = core == 0
    arrived = jnp.concatenate([got_rows[2:3, :], got_rows[3:4, :]], axis=1)
    robot = jnp.where(core == kind, robot_ref[...].astype(F32), arrived)
    bias = jnp.zeros((1, count), F32)
    for each in range(bias_ref.shape[1]):
        bias = jnp.where(robot == each, bias_ref[:, each : each + 1], bias)
    zero = jnp.zeros((1, count), F32)
    action = (lax.broadcasted_iota(jnp.int32, (1, count), 1) + index * count).astype(F32)
    rows = [jnp.where(first, zero, bias), jnp.where(first, positive_ref[...].astype(F32), action)]
    rows = jnp.concatenate(rows + [zero] * 6, axis=0).T
    column_bias = jnp.where(first, bias, zero)[:, part]
    column_key = jnp.where(first, action[:, part], got_rows[0:1, :] * LANES + got_rows[1:2, :])
    return rows[:, 0:1], rows[:, 1:2], column_bias, column_key


def logits_kernel(n_clip, scale, start, bias_ref, positive_ref, robot_ref, own_ref, own_t_ref, got_ref, before_ref,
                  weights_ref, grad_ref, loss_ref):
    width = own_ref.shape[0]
    got_rows = got_ref[width:, :].astype(F32)
    row_bias, row_key, column_bias, column_key = sides(n_clip, start, bias_ref, positive_ref, robot_ref, got_rows)
    got = got_ref[:width, :]
    total = jnp.zeros((1, got.shape[1]), F32)
    for row in range(0, own_t_ref.shape[0], LANES):
        part = slice(row, row + LANES)
        logits = jnp.dot(own_t_ref[part, :], got, preferred_element_type=F32) * scale
        logits = logits + (row_bias[part] + column_bias)
        positive = row_key[part] == column_key
        margin = jnp.where(positive, -logits, logits)
        small = jnp.exp(-jnp.abs(margin))
        above = 1.0 + small
        inverse = 1.0 / above
        log = jnp.log(above) + (small - (above - 1.0)) * inverse
        sigmoid = jnp.where(margin >= 0.0, inverse, small * inverse)
        weights_ref[part, :] = jnp.where(positive, -sigmoid, sigmoid).astype(BF16)
        total = total + jnp.sum(jnp.maximum(margin, 0.0) + log, axis=0, keepdims=True)
    store_blocks(grad_ref, jnp.dot(own_ref[...], weights_ref[...], preferred_element_type=F32), 0)
    total = jnp.sum(total, keepdims=True)
    if before_ref is None:
        loss_ref[...] = jnp.broadcast_to(total, loss_ref.shape)
    else:
        total = jnp.broadcast_to((total + before_ref[0:1, 0:1])[None], loss_ref.shape)
        loss_ref[...] = loss_rows(total, loss_ref.shape)


def low_kernel(n_clip, scale, *refs):
    logits_kernel(n_clip, scale, 0, *refs[:6], None, *refs[6:])


def high_kernel(n_clip, scale, *refs):
    logits_kernel(n_clip, scale, refs[5].shape[1], *refs)


def received_loss(rows):
    return rows[0:1] + rows[4:5] + rows[8:9]


def second_kernel(low_ref, high_ref, low_weights_ref, high_weights_ref, low_got_ref, high_got_ref, loss_ref, out_ref):
    blocks = out_ref.shape[0]
    step = low_ref.shape[1]
    width = low_ref.shape[0] - EXTRA
    size = width // blocks
    total = loss_ref[0].astype(F32)
    for block in range(1, blocks):
        total = total + loss_ref[block].astype(F32)
    rows = loss_rows(jnp.broadcast_to(received_loss(total), total.shape), total.shape)
    for block in range(blocks):
        out_ref[block, out_ref.shape[1] - EXTRA :, :] = rows
    by_columns = (((1,), (1,)), ((), ()))
    for start, got_ref in ((0, low_got_ref), (step, high_got_ref)):
        half = slice(start, start + step)
        grad = lax.dot_general(low_ref[:width, :], low_weights_ref[half, :], by_columns, preferred_element_type=F32)
        grad += lax.dot_general(high_ref[:width, :], high_weights_ref[half, :], by_columns, preferred_element_type=F32)
        for part in range(step // LANES):
            at = slice(part * size, (part + 1) * size)
            columns = grad[:, part * LANES : (part + 1) * LANES].astype(BF16).reshape(blocks, size, LANES)
            added = columns.astype(F32) + got_ref[:, at, :].astype(F32)
            first = (start // LANES + part) * size
            out_ref[:, first : first + size, :] = added.astype(BF16)


def sum_kernel(clip_scale, action_scale, got_ref, keep_ref, give_ref):
    blocks = got_ref.shape[0]
    rows, count = keep_ref.shape
    half = rows // 2
    core = place(blocks)[0]

    def over(kind):
        chosen = [block for block in range(blocks) if block_of(member(block), blocks) == kind]
        total = got_ref[chosen[0]].astype(F32)
        for block in chosen[1:]:
            total = total + got_ref[block].astype(F32)
        return total

    lower = over(0)
    upper = over(1)
    both = lower + upper
    loss = received_loss(both[both.shape[0] - EXTRA :])
    give_ref[rows:, :] = jnp.concatenate([jnp.broadcast_to(loss, (8, LANES))] * (count // LANES), axis=1)
    for part in range(count // LANES):
        columns = slice(part * LANES, (part + 1) * LANES)
        at = slice(part * rows, (part + 1) * rows)

        @pl.when(core == 0)
        def _():
            keep_ref[:half, columns] = both[at][:half] * clip_scale
            give_ref[:half, columns] = both[at][half:] * clip_scale

        @pl.when(core != 0)
        def _():
            keep_ref[:, columns] = upper[at] * action_scale
            give_ref[:rows, columns] = lower[at] * action_scale


def last_kernel(n_clip, loss_scale, keep_ref, give_ref, taken_ref, clip_ref, action_ref, loss_ref, loss, sent):
    rows = keep_ref.shape[0]
    half = clip_ref.shape[0]
    core = place(n_clip)[0]
    loss[...] = (give_ref[rows : rows + 1, :1] + taken_ref[rows : rows + 1, :1]) * loss_scale

    def write(clip, action):
        pairs = [(clip, clip_ref), (action, action_ref), (loss, loss_ref)]
        copies = [pltpu.make_async_copy(source, target, sent.at[i]) for i, (source, target) in enumerate(pairs)]
        for copy in copies:
            copy.start()
        for copy in copies:
            copy.wait()

    @pl.when(core == 0)
    def _():
        write(keep_ref.at[:half, :], taken_ref.at[:rows, :])

    @pl.when(core != 0)
    def _():
        write(taken_ref.at[:half, :], keep_ref)


def call(kernel, out_shape, in_specs, out_specs=None, scratch=(), flops=0, moved=0):
    return pl.pallas_call(
        kernel,
        out_shape=out_shape,
        in_specs=in_specs,
        out_specs=jax.tree.map(lambda _: VMEM, out_shape) if out_specs is None else out_specs,
        scratch_shapes=scratch,
        compiler_params=pltpu.CompilerParams(vmem_limit_bytes=12 * 1024 * 1024),
        cost_estimate=pl.CostEstimate(flops=flops, bytes_accessed=moved, transcendentals=0),
    )


def shards(n_clip, n_act, clips, actions, positive_ids, robot_ids, robot_bias):
    both = ("clip", "act")
    pairs = n_act // 2
    near = n_clip // 2
    order = [member(i) for i in range(n_clip)]
    along_act = [[[k * n_act + 2 * m + c for m in order] for k in range(n_clip)] for c in range(2)]
    along_clip = [[[k * n_act + 2 * m + c for k in order] for m in range(pairs)] for c in range(2)]
    clips_first = along_act[0] + along_clip[1]
    actions_first = along_clip[0] + along_act[1]
    swap = [(i, i ^ 1) for i in range(n_act)]
    gather_pass, scatter_pass = [], []
    for neighbour in (lambda k: (k + near) % n_clip, lambda k: k ^ 1):
        there = [(k * n_act + 2 * m, neighbour(k) * n_act + 2 * m + 1) for k in range(n_clip) for m in range(pairs)]
        here = [(k * n_act + 2 * m, k * n_act + 2 * m + 1) for k in range(n_clip) for m in range(pairs)]
        gather_pass.append(there + [(b, a) for a, b in here])
        scatter_pass.append(here + [(b, a) for a, b in there])
    exchange = functools.partial(lax.all_to_all, axis_name=both, split_axis=0, concat_axis=0)

    half, count = clips.shape
    rows = actions.shape[0]
    width = rows * n_clip
    parts = count // LANES
    act = lax.axis_index("act")
    shape = jax.ShapeDtypeStruct

    first_core = act % 2 == 0
    clip_twice = jnp.broadcast_to(clips[None], (2, half, count)).reshape(rows, count)
    send = jnp.where(first_core, actions, clip_twice).astype(BF16)
    mine = jnp.where(first_core, clip_twice, actions).astype(BF16)
    other = lax.ppermute(send, "act", swap)
    pair = jnp.concatenate([mine[:half], other[:half]], axis=0)
    takes_mine = jnp.array([block_of(k, n_clip) == 1 for k in order])[:, None, None]
    chunks = jnp.where(first_core, pair[None], jnp.where(takes_mine, mine[None], other[None]))
    positive_ids, robot_ids = positive_ids[None, :], robot_ids[None, :]
    own = exchange(chunks, axis_index_groups=clips_first).reshape(width, count)
    halves = shape((width + EXTRA, count // 2), BF16)
    low, high = call(split_kernel, (halves, halves), [VMEM] * 3)(own, positive_ids, robot_ids)
    low = lax.ppermute(low, both, gather_pass[0])
    high = lax.ppermute(high, both, gather_pass[1])
    own_t = call(transpose_kernel, shape((count, width), BF16), [VMEM])(own)

    flops = 2 * width * count * count
    half_blocks = shape((n_clip, parts * rows // 2, LANES), BF16)
    scale = 2.0 / math.sqrt(width)
    fixed = (robot_bias[None, :], positive_ids, robot_ids, own, own_t)
    def results(loss):
        return (shape((count, count // 2), BF16), half_blocks, loss)

    cost = {"flops": flops, "moved": 4 * width * count}
    specs = [VMEM] * 6
    low_weights, low_grad, loss = call(
        functools.partial(low_kernel, n_clip, scale), results(shape((8, LANES), F32)), specs, **cost
    )(*fixed, low)
    low_got = lax.ppermute(low_grad, both, scatter_pass[0])
    high_weights, high_grad, loss_sent = call(
        functools.partial(high_kernel, n_clip, scale), results(shape((n_clip, EXTRA, LANES), BF16)), specs + [VMEM], **cost
    )(*fixed, high, loss)
    high_got = lax.ppermute(high_grad, both, scatter_pass[1])
    loss_got = exchange(loss_sent, axis_index_groups=actions_first)
    operands = (low, high, low_weights, high_weights)
    low_got, loss_got = lax.optimization_barrier((low_got, loss_got))
    ready = call(second_kernel, shape((n_clip, parts * rows + EXTRA, LANES), BF16), [VMEM] * 7, **cost)(
        *operands, low_got, high_got, loss_got
    )
    scattered = exchange(ready, axis_index_groups=clips_first)

    total_clips = count * n_clip
    total_actions = count * n_act
    keep, give = call(
        functools.partial(sum_kernel, 1.0 / math.sqrt(total_actions), 1.0 / math.sqrt(total_clips)),
        (shape((rows, count), F32), shape((rows + 8, count), F32)),
        [VMEM],
    )(scattered)
    taken = lax.ppermute(give, "act", swap)
    clip_grad, action_grad, loss = call(
        functools.partial(last_kernel, n_clip, 1.0 / (total_clips * total_actions)),
        (shape((half, count), F32), shape((rows, count), F32), shape((1, 1), F32)),
        [VMEM] * 3,
        (ANY, ANY, ANY),
        [pltpu.VMEM((1, 1), F32), pltpu.SemaphoreType.DMA((3,))],
    )(keep, give, taken)
    return clip_grad, action_grad, loss.reshape(())


def solution(mesh):
    return jax.shard_map(
        functools.partial(shards, mesh.shape["clip"], mesh.shape["act"]),
        mesh=mesh,
        in_specs=(P("act", "clip"), P("clip", "act"), P("clip"), P("act"), P()),
        out_specs=(P("act", "clip"), P("clip", "act"), P()),
        check_vma=False,
    )
```

```python
import functools
import math

import jax
import jax.numpy as jnp
from jax import lax
from jax.experimental import pallas as pl
from jax.experimental.pallas import tpu as pltpu
from jax.sharding import PartitionSpec as P

BF16 = jnp.bfloat16
F32 = jnp.float32
LANES = 128
ORDER = (13, 12, 14, 15, 11, 10, 9, 6, 8, 7, 4, 5, 3, 2, 1, 0)
EXTRA = 16
VMEM = pl.BlockSpec(memory_space=pltpu.VMEM)
ANY = pl.BlockSpec(memory_space=pl.ANY)


def loss_rows(value, shape):
    high = value.astype(BF16).astype(F32)
    middle = (value - high).astype(BF16).astype(F32)
    low = (value - high - middle).astype(BF16).astype(F32)
    row = lax.broadcasted_iota(jnp.int32, shape, len(shape) - 2)
    rows = jnp.where(row < 4, high, jnp.where(row < 8, middle, jnp.where(row < 12, low, 0.0)))
    return rows.astype(BF16)


def store_blocks(out_ref, values, first_column):
    blocks = out_ref.shape[0]
    rows = values.shape[0] // blocks
    for part in range(values.shape[1] // LANES):
        at = (first_column // LANES + part) * rows
        columns = values[:, part * LANES : (part + 1) * LANES]
        out_ref[:, at : at + rows, :] = columns.reshape(blocks, rows, LANES).astype(BF16)


def block_of(index, blocks):
    return (index // (blocks // 2) + index) % 2


def member(position):
    return ORDER[position]


def place(n_clip):
    act = lax.axis_index("act")
    core = lax.rem(act, 2)
    clip = lax.axis_index("clip")
    kind = lax.rem(lax.div(clip, n_clip // 2) + clip, 2)
    return core, kind, act - core + kind


def split_kernel(own_ref, positive_ref, robot_ref, low_ref, high_ref):
    width = own_ref.shape[0]
    half = low_ref.shape[1]
    positive = positive_ref[...]
    robots = [robot_ref[:, :half], robot_ref[:, half:]]
    padding = [jnp.zeros_like(robots[0])] * (EXTRA - 4)
    for out_ref, start in ((low_ref, 0), (high_ref, half)):
        part = positive[:, start : start + half]
        rows = jnp.concatenate([part // LANES, part % LANES] + robots + padding, axis=0)
        out_ref[:width, :] = own_ref[:, start : start + half]
        out_ref[width:, :] = rows.astype(F32).astype(BF16)


def transpose_kernel(own_ref, own_t_ref):
    own_t_ref[...] = own_ref[...].T


def sides(n_clip, start, bias_ref, positive_ref, robot_ref, got_rows):
    count = robot_ref.shape[1]
    step = got_rows.shape[1]
    part = slice(start, start + step)
    core, kind, index = place(n_clip)
    first = core == 0
    arrived = jnp.concatenate([got_rows[2:3, :], got_rows[3:4, :]], axis=1)
    robot = jnp.where(core == kind, robot_ref[...].astype(F32), arrived)
    bias = jnp.zeros((1, count), F32)
    for each in range(bias_ref.shape[1]):
        bias = jnp.where(robot == each, bias_ref[:, each : each + 1], bias)
    zero = jnp.zeros((1, count), F32)
    action = (lax.broadcasted_iota(jnp.int32, (1, count), 1) + index * count).astype(F32)
    rows = [jnp.where(first, zero, bias), jnp.where(first, positive_ref[...].astype(F32), action)]
    rows = jnp.concatenate(rows + [zero] * 6, axis=0).T
    column_bias = jnp.where(first, bias, zero)[:, part]
    column_key = jnp.where(first, action[:, part], got_rows[0:1, :] * LANES + got_rows[1:2, :])
    return rows[:, 0:1], rows[:, 1:2], column_bias, column_key


def logits_kernel(n_clip, scale, start, bias_ref, positive_ref, robot_ref, own_ref, own_t_ref, got_ref, before_ref,
                  weights_ref, grad_ref, loss_ref):
    width = own_ref.shape[0]
    got_rows = got_ref[width:, :].astype(F32)
    row_bias, row_key, column_bias, column_key = sides(n_clip, start, bias_ref, positive_ref, robot_ref, got_rows)
    got = got_ref[:width, :]
    total = jnp.zeros((1, got.shape[1]), F32)
    for row in range(0, own_t_ref.shape[0], LANES):
        part = slice(row, row + LANES)
        logits = jnp.dot(own_t_ref[part, :], got, preferred_element_type=F32) * scale
        logits = logits + (row_bias[part] + column_bias)
        positive = row_key[part] == column_key
        margin = jnp.where(positive, -logits, logits)
        small = jnp.exp(-jnp.abs(margin))
        above = 1.0 + small
        inverse = 1.0 / above
        log = jnp.log(above) + (small - (above - 1.0)) * inverse
        sigmoid = jnp.where(margin >= 0.0, inverse, small * inverse)
        weights_ref[part, :] = jnp.where(positive, -sigmoid, sigmoid).astype(BF16)
        total = total + jnp.sum(jnp.maximum(margin, 0.0) + log, axis=0, keepdims=True)
    store_blocks(grad_ref, jnp.dot(own_ref[...], weights_ref[...], preferred_element_type=F32), 0)
    total = jnp.sum(total, keepdims=True)
    if before_ref is None:
        loss_ref[...] = jnp.broadcast_to(total, loss_ref.shape)
    else:
        total = jnp.broadcast_to((total + before_ref[0:1, 0:1])[None], loss_ref.shape)
        loss_ref[...] = loss_rows(total, loss_ref.shape)


def low_kernel(n_clip, scale, *refs):
    logits_kernel(n_clip, scale, 0, *refs[:6], None, *refs[6:])


def high_kernel(n_clip, scale, *refs):
    logits_kernel(n_clip, scale, refs[5].shape[1], *refs)


def received_loss(rows):
    return rows[0:1] + rows[4:5] + rows[8:9]


def second_kernel(low_ref, high_ref, low_weights_ref, high_weights_ref, low_got_ref, high_got_ref, loss_ref, out_ref):
    blocks = out_ref.shape[0]
    step = low_ref.shape[1]
    width = low_ref.shape[0] - EXTRA
    size = width // blocks
    total = loss_ref[0].astype(F32)
    for block in range(1, blocks):
        total = total + loss_ref[block].astype(F32)
    rows = loss_rows(jnp.broadcast_to(received_loss(total), total.shape), total.shape)
    for block in range(blocks):
        out_ref[block, out_ref.shape[1] - EXTRA :, :] = rows
    by_columns = (((1,), (1,)), ((), ()))
    for start, got_ref in ((0, low_got_ref), (step, high_got_ref)):
        half = slice(start, start + step)
        grad = lax.dot_general(low_ref[:width, :], low_weights_ref[half, :], by_columns, preferred_element_type=F32)
        grad += lax.dot_general(high_ref[:width, :], high_weights_ref[half, :], by_columns, preferred_element_type=F32)
        for part in range(step // LANES):
            at = slice(part * size, (part + 1) * size)
            columns = grad[:, part * LANES : (part + 1) * LANES].astype(BF16).reshape(blocks, size, LANES)
            added = columns.astype(F32) + got_ref[:, at, :].astype(F32)
            first = (start // LANES + part) * size
            out_ref[:, first : first + size, :] = added.astype(BF16)


def sum_kernel(clip_scale, action_scale, got_ref, keep_ref, give_ref):
    blocks = got_ref.shape[0]
    rows, count = keep_ref.shape
    half = rows // 2
    core = place(blocks)[0]

    def over(kind):
        chosen = [block for block in range(blocks) if block_of(member(block), blocks) == kind]
        total = got_ref[chosen[0]].astype(F32)
        for block in chosen[1:]:
            total = total + got_ref[block].astype(F32)
        return total

    lower = over(0)
    upper = over(1)
    both = lower + upper
    loss = received_loss(both[both.shape[0] - EXTRA :])
    give_ref[rows:, :] = jnp.concatenate([jnp.broadcast_to(loss, (8, LANES))] * (count // LANES), axis=1)
    for part in range(count // LANES):
        columns = slice(part * LANES, (part + 1) * LANES)
        at = slice(part * rows, (part + 1) * rows)

        @pl.when(core == 0)
        def _():
            keep_ref[:half, columns] = both[at][:half] * clip_scale
            give_ref[:half, columns] = both[at][half:] * clip_scale

        @pl.when(core != 0)
        def _():
            keep_ref[:, columns] = upper[at] * action_scale
            give_ref[:rows, columns] = lower[at] * action_scale


def last_kernel(n_clip, loss_scale, keep_ref, give_ref, taken_ref, clip_ref, action_ref, loss_ref, loss, sent):
    rows = keep_ref.shape[0]
    half = clip_ref.shape[0]
    core = place(n_clip)[0]
    loss[...] = (give_ref[rows : rows + 1, :1] + taken_ref[rows : rows + 1, :1]) * loss_scale

    def write(clip, action):
        pairs = [(clip, clip_ref), (action, action_ref), (loss, loss_ref)]
        copies = [pltpu.make_async_copy(source, target, sent.at[i]) for i, (source, target) in enumerate(pairs)]
        for copy in copies:
            copy.start()
        for copy in copies:
            copy.wait()

    @pl.when(core == 0)
    def _():
        write(keep_ref.at[:half, :], taken_ref.at[:rows, :])

    @pl.when(core != 0)
    def _():
        write(taken_ref.at[:half, :], keep_ref)


def call(kernel, out_shape, in_specs, out_specs=None, scratch=(), flops=0, moved=0):
    return pl.pallas_call(
        kernel,
        out_shape=out_shape,
        in_specs=in_specs,
        out_specs=jax.tree.map(lambda _: VMEM, out_shape) if out_specs is None else out_specs,
        scratch_shapes=scratch,
        compiler_params=pltpu.CompilerParams(vmem_limit_bytes=12 * 1024 * 1024),
        cost_estimate=pl.CostEstimate(flops=flops, bytes_accessed=moved, transcendentals=0),
    )


def shards(n_clip, n_act, clips, actions, positive_ids, robot_ids, robot_bias):
    both = ("clip", "act")
    pairs = n_act // 2
    near = n_clip // 2
    order = [member(i) for i in range(n_clip)]
    along_act = [[[k * n_act + 2 * m + c for m in order] for k in range(n_clip)] for c in range(2)]
    along_clip = [[[k * n_act + 2 * m + c for k in order] for m in range(pairs)] for c in range(2)]
    clips_first = along_act[0] + along_clip[1]
    actions_first = along_clip[0] + along_act[1]
    swap = [(i, i ^ 1) for i in range(n_act)]
    gather_pass, scatter_pass = [], []
    for neighbour in (lambda k: k ^ 1, lambda k: (k + near) % n_clip):
        there = [(k * n_act + 2 * m, neighbour(k) * n_act + 2 * m + 1) for k in range(n_clip) for m in range(pairs)]
        here = [(k * n_act + 2 * m, k * n_act + 2 * m + 1) for k in range(n_clip) for m in range(pairs)]
        gather_pass.append(there + [(b, a) for a, b in here])
        scatter_pass.append(here + [(b, a) for a, b in there])
    exchange = functools.partial(lax.all_to_all, axis_name=both, split_axis=0, concat_axis=0)

    half, count = clips.shape
    rows = actions.shape[0]
    width = rows * n_clip
    parts = count // LANES
    act = lax.axis_index("act")
    shape = jax.ShapeDtypeStruct

    first_core = act % 2 == 0
    clip_twice = jnp.broadcast_to(clips[None], (2, half, count)).reshape(rows, count)
    send = jnp.where(first_core, actions, clip_twice).astype(BF16)
    mine = jnp.where(first_core, clip_twice, actions).astype(BF16)
    other = lax.ppermute(send, "act", swap)
    pair = jnp.concatenate([mine[:half], other[:half]], axis=0)
    takes_mine = jnp.array([block_of(k, n_clip) == 1 for k in order])[:, None, None]
    chunks = jnp.where(first_core, pair[None], jnp.where(takes_mine, mine[None], other[None]))
    positive_ids, robot_ids = positive_ids[None, :], robot_ids[None, :]
    own = exchange(chunks, axis_index_groups=clips_first).reshape(width, count)
    halves = shape((width + EXTRA, count // 2), BF16)
    low, high = call(split_kernel, (halves, halves), [VMEM] * 3)(own, positive_ids, robot_ids)
    low = lax.ppermute(low, both, gather_pass[0])
    high = lax.ppermute(high, both, gather_pass[1])
    own_t = call(transpose_kernel, shape((count, width), BF16), [VMEM])(own)

    flops = 2 * width * count * count
    half_blocks = shape((n_clip, parts * rows // 2, LANES), BF16)
    scale = 2.0 / math.sqrt(width)
    fixed = (robot_bias[None, :], positive_ids, robot_ids, own, own_t)
    def results(loss):
        return (shape((count, count // 2), BF16), half_blocks, loss)

    cost = {"flops": flops, "moved": 4 * width * count}
    specs = [VMEM] * 6
    low_weights, low_grad, loss = call(
        functools.partial(low_kernel, n_clip, scale), results(shape((8, LANES), F32)), specs, **cost
    )(*fixed, low)
    low_got = lax.ppermute(low_grad, both, scatter_pass[0])
    high_weights, high_grad, loss_sent = call(
        functools.partial(high_kernel, n_clip, scale), results(shape((n_clip, EXTRA, LANES), BF16)), specs + [VMEM], **cost
    )(*fixed, high, loss)
    high_got = lax.ppermute(high_grad, both, scatter_pass[1])
    loss_got = exchange(loss_sent, axis_index_groups=actions_first)
    operands = (low, high, low_weights, high_weights)
    low_got, loss_got = lax.optimization_barrier((low_got, loss_got))
    ready = call(second_kernel, shape((n_clip, parts * rows + EXTRA, LANES), BF16), [VMEM] * 7, **cost)(
        *operands, low_got, high_got, loss_got
    )
    scattered = exchange(ready, axis_index_groups=clips_first)

    total_clips = count * n_clip
    total_actions = count * n_act
    keep, give = call(
        functools.partial(sum_kernel, 1.0 / math.sqrt(total_actions), 1.0 / math.sqrt(total_clips)),
        (shape((rows, count), F32), shape((rows + 8, count), F32)),
        [VMEM],
    )(scattered)
    taken = lax.ppermute(give, "act", swap)
    clip_grad, action_grad, loss = call(
        functools.partial(last_kernel, n_clip, 1.0 / (total_clips * total_actions)),
        (shape((half, count), F32), shape((rows, count), F32), shape((1, 1), F32)),
        [VMEM] * 3,
        (ANY, ANY, ANY),
        [pltpu.VMEM((1, 1), F32), pltpu.SemaphoreType.DMA((3,))],
    )(keep, give, taken)
    return clip_grad, action_grad, loss.reshape(())


def solution(mesh):
    return jax.shard_map(
        functools.partial(shards, mesh.shape["clip"], mesh.shape["act"]),
        mesh=mesh,
        in_specs=(P("act", "clip"), P("clip", "act"), P("clip"), P("act"), P()),
        out_specs=(P("act", "clip"), P("clip", "act"), P()),
        check_vma=False,
    )
```
